256 devices in a mesh: order: 32 (over y, x, core), blk: 8 (over z).
Axes of the slice: x: 4, y: 4, z: 8, core: 2. Of those that a mesh axis runs over, the one named last changes fastest.
Arguments:
- right_side: float32 [2, 2, 256, 3072], P(None, None, 'order'), may hold values from -6 to 6
- start_guess: float32 [2, 2, 256, 3072], P(None, None, 'order'), may hold values from -6 to 6
- legendre: bfloat16 [256, 1536, 3072], P('order', 'blk'), may hold values from -0.15309311 to 0.15309311, as said below
- orders: int32 [256], P('order'), may hold values from 0 to 3071, as said below
- prior_inv: float32 [3072], replicated, may hold values from 0.1 to 10
- noise_inv: float32 [2, 1536, 6144], P(None, ('blk', 'order')), may hold values from 0.05 to 0.8
- pixel_flags: int32 [2, 1536, 6144], P(None, ('blk', 'order')), may hold values 0 or 1
Outputs:
- solution: float32 [2, 2, 256, 3072], P(None, None, 'order')
- residual: float32 [2, 2, 256, 3072], P(None, None, 'order')
The draws below stay inside these ranges and needn't reach their ends.
Inputs may be any that keep to these rules, and one draw needn't show every extreme that they name: `orders`: distinct order numbers; 0 is among them, and entries 2k and 2k + 1 hold m and 3071 - m. `legendre`: zero wherever the degree is below the slot's order number.
All inputs are finite; a program needn't handle non-finite values. No bound on the sum of `pixel_flags` on one device may be relied on, other than what follows from the above.
Results may differ from the reference program's by a relative error of at most 0.0059.
Values may be sent and summed in bfloat16 or wider, within the bound.
A program may use at most 128 MiB of HBM per device.

```python
import math
import jax
import jax.numpy as jnp
from jax import lax

L = 3072
NHALF = 1536
NPHI = 6144
R = 2
ITERS = 2
M_TOT = 256


def pick_orders(key):
    half_count = M_TOT // 2
    chosen = jax.random.permutation(key, L // 2 - 1)[:half_count - 1] + 1
    lower = jnp.concatenate([jnp.zeros((1,), jnp.int32), chosen.astype(jnp.int32)])
    return jnp.stack([lower, L - 1 - lower], axis=1).reshape(M_TOT).astype(jnp.int32)


def draw_orders(key, part):
    return pick_orders(key)


def draw_legendre(key, part):
    order_values = pick_orders(key)
    key = jax.random.fold_in(key, 11)
    first_key = jax.random.fold_in(key, 0)
    live_mask = (jnp.arange(L, dtype=jnp.int32)[None, None, :] >= order_values[:, None, None]).astype(jnp.float32)
    values_raw = jnp.clip(jax.random.normal(first_key, (M_TOT, NHALF, L), jnp.float32), -6.0, 6.0)
    return (values_raw * live_mask * NHALF ** (-0.5)).astype(jnp.bfloat16)


def with_ends(entries, rng, low, largest):
    longest = entries.shape.index(max(entries.shape))
    spots = []
    for shift in (0, 1):
        where = [jax.random.randint(jax.random.fold_in(rng, axis), (), 0, length) for axis, length in enumerate(entries.shape)]
        where[longest] = (where[longest] + shift) % entries.shape[longest]
        spots.append(tuple(where))
    return entries.at[spots[0]].set(low).at[spots[1]].set(largest)


def steps_of(stream_key, shape, cuts, smallest, top_value):
    def one(axis_at, blocks):
        draws = jax.random.uniform(jax.random.fold_in(jax.random.fold_in(stream_key, 6), axis_at), (blocks,), jnp.float32, smallest / len(cuts), top_value / len(cuts))
        return jnp.repeat(jnp.exp(draws), shape[axis_at] // blocks).reshape((-1,) + (1,) * (len(shape) - axis_at - 1))

    loudness = one(*cuts[0])
    for cut in cuts[1:]:
        loudness = loudness * one(*cut)
    return loudness


def scatter_about(own_key, shape, spread, limit, cuts=(), kind=jnp.bfloat16):
    level = steps_of(own_key, shape, cuts, -0.22, 0.18) if cuts else 1.0
    drawn = jax.random.normal(own_key, shape, jnp.float32) * spread * level
    return jnp.minimum(jnp.maximum(drawn, -limit), limit).astype(kind)


def setup_inputs(seed: int = 0) -> dict:
    splits = jax.random.split(jax.random.key(seed), 8)
    right_side = scatter_about(splits[0], (R, 2, M_TOT, L), 1.0, 6.0, ((2, 32),), jnp.float32)
    start_guess = scatter_about(splits[1], (R, 2, M_TOT, L), 1.0, 6.0, ((2, 32),), jnp.float32)
    legendre = draw_legendre(jax.random.fold_in(splits[7], 71), 0)
    orders = draw_orders(jax.random.fold_in(splits[7], 71), 0)
    prior_inv = jnp.clip(jnp.exp(jax.random.uniform(splits[4], (L,), jnp.float32, math.log(0.1), math.log(10.0))), 0.1, 10.0)
    noise_inv = jnp.clip(jnp.exp(math.log(0.8) - 2.7725887 * jax.random.uniform(splits[5], (2, NHALF, NPHI), jnp.float32) ** steps_of(splits[5], (2, NHALF, NPHI), ((1, 256),), -0.2, 0.2)), 0.05, 0.8)
    pixel_flags = with_ends((jax.random.randint(splits[6], (2, NHALF, NPHI), 0, 5) < 4).astype(jnp.int32), jax.random.fold_in(splits[6], 1), 0, 1)
    return dict(right_side=right_side, start_guess=start_guess, legendre=legendre, orders=orders, prior_inv=prior_inv, noise_inv=noise_inv, pixel_flags=pixel_flags)


def fourier_of(orders):
    longitude = jnp.arange(NPHI, dtype=jnp.int32)
    phase_index = (orders[:, None] * longitude[None, :]) % NPHI
    angles = phase_index.astype(jnp.float32) * (2.0 * jnp.pi / NPHI)
    weight = jnp.where(orders == 0, 1.0, 2.0).astype(jnp.float32) * (NPHI ** -0.5)
    return jnp.stack([weight[:, None] * jnp.cos(angles), -weight[:, None] * jnp.sin(angles)])


def reference(right_side, start_guess, legendre, orders, prior_inv, noise_inv, pixel_flags):
    fourier_table = fourier_of(orders)
    degrees = jnp.arange(L, dtype=jnp.int32)
    parity_sign = 1.0 - 2.0 * ((degrees[None, :] + orders[:, None]) % 2).astype(jnp.float32)
    pixel_weight = noise_inv * pixel_flags.astype(jnp.float32)
    slots = jnp.arange(M_TOT, dtype=jnp.int32)
    high = lax.Precision.HIGHEST

    def operator(vector):
        rounded = vector.astype(jnp.bfloat16)
        hemispheres = jnp.stack([rounded, rounded * parity_sign.astype(jnp.bfloat16)], axis=2)

        def synthesize(order_slot):
            return jnp.einsum('rchl,jl->rchj', hemispheres[:, :, :, order_slot].astype(jnp.float32),
                              legendre[order_slot].astype(jnp.float32), precision=high)

        cycle_modes = jnp.moveaxis(lax.map(synthesize, slots), 0, -1)
        sky_map = jnp.einsum('rchkm,cmp->rhkp', cycle_modes, fourier_table, precision=high)
        analysed = jnp.einsum('rhkp,cmp->rchkm', sky_map * pixel_weight[None], fourier_table,
                              precision=high).astype(jnp.bfloat16)

        def analyze(order_slot):
            partial_value = jnp.einsum('rchj,jl->rchl', analysed[..., order_slot].astype(jnp.float32),
                                 legendre[order_slot].astype(jnp.float32), precision=high)
            return partial_value[:, :, 0] + parity_sign[order_slot] * partial_value[:, :, 1]

        applied = jnp.moveaxis(lax.map(analyze, slots), 0, 2)
        return prior_inv * vector + applied

    def inner_sum(first_vec, second_vec):
        return jnp.sum(first_vec * second_vec, axis=(1, 2, 3))

    solution = start_guess
    residual = right_side - operator(start_guess)
    direction = residual
    norm_now = inner_sum(residual, residual)
    for iteration in range(ITERS):
        image = operator(direction)
        step_size = (norm_now / inner_sum(direction, image))[:, None, None, None]
        solution = solution + step_size * direction
        residual = residual - step_size * image
        norm_next = inner_sum(residual, residual)
        direction = residual + (norm_next / norm_now)[:, None, None, None] * direction
        norm_now = norm_next
    return solution, residual
```

```python
import functools

import jax
import jax.numpy as jnp
from jax import lax
from jax.experimental import pallas as pl
from jax.experimental.pallas import tpu as pltpu
from jax.sharding import PartitionSpec as P

MESH = pl.DeviceIdType.MESH
F32 = jnp.float32
BF16 = jnp.bfloat16
VMEM_LIMIT = 56 * 1024 * 1024
NT = (((1,), (1,)), ((), ()))


def iota(shape, dim):
    return lax.broadcasted_iota(jnp.int32, shape, dim)


def pack_kernel(degrees, rows_step, orders, leg, rhs, guess, prior,
                leg_out, rhs_live, rhs_dead, x_live, x_dead, prior_live, prior_dead,
                mask_out, parity_out, row_a, row_b):
    pair = pl.program_id(0)
    block = pl.program_id(1)
    shift = orders[2 * pair]
    width = mask_out.shape[2]

    def rows_of(step, carry):
        rows = pl.ds(pl.multiple_of(step * 16, 16), 16)
        first = leg[0, 0, rows, :].astype(F32)
        second = pltpu.roll(leg[0, 1, rows, :].astype(F32), shift, 1)
        place = iota((16, degrees), 1)
        leg_out[0, rows, pl.ds(0, degrees)] = jnp.where(place >= shift, first, second).astype(BF16)
        extra = jnp.where(iota((16, 128), 1) == 0, second[:, degrees - 1:degrees], 0.0)
        leg_out[0, rows, pl.ds(degrees, 128)] = extra.astype(BF16)
        return carry

    lax.fori_loop(0, rows_step // 16, rows_of, 0)

    @pl.when((pair == 0) & (block == 0))
    def _():
        for quad in range(2):
            low, high = orders[4 * quad], orders[4 * quad + 2]
            low_b, high_b = orders[4 * quad + 1], orders[4 * quad + 3]
            upper = iota((8, degrees), 0) < 4
            shifts = jnp.where(upper, low, high)
            place = iota((8, degrees), 1)
            own = place >= shifts
            tail = iota((8, 128), 1) == 0

            def split(values_a, values_b, live, dead):
                rolled = jnp.where(upper, pltpu.roll(values_b, low, 1), pltpu.roll(values_b, high, 1))
                live[quad, :, pl.ds(0, degrees)] = jnp.where(own, values_a, rolled)
                live[quad, :, pl.ds(degrees, 128)] = jnp.where(tail, rolled[:, degrees - 1:degrees], 0.0)
                if width > degrees + 128:
                    live[quad, :, pl.ds(degrees + 128, width - degrees - 128)] = jnp.zeros(
                        (8, width - degrees - 128), F32)
                dead_values = jnp.where(own, rolled, values_a)
                dead[quad] = jnp.where(place == degrees - 1, 0.0, dead_values)

            for source, live, dead in ((rhs, rhs_live, rhs_dead), (guess, x_live, x_dead)):
                for half in range(2):
                    slot = 4 * quad + 2 * half
                    for r in range(2):
                        for c in range(2):
                            at = half * 4 + r * 2 + c
                            row_a[at:at + 1, :] = source[r, c, slot:slot + 1, :]
                            row_b[at:at + 1, :] = source[r, c, slot + 1:slot + 2, :]
                split(row_a[...], row_b[...], live, dead)
            every = jnp.broadcast_to(prior[...], (8, degrees))
            split(every, every, prior_live, prior_dead)
            degree = jnp.where(own, place, place - shifts + degrees)
            number = jnp.where(own, shifts, jnp.where(upper, low_b, high_b))
            parity = 1 - 2 * ((degree + number) & 1)
            parity_out[quad, :, pl.ds(0, degrees)] = parity.astype(F32)
            parity_out[quad, :, pl.ds(degrees, width - degrees)] = jnp.ones((8, width - degrees), F32)
            mask_out[quad, :, pl.ds(0, degrees)] = own.astype(F32)
            mask_out[quad, :, pl.ds(degrees, width - degrees)] = jnp.zeros((8, width - degrees), F32)


def unpack_kernel(degrees, orders, x_live, x_dead, r_live, r_dead, x_out, r_out, row_b):
    for quad in range(2):
        low, high = orders[4 * quad], orders[4 * quad + 2]
        upper = iota((8, degrees), 0) < 4
        place = iota((8, degrees), 1)
        own = place >= jnp.where(upper, low, high)
        for live, dead, out in ((x_live, x_dead, x_out), (r_live, r_dead, r_out)):
            alive = live[quad, :, pl.ds(0, degrees)]
            idle = dead[quad]
            values_a = jnp.where(own, alive, idle)
            values_b = jnp.where(own, idle, alive)
            extra = live[quad, :, pl.ds(degrees, 128)][:, 0:1]
            values_b = jnp.where(place == degrees - 1, extra, values_b)
            back = jnp.where(upper,
                             pltpu.roll(values_b, lax.rem(degrees - low, degrees), 1),
                             pltpu.roll(values_b, lax.rem(degrees - high, degrees), 1))
            row_b[0] = values_a
            row_b[1] = back
            for half in range(2):
                slot = 4 * quad + 2 * half
                for r in range(2):
                    for c in range(2):
                        at = half * 4 + r * 2 + c
                        out[r, c, slot:slot + 1, :] = row_b[0, at:at + 1, :]
                        out[r, c, slot + 1:slot + 2, :] = row_b[1, at:at + 1, :]


def split_bf16(values):
    high = values.astype(BF16)
    return high, (values - high.astype(F32)).astype(BF16)


def main_kernel(n_order, n_blk, degrees, cycles, pixels,
                own_orders, leg, rhs_live, rhs_dead, x_live, x_dead, prior_live, prior_dead,
                mask, parity, noise, flags,
                x_out_live, x_out_dead, r_out_live, r_out_dead,
                live, dead, lhs, modes, turned, back, send, recv, order_recv, scalar,
                flhs, weight, anal, sign, current, turn, table_hi, table_lo,
                partial, shard, rs_recv, summed, r1_live, r1_dead, steps,
                order_sems, a2a_send, a2a_recv, rs_send, rs_recv_sem, ag_send, ag_recv):
    me = lax.axis_index("order")
    mine = lax.axis_index("blk")
    width = degrees + 128
    half_turn = pixels // 2
    columns = 16 * n_order
    groups = columns // 128
    local = cycles * n_order
    shard_lanes = shard.shape[1]
    per_quad = n_blk // 2
    sheets = modes.shape[0]

    barrier = pltpu.get_barrier_semaphore()

    def greet_order(i, carry):
        pl.semaphore_signal(barrier, inc=1, device_id=(lax.rem(me + i, n_order), mine), device_id_type=MESH)
        return carry

    def greet_blk(i, carry):
        pl.semaphore_signal(barrier, inc=1, device_id=(me, lax.rem(mine + i, n_blk)), device_id_type=MESH)
        return carry

    lax.fori_loop(1, n_order, greet_order, 0)
    lax.fori_loop(1, n_blk, greet_blk, 0)

    weight[...] = jnp.zeros_like(weight)
    for h in range(2):
        for image in range(2):
            at = pl.ds(image * half_turn, half_turn)
            value = noise[h, :, at] * flags[h, :, at].astype(F32)
            for r in range(2):
                weight[image * 4 + h * 2 + r, 0:cycles, :] = value
    modes[...] = jnp.zeros_like(modes)
    turned[...] = jnp.zeros_like(turned)
    partial[...] = jnp.zeros_like(partial)
    scalar[...] = jnp.zeros_like(scalar)
    live[0] = x_live[...]
    dead[0] = x_dead[...]

    pl.semaphore_wait(barrier, n_order - 1 + n_blk - 1)

    def order_copy(i):
        return pltpu.make_async_remote_copy(
            src_ref=own_orders, dst_ref=order_recv.at[me],
            send_sem=order_sems.at[0], recv_sem=order_sems.at[1],
            device_id=(lax.rem(me + i, n_order), mine), device_id_type=MESH)

    def order_start(i, carry):
        order_copy(i).start()
        return carry

    lax.fori_loop(1, n_order, order_start, 0)
    order_recv[me] = own_orders[...]

    def wait_bytes(ref, sem):
        pltpu.make_async_copy(ref, ref, sem).wait()

    def exchange_start(step):
        def one(i, carry):
            to = lax.rem(me + i, n_order)
            pltpu.make_async_remote_copy(
                src_ref=send.at[to], dst_ref=recv.at[step, me],
                send_sem=a2a_send.at[step], recv_sem=a2a_recv.at[step],
                device_id=(to, mine), device_id_type=MESH).start()
            return carry

        lax.fori_loop(1, n_order, one, 0)

    def exchange_wait(step):
        wait_bytes(recv.at[step, pl.ds(0, n_order - 1)], a2a_recv.at[step])
        wait_bytes(send.at[pl.ds(0, n_order - 1)], a2a_send.at[step])
        recv[step, me] = send[me]

    def build_table():
        wait_bytes(order_recv.at[pl.ds(0, n_order - 1)], order_sems.at[1])
        wait_bytes(order_recv.at[pl.ds(0, n_order - 1)], order_sems.at[0])
        number = order_recv[...]
        lane = iota((n_order, 8, 128), 2)
        number_f = number.astype(F32)
        scale = jnp.where(number == 0, 1.0, 2.0) * (pixels ** -0.5)

        def angle(product):
            value = product.astype(F32)
            value = value - pixels * jnp.floor(value * (1.0 / pixels))
            return value * (2.0 * jnp.pi / pixels)

        base = angle(number * lane)
        current[:, 0] = scale * jnp.cos(base)
        current[:, 1] = -scale * jnp.sin(base)
        step = angle(number * 128)
        turn[:, 0] = jnp.cos(step)
        turn[:, 1] = jnp.sin(step)
        odd = (1 - 2 * (number & 1)).astype(F32)
        sign_rows = jnp.concatenate([odd, odd], axis=1).reshape(columns, 128)
        sign[...] = sign_rows.T[0:8]

        def block(q, carry):
            lanes = pl.ds(pl.multiple_of(q * 128, 128), 128)

            def some(part, inner):
                for k in range(8):
                    s = part * 8 + k
                    cosine, sine = current[s, 0], current[s, 1]
                    rows = pl.ds(pl.multiple_of(s * 16, 16), 16)
                    both = jnp.concatenate([cosine, sine], axis=0)
                    high, rest = split_bf16(both)
                    table_hi[rows, lanes] = high
                    table_lo[rows, lanes] = rest
                    turn_c, turn_s = turn[s, 0], turn[s, 1]
                    current[s, 0] = cosine * turn_c + sine * turn_s
                    current[s, 1] = sine * turn_c - cosine * turn_s
                return inner

            return lax.fori_loop(0, n_order // 8, some, carry)

        lax.fori_loop(0, half_turn // 128, block, 0)

    row8 = iota((8, 128), 0)
    lane8 = iota((8, 128), 1)
    group8 = lane8 // 16
    spare = lane8 >= 64

    def inner(first_live, second_live, first_dead, second_dead):
        total = jnp.zeros((8, 1), F32)
        for quad in range(2):
            total = total + jnp.sum(first_live(quad) * second_live(quad), axis=1, keepdims=True)
            total = total + jnp.sum(first_dead(quad) * second_dead(quad), axis=1, keepdims=True)
        first_row = (iota((8, 1), 0) % 4) < 2
        zero = jnp.sum(jnp.where(first_row, total, 0.0), axis=0, keepdims=True)
        one = jnp.sum(jnp.where(first_row, 0.0, total), axis=0, keepdims=True)
        return zero, one

    def put_scalars(values):
        tile = jnp.zeros((8, 128), F32)
        for at, value in enumerate(values):
            tile = jnp.where(row8 == at, value, tile)
        return jnp.where(spare, tile, 0.0)

    def sum_of(step):
        total = recv[step, 0]
        for s in range(1, n_order):
            total = total + recv[step, s]
        return total

    def by_row(total, at):
        return jnp.where((iota((8, 1), 0) % 4) < 2, total[at:at + 1, 64:65], total[at + 1:at + 2, 64:65])

    lane_step = 128 * max(n for n in (5, 3, 1) if (width // 128) % n == 0)

    def application(p, carry):
        for quad in range(2):
            def build(t, inner_carry):
                at = pl.ds(pl.multiple_of(t * lane_step, 128), lane_step)
                value = live[p, quad, :, at]
                first = mask[quad, :, at]
                second = 1.0 - first
                flip = parity[quad, :, at]
                high = value.astype(BF16).astype(F32)
                rest = value - high
                pieces = []
                for part in (high, rest):
                    for keep in (first, second):
                        kept = part * keep
                        pieces.append(kept)
                        pieces.append(kept * flip)
                lhs[quad, :, at] = jnp.concatenate(pieces, axis=0).astype(BF16)
                return inner_carry

            lax.fori_loop(0, width // lane_step, build, 0)
        for pair in range(4):
            quad, half = pair // 2, pair % 2
            out = lax.dot_general(lhs[quad], leg[pair], NT, preferred_element_type=F32)
            out = out[0:32] + out[32:64]
            at = 4 * half
            for slot in range(2):
                rows = jnp.concatenate([out[16 * slot + at:16 * slot + at + 4],
                                        out[16 * slot + 8 + at:16 * slot + 8 + at + 4]], axis=0)
                if sheets * 128 > local:
                    rows = jnp.concatenate([rows, jnp.zeros((8, sheets * 128 - local), F32)], axis=1)
                for sheet in range(sheets):
                    modes[sheet, pl.ds(2 * pair + slot, 8, stride=8), :] = rows[:, 128 * sheet:128 * sheet + 128]
        for sheet in range(sheets):
            turned[128 * sheet:128 * sheet + 128, :] = modes[sheet].T

        @pl.when(p == 2)
        def _():
            norm = inner(lambda q: live[1, q], lambda q: live[1, q], lambda q: dead[1, q], lambda q: dead[1, q])
            cross = inner(lambda q: live[1, q], lambda q: live[2, q], lambda q: dead[1, q], lambda q: dead[2, q])
            scalar[...] = put_scalars(norm + cross)

        for d in range(n_order):
            send[d] = turned[cycles * d:cycles * d + 8, :] + scalar[...]
        exchange_start(2 * p)

        @pl.when(p == 0)
        def _():
            build_table()

        exchange_wait(2 * p)

        @pl.when(p == 2)
        def _():
            total = sum_of(2 * p)
            norm, cross = by_row(total, 0), by_row(total, 2)
            step = norm / cross
            steps[0] = jnp.broadcast_to(norm, (8, 128))
            steps[1] = jnp.broadcast_to(step, (8, 128))
            for quad in range(2):
                r1_live[quad] = live[1, quad] - step * live[2, quad]
                r1_dead[quad] = dead[1, quad] - step * dead[2, quad]
            after = inner(lambda q: r1_live[q], lambda q: r1_live[q], lambda q: r1_dead[q], lambda q: r1_dead[q])
            scalar[...] = put_scalars(after)

        def shuffle(g, inner_carry):
            lanes = pl.ds(pl.multiple_of(g * 128, 128), 128)
            flip = sign[:, lanes]
            tiles = [recv[2 * p, g * 8 + i] for i in range(8)]
            straight = []
            for hr in range(4):
                acc = tiles[0] if hr == 0 else pltpu.roll(tiles[0], (128 - 16 * hr) % 128, 1)
                for i in range(1, 8):
                    by = (16 * i - 16 * hr) % 128
                    moved = tiles[i] if by == 0 else pltpu.roll(tiles[i], by, 1)
                    acc = jnp.where(group8 == i, moved, acc)
                straight.append(acc)
            flipped = [acc * flip for acc in straight]
            rows = jnp.concatenate(straight + flipped, axis=0)
            high, rest = split_bf16(rows)
            flhs[0:64, lanes] = high
            flhs[64:128, lanes] = rest
            return inner_carry

        lax.fori_loop(0, groups, shuffle, 0)

        anal[...] = jnp.zeros_like(anal)
        chunk = min(512, half_turn)

        def fourier(t, inner_carry):
            lanes = pl.ds(pl.multiple_of(t * chunk, 128), chunk)
            high_t, low_t = table_hi[:, lanes], table_lo[:, lanes]
            sky = jnp.dot(flhs[...], high_t, preferred_element_type=F32)
            sky = sky[0:64] + sky[64:128] + jnp.dot(flhs[0:64, :], low_t, preferred_element_type=F32)
            value = sky * weight[:, :, lanes].reshape(64, chunk)
            high, rest = split_bf16(value)
            out = lax.dot_general(jnp.concatenate([high, rest], axis=0), high_t, NT, preferred_element_type=F32)
            anal[...] += out[0:64] + out[64:128] + lax.dot_general(high, low_t, NT, preferred_element_type=F32)
            return inner_carry

        lax.fori_loop(0, half_turn // chunk, fourier, 0)

        def shuffle_back(g, inner_carry):
            lanes = pl.ds(pl.multiple_of(g * 128, 128), 128)
            flip = sign[:, lanes]
            rows = [anal[8 * hr:8 * hr + 8, lanes] + flip * anal[32 + 8 * hr:40 + 8 * hr, lanes] for hr in range(4)]
            base = scalar[...]
            for i in range(8):
                acc = base
                for hr in range(4):
                    by = (16 * hr - 16 * i) % 128
                    moved = rows[hr] if by == 0 else pltpu.roll(rows[hr], by, 1)
                    acc = jnp.where(group8 == hr, moved, acc)
                send[g * 8 + i] = acc
            return inner_carry

        lax.fori_loop(0, groups, shuffle_back, 0)
        exchange_start(2 * p + 1)
        exchange_wait(2 * p + 1)

        for d in range(n_order):
            turned[cycles * d:cycles * d + cycles, :] = recv[2 * p + 1, d, 0:cycles, :]
        for sheet in range(sheets):
            back[sheet] = turned[128 * sheet:128 * sheet + 128, :].T

        def rs_copy(b):
            return pltpu.make_async_remote_copy(
                src_ref=partial.at[b // per_quad, :, pl.ds((b % per_quad) * shard_lanes, shard_lanes)],
                dst_ref=rs_recv.at[p, mine],
                send_sem=rs_send.at[p], recv_sem=rs_recv_sem.at[p],
                device_id=(me, b), device_id_type=MESH)

        for quad in range(2):
            for half in range(2):
                pair = 2 * quad + half
                rows = jnp.concatenate([
                    jnp.concatenate([back[sheet, pl.ds(2 * pair + slot, 8, stride=8), :] for sheet in range(sheets)],
                                    axis=1)
                    for slot in range(2)], axis=0)
                high, rest = split_bf16(rows[:, 0:local])
                both = jnp.concatenate([high, rest], axis=0)

                def analyse(t, inner_carry):
                    at = pl.ds(pl.multiple_of(t * lane_step, 128), lane_step)
                    out = jnp.dot(both, leg[pair, :, at], preferred_element_type=F32)
                    out = out[0:16] + out[16:32]
                    first = mask[quad, 4 * half:4 * half + 1, at]
                    flip = parity[quad, 4 * half:4 * half + 1, at]
                    kept = jnp.where(first > 0.5, out[0:8], out[8:16])
                    partial[quad, 4 * half:4 * half + 4, at] = kept[0:4] + flip * kept[4:8]
                    return inner_carry

                lax.fori_loop(0, width // lane_step, analyse, 0)
            for b in range(per_quad * quad, per_quad * quad + per_quad):
                @pl.when(mine != b)
                def _():
                    rs_copy(b).start()

        wait_bytes(rs_recv.at[p, pl.ds(0, n_blk - 1)], rs_recv_sem.at[p])
        wait_bytes(rs_recv.at[p, pl.ds(0, n_blk - 1)], rs_send.at[p])
        my_quad = mine // per_quad
        my_lanes = pl.ds(pl.multiple_of((mine % per_quad) * shard_lanes, 128), shard_lanes)
        rs_recv[p, mine] = partial[my_quad, :, my_lanes]
        total = rs_recv[p, 0]
        for b in range(1, n_blk):
            total = total + rs_recv[p, b]
        shard[...] = total

        def ag_start(i, inner_carry):
            pltpu.make_async_remote_copy(
                src_ref=shard, dst_ref=summed.at[p, my_quad, :, my_lanes],
                send_sem=ag_send.at[p], recv_sem=ag_recv.at[p],
                device_id=(me, lax.rem(mine + i, n_blk)), device_id_type=MESH).start()
            return inner_carry

        lax.fori_loop(1, n_blk, ag_start, 0)
        summed[p, my_quad, :, my_lanes] = total
        wait_bytes(rs_recv.at[p, pl.ds(0, n_blk - 1)], ag_recv.at[p])
        wait_bytes(rs_recv.at[p, pl.ds(0, n_blk - 1)], ag_send.at[p])

        for quad in range(2):
            image = prior_live[quad] * live[p, quad] + summed[p, quad]
            live[p + 1, quad] = jnp.where(p == 0, rhs_live[quad] - image, image)
            image = prior_dead[quad] * dead[p, quad]
            dead[p + 1, quad] = jnp.where(p == 0, rhs_dead[quad] - image, image)
        return carry

    lax.fori_loop(0, 3, application, 0)

    after = by_row(sum_of(5), 0)
    ratio = after / steps[0, :, 0:1]
    step = steps[1, :, 0:1]

    def direction(q, r1, stored):
        return r1[q] + ratio * stored[1, q]

    def image_of(q, stored):
        return (1.0 + ratio) * stored[2, q] - step * stored[3, q]

    curve = inner(lambda q: direction(q, r1_live, live), lambda q: image_of(q, live),
                  lambda q: direction(q, r1_dead, dead), lambda q: image_of(q, dead))
    tile = put_scalars(curve)
    for d in range(n_order):
        send[d] = tile
    exchange_start(6)
    exchange_wait(6)
    second = after / by_row(sum_of(6), 0)
    for q in range(2):
        for r1, stored, x_out, r_out in ((r1_live, live, x_out_live, r_out_live),
                                         (r1_dead, dead, x_out_dead, r_out_dead)):
            x_out[q] = stored[0, q] + step * stored[1, q] + second * direction(q, r1, stored)
            r_out[q] = r1[q] - second * image_of(q, stored)


def per_device(n_order, n_blk, right_side, start_guess, legendre, orders, prior_inv, noise_inv, pixel_flags):
    slots, local, degrees = legendre.shape
    cycles, pixels = noise_inv.shape[1], noise_inv.shape[2]
    unit = 128 * (n_blk // 2)
    width = -(-(degrees + 128) // unit) * unit
    shard_lanes = width // (n_blk // 2)
    rows_step = local // 2 if (local // 2) % 16 == 0 else local
    smem = pl.BlockSpec(memory_space=pltpu.SMEM)
    vmem = pl.BlockSpec(memory_space=pltpu.VMEM)
    live_shape = jax.ShapeDtypeStruct((2, 8, width), F32)
    dead_shape = jax.ShapeDtypeStruct((2, 8, degrees), F32)

    packed = pl.pallas_call(
        functools.partial(pack_kernel, degrees, rows_step),
        grid=(4, local // rows_step),
        in_specs=[smem, pl.BlockSpec((1, 2, rows_step, degrees), lambda k, b: (k, 0, b, 0)), vmem, vmem, vmem],
        out_specs=[pl.BlockSpec((1, rows_step, degrees + 128), lambda k, b: (k, b, 0))] + [vmem] * 8,
        out_shape=[jax.ShapeDtypeStruct((4, local, degrees + 128), BF16),
                   live_shape, dead_shape, live_shape, dead_shape, live_shape, dead_shape, live_shape, live_shape],
        scratch_shapes=[pltpu.VMEM((8, degrees), F32), pltpu.VMEM((8, degrees), F32)],
        compiler_params=pltpu.CompilerParams(vmem_limit_bytes=VMEM_LIMIT),
        name="pack",
    )(orders, legendre.reshape(4, 2, local, degrees), right_side, start_guess, prior_inv.reshape(1, degrees))
    leg, rhs_live, rhs_dead, x_live, x_dead, prior_live, prior_dead, mask, parity = packed

    columns = 16 * n_order
    turned_rows = -(-(local + 8) // 128) * 128
    half_turn = pixels // 2
    own_orders = jnp.broadcast_to(orders[:, None], (8, 128))
    scratch = [
        pltpu.VMEM((4, 2, 8, width), F32),
        pltpu.VMEM((4, 2, 8, degrees), F32),
        pltpu.VMEM((2, 64, degrees + 128), BF16),
        pltpu.VMEM((turned_rows // 128, 128, 128), F32),
        pltpu.VMEM((turned_rows, 128), F32),
        pltpu.VMEM((turned_rows // 128, 128, 128), F32),
        pltpu.VMEM((n_order, 8, 128), F32),
        pltpu.VMEM((7, n_order, 8, 128), F32),
        pltpu.VMEM((n_order, 8, 128), jnp.int32),
        pltpu.VMEM((8, 128), F32),
        pltpu.VMEM((128, columns), BF16),
        pltpu.VMEM((8, 8, half_turn), F32),
        pltpu.VMEM((64, columns), F32),
        pltpu.VMEM((8, columns), F32),
        pltpu.VMEM((n_order, 2, 8, 128), F32),
        pltpu.VMEM((n_order, 2, 8, 128), F32),
        pltpu.VMEM((columns, half_turn), BF16),
        pltpu.VMEM((columns, half_turn), BF16),
        pltpu.VMEM((2, 8, width), F32),
        pltpu.VMEM((8, shard_lanes), F32),
        pltpu.VMEM((3, n_blk, 8, shard_lanes), F32),
        pltpu.VMEM((3, 2, 8, width), F32),
        pltpu.VMEM((2, 8, width), F32),
        pltpu.VMEM((2, 8, degrees), F32),
        pltpu.VMEM((2, 8, 128), F32),
        pltpu.SemaphoreType.DMA((2,)),
        pltpu.SemaphoreType.DMA((7,)),
        pltpu.SemaphoreType.DMA((7,)),
        pltpu.SemaphoreType.DMA((3,)),
        pltpu.SemaphoreType.DMA((3,)),
        pltpu.SemaphoreType.DMA((3,)),
        pltpu.SemaphoreType.DMA((3,)),
    ]
    results = pl.pallas_call(
        functools.partial(main_kernel, n_order, n_blk, degrees, cycles, pixels),
        in_specs=[vmem] * 12,
        out_specs=[vmem] * 4,
        out_shape=[live_shape, dead_shape, live_shape, dead_shape],
        scratch_shapes=scratch,
        compiler_params=pltpu.CompilerParams(
            collective_id=0, has_side_effects=True, vmem_limit_bytes=VMEM_LIMIT),
        name="steps",
    )(own_orders, leg, rhs_live, rhs_dead, x_live, x_dead, prior_live, prior_dead, mask, parity,
      noise_inv, pixel_flags)

    full = jax.ShapeDtypeStruct(right_side.shape, F32)
    return tuple(pl.pallas_call(
        functools.partial(unpack_kernel, degrees),
        in_specs=[smem] + [vmem] * 4,
        out_specs=[vmem] * 2,
        out_shape=[full, full],
        scratch_shapes=[pltpu.VMEM((2, 8, degrees), F32)],
        compiler_params=pltpu.CompilerParams(vmem_limit_bytes=VMEM_LIMIT),
        name="unpack",
    )(orders, *results))


def solution(mesh):
    in_specs = (
        P(None, None, "order", None),
        P(None, None, "order", None),
        P("order", "blk", None),
        P("order"),
        P(),
        P(None, ("blk", "order"), None),
        P(None, ("blk", "order"), None),
    )
    out_specs = (P(None, None, "order", None), P(None, None, "order", None))
    body = functools.partial(per_device, mesh.shape["order"], mesh.shape["blk"])
    return jax.shard_map(body, mesh=mesh, in_specs=in_specs, out_specs=out_specs, check_vma=False)
```

```python
import functools

import jax
import jax.numpy as jnp
from jax import lax
from jax.experimental import pallas as pl
from jax.experimental.pallas import tpu as pltpu
from jax.sharding import PartitionSpec as P

MESH = pl.DeviceIdType.MESH
F32 = jnp.float32
BF16 = jnp.bfloat16
VMEM_LIMIT = 56 * 1024 * 1024
NT = (((1,), (1,)), ((), ()))


def iota(shape, dim):
    return lax.broadcasted_iota(jnp.int32, shape, dim)


def tile_lanes(t, shift, less, tiles):
    at = lax.rem(t - shift // 128 - less + 2 * tiles, tiles) * 128
    return pl.ds(pl.multiple_of(at, 128), 128)


def rolled_tiles(load, shift, tiles, lane):
    within = lax.rem(shift, 128)
    before = pltpu.roll(load(tile_lanes(0, shift, 1, tiles)), within, 1)
    for t in range(tiles):
        now = pltpu.roll(load(tile_lanes(t, shift, 0, tiles)), within, 1)
        yield jnp.where(lane >= within, now, before)
        before = now


def pack_kernel(degrees, rows_step, orders, leg, rhs, guess, prior,
                leg_out, numbers, rhs_live, rhs_dead, x_live, x_dead, prior_live, prior_dead,
                mask, parity, rows_a, rows_b):
    pair = pl.program_id(0)
    block = pl.program_id(1)
    shift = orders[2 * pair]
    tiles = degrees // 128
    lane16 = iota((16, 128), 1)
    lane8 = iota((8, 128), 1)
    row8 = iota((8, 128), 0)

    def rows_of(step, carry):
        rows = pl.ds(pl.multiple_of(step * 16, 16), 16)
        moved = rolled_tiles(lambda at: leg[0, 1, rows, at], shift, tiles, lane16)
        for t, rolled in enumerate(moved):
            first = leg[0, 0, rows, t * 128:t * 128 + 128]
            kept = jnp.where(lane16 + t * 128 >= shift, first, rolled)
            leg_out[0, rows, t * 128:t * 128 + 128] = kept.astype(BF16)
        extra = jnp.where(lane16 == 0, pltpu.roll(rolled, 1, 1), jnp.zeros_like(rolled))
        leg_out[0, rows, degrees:degrees + 128] = extra.astype(BF16)
        return carry

    lax.fori_loop(0, rows_step // 16, rows_of, 0)

    @pl.when((pair == 0) & (block == 0))
    def _():
        tile = jnp.zeros((8, 128), jnp.int32)
        for m in range(8):
            tile = jnp.where(row8 == m, orders[m], tile)
        numbers[...] = tile

    for quad in range(2):
        @pl.when((pair == quad) & (block == 0))
        def _():
            upper = row8 < 4
            low, high = orders[4 * quad], orders[4 * quad + 2]
            shifts = jnp.where(upper, low, high)
            number_b = jnp.where(upper, orders[4 * quad + 1], orders[4 * quad + 3])
            tail = slice(degrees, degrees + 128)
            sources = [(rhs, rhs_live, rhs_dead), (guess, x_live, x_dead)]
            for at, (source, live, dead) in enumerate(sources):
                for half in range(2):
                    slot = 4 * quad + 2 * half
                    for r in range(2):
                        for c in range(2):
                            row = half * 4 + r * 2 + c
                            rows_a[at, row:row + 1, :] = source[r, c, slot:slot + 1, :]
                            rows_b[at, row:row + 1, :] = source[r, c, slot + 1:slot + 2, :]

            def both(load):
                for one, two in zip(rolled_tiles(load, low, tiles, lane8), rolled_tiles(load, high, tiles, lane8)):
                    yield jnp.where(upper, one, two)

            for at, (source, live, dead) in enumerate(sources):
                for t, rolled in enumerate(both(lambda lanes: rows_b[at, :, lanes])):
                    lanes = slice(t * 128, t * 128 + 128)
                    own = lane8 + t * 128 >= shifts
                    first = rows_a[at, :, lanes]
                    idle = jnp.where(own, rolled, first)
                    if t == tiles - 1:
                        idle = jnp.where(lane8 == 127, 0.0, idle)
                    live[quad, :, lanes] = jnp.where(own, first, rolled)
                    dead[quad, :, lanes] = idle
                live[quad, :, tail] = jnp.where(lane8 == 0, pltpu.roll(rolled, 1, 1), 0.0)
            for t, rolled in enumerate(both(lambda lanes: jnp.broadcast_to(prior[:, lanes], (8, 128)))):
                lanes = slice(t * 128, t * 128 + 128)
                place = lane8 + t * 128
                own = place >= shifts
                first = jnp.broadcast_to(prior[:, lanes], (8, 128))
                prior_live[quad, :, lanes] = jnp.where(own, first, rolled)
                prior_dead[quad, :, lanes] = jnp.where(own, rolled, first)
                total = jnp.where(own, place + shifts, place - shifts + degrees + number_b)
                parity[quad, :, lanes] = (1 - 2 * (total & 1)).astype(F32)
                mask[quad, :, lanes] = own.astype(F32)
            prior_live[quad, :, tail] = jnp.where(lane8 == 0, pltpu.roll(rolled, 1, 1), 0.0)
            parity[quad, :, tail] = jnp.ones((8, 128), F32)
            mask[quad, :, tail] = jnp.zeros((8, 128), F32)


def unpack_kernel(degrees, orders, x_live, x_dead, r_live, r_dead, x_out, r_out, rows_a, rows_b):
    tiles = degrees // 128
    lane8 = iota((8, 128), 1)
    upper = iota((8, 128), 0) < 4
    for quad in range(2):
        low, high = orders[4 * quad], orders[4 * quad + 2]
        shifts = jnp.where(upper, low, high)
        back_low, back_high = lax.rem(degrees - low, degrees), lax.rem(degrees - high, degrees)
        for at, (live, dead, out) in enumerate(((x_live, x_dead, x_out), (r_live, r_dead, r_out))):
            for t in range(tiles):
                lanes = slice(t * 128, t * 128 + 128)
                own = lane8 + t * 128 >= shifts
                alive, idle = live[quad, :, lanes], dead[quad, :, lanes]
                rows_a[at, :, lanes] = jnp.where(own, alive, idle)
                second = jnp.where(own, idle, alive)
                if t == tiles - 1:
                    extra = live[quad, :, degrees:degrees + 128]
                    second = jnp.where(lane8 == 127, pltpu.roll(extra, 127, 1), second)
                rows_b[at, :, lanes] = second
            load = lambda lanes: rows_b[at, :, lanes]
            back = zip(rolled_tiles(load, back_low, tiles, lane8), rolled_tiles(load, back_high, tiles, lane8))
            kept = [jnp.where(upper, one, two) for one, two in back]
            for t, value in enumerate(kept):
                rows_b[at, :, t * 128:t * 128 + 128] = value
            for half in range(2):
                slot = 4 * quad + 2 * half
                for r in range(2):
                    for c in range(2):
                        row = half * 4 + r * 2 + c
                        out[r, c, slot:slot + 1, :] = rows_a[at, row:row + 1, :]
                        out[r, c, slot + 1:slot + 2, :] = rows_b[at, row:row + 1, :]


def split_bf16(values):
    high = values.astype(BF16)
    return high, (values - high.astype(F32)).astype(BF16)


def main_kernel(n_order, n_blk, degrees, cycles, pixels,
                own_orders, leg_hbm, rhs_live_hbm, rhs_dead_hbm, x_live, x_dead_hbm, prior_live_hbm, prior_dead_hbm,
                mask, parity, noise_hbm, flags_hbm,
                x_out_live, x_out_dead, r_out_live, r_out_dead,
                leg, live, dead, rhs_live, rhs_dead, prior_live, prior_dead, noise, flags,
                lhs, modes, turned, back, send, recv, order_recv, scalar,
                flhs, weight, anal, sign, current, turn, table, sky_kept, pixel_sums,
                partial, extras, shard, rs_recv0, rs_recv1, summed, extra_sum,
                r1_live, r1_dead, steps,
                leg_sems, load_sems, order_sems, a2a_send, a2a_recv, rs_send, rs_arrive, ag_send, ag_arrive):
    me = lax.axis_index("order")
    mine = lax.axis_index("blk")
    tiles = degrees // 128
    half_turn = pixels // 2
    columns = 16 * n_order
    groups = columns // 128
    local = cycles * n_order
    part = degrees // n_blk
    sheets = modes.shape[0]

    def leg_copy(pair):
        return pltpu.make_async_copy(leg_hbm.at[pair], leg.at[pair], leg_sems.at[pair])

    def load_copy(at):
        source, target = ((x_dead_hbm, dead.at[0]), (prior_live_hbm, prior_live), (prior_dead_hbm, prior_dead),
                          (noise_hbm, noise), (flags_hbm, flags), (rhs_live_hbm, rhs_live),
                          (rhs_dead_hbm, rhs_dead))[at]
        return pltpu.make_async_copy(source, target, load_sems.at[at])

    for pair in range(4):
        leg_copy(pair).start()
    for at in range(7):
        load_copy(at).start()

    side_x = 2
    side_y = n_order // 4
    if n_order == 32:
        side_x, side_y = 4, 4
    offsets = [(a, b, c) for a in range(side_y) for b in range(side_x) for c in range(2) if a or b or c]
    offsets.sort(key=lambda o: -(2 * min(o[0], side_y - o[0]) + 2 * min(o[1], side_x - o[1]) + o[2]))
    my_y, my_x, my_c = me // (2 * side_x), (me // 2) % side_x, me % 2
    peers = [lax.rem(my_y + a, side_y) * (2 * side_x) + lax.rem(my_x + b, side_x) * 2 + lax.rem(my_c + c, 2)
             for a, b, c in offsets]
    steps_z = sorted(range(1, n_blk), key=lambda i: -min(i, n_blk - i))
    partners = [lax.rem(mine + i, n_blk) for i in steps_z]

    barrier = pltpu.get_barrier_semaphore()
    for to in peers:
        pl.semaphore_signal(barrier, inc=1, device_id=(to, mine), device_id_type=MESH)
    for to in partners:
        pl.semaphore_signal(barrier, inc=1, device_id=(me, to), device_id_type=MESH)

    def wait_bytes(ref, sem):
        pltpu.make_async_copy(ref, ref, sem).wait()

    row8 = iota((8, 128), 0)
    lane8 = iota((8, 128), 1)
    modes[...] = jnp.zeros_like(modes)
    turned[...] = jnp.zeros_like(turned)
    scalar[...] = jnp.zeros_like(scalar)
    pixel_sums[...] = jnp.zeros_like(pixel_sums)
    live[0] = x_live[...]

    pl.semaphore_wait(barrier, n_order - 1 + n_blk - 1)

    for to in peers:
        pltpu.make_async_remote_copy(
            src_ref=own_orders, dst_ref=order_recv.at[me],
            send_sem=order_sems.at[0], recv_sem=order_sems.at[1],
            device_id=(to, mine), device_id_type=MESH).start()
    order_recv[me] = own_orders[...]

    def exchange_start(step):
        for to in peers:
            pltpu.make_async_remote_copy(
                src_ref=send.at[to], dst_ref=recv.at[step, me],
                send_sem=a2a_send.at[step], recv_sem=a2a_recv.at[step],
                device_id=(to, mine), device_id_type=MESH).start()
        recv[step, me] = send[me]

    def exchange_wait(step):
        wait_bytes(recv.at[step, pl.ds(0, n_order - 1)], a2a_recv.at[step])
        wait_bytes(send.at[pl.ds(0, n_order - 1)], a2a_send.at[step])

    def build_weight():
        weight[...] = jnp.zeros_like(weight)
        for j in range(cycles):
            value = noise[j] * flags[j].astype(F32)
            for h in range(2):
                for image in range(2):
                    row = value[h:h + 1, image * half_turn:(image + 1) * half_turn]
                    for r in range(2):
                        weight[image * 4 + h * 2 + r, j:j + 1, :] = row

    def build_table():
        wait_bytes(order_recv.at[pl.ds(0, n_order - 1)], order_sems.at[1])
        wait_bytes(order_recv.at[pl.ds(0, n_order - 1)], order_sems.at[0])
        number = order_recv[...]
        lane = iota((n_order, 8, 128), 2)
        scale = jnp.where(number == 0, 1.0, 2.0) * (pixels ** -0.5)

        def angle(product):
            value = product.astype(F32)
            value = value - pixels * jnp.floor(value * (1.0 / pixels))
            return value * (2.0 * jnp.pi / pixels)

        base = angle(number * lane)
        current[:, 0] = scale * jnp.cos(base)
        current[:, 1] = -scale * jnp.sin(base)
        step = angle(number * 128)
        turn[:, 0] = jnp.cos(step)
        turn[:, 1] = jnp.sin(step)
        odd = (1 - 2 * (number & 1)).astype(F32)
        sign_rows = jnp.concatenate([odd, odd], axis=1).reshape(columns, 128)
        sign[...] = sign_rows.T[0:8]

        def block(q, carry):
            lanes = pl.ds(pl.multiple_of(q * 128, 128), 128)

            def some(piece, inner):
                for k in range(8):
                    s = piece * 8 + k
                    cosine, sine = current[s, 0], current[s, 1]
                    rows = pl.ds(pl.multiple_of(s * 16, 16), 16)
                    table[rows, lanes] = jnp.concatenate([cosine, sine], axis=0).astype(BF16)
                    turn_c, turn_s = turn[s, 0], turn[s, 1]
                    current[s, 0] = cosine * turn_c + sine * turn_s
                    current[s, 1] = sine * turn_c - cosine * turn_s
                return inner

            return lax.fori_loop(0, n_order // 8, some, carry)

        lax.fori_loop(0, half_turn // 128, block, 0)

    group8 = lane8 // 16
    item8 = lane8 // 8
    first_row8 = (iota((8, 1), 0) % 4) < 2

    def by_realization(total):
        zero = jnp.sum(jnp.where(first_row8, total, 0.0), axis=0, keepdims=True)
        one = jnp.sum(jnp.where(first_row8, 0.0, total), axis=0, keepdims=True)
        return [zero, one]

    def lane_sum(value):
        return jnp.sum(value, axis=1, keepdims=True)

    def put_scalars(values):
        tile = jnp.zeros((8, 128), F32)
        for at, value in enumerate(values):
            tile = jnp.where(item8 == at, value, tile)
        return tile

    def sum_tiles(load, count):
        values = [load(s) for s in range(count)]
        while len(values) > 1:
            values = [a + b for a, b in zip(values[::2], values[1::2])]
        return values[0]

    def scalar_at(total, row, at):
        return total[row:row + 1, 8 * at:8 * at + 1]

    def rows_from(pair):
        return jnp.where(first_row8, pair[0], pair[1])

    def pair_at(total, row, at):
        return [scalar_at(total, row, at), scalar_at(total, row, at + 1)]

    lane_step = 128 * max(n for n in (5, 3, 1) if (tiles + 1) % n == 0)
    width = degrees + 128

    def application(p, carry):
        for quad in range(2):
            @pl.when(p > 0)
            def _():
                wait_bytes(rs_recv0.at[p - 1, pl.ds(0, n_blk - 1)], ag_arrive.at[p - 1, quad])
                main = pl.ds(0, degrees)
                image = prior_live[quad, :, main] * live[p - 1, quad, :, main] + summed[p - 1, quad]
                live[p, quad, :, main] = jnp.where(p == 1, rhs_live[quad, :, main] - image, image)
                tail = pl.ds(degrees, 128)
                image = prior_live[quad, :, tail] * live[p - 1, quad, :, tail] + extra_sum[quad]
                live[p, quad, :, tail] = jnp.where(p == 1, rhs_live[quad, :, tail] - image, image)

            def build(t, inner_carry):
                at = pl.ds(pl.multiple_of(t * lane_step, 128), lane_step)
                value = live[p, quad, :, at]
                first = mask[quad, :, at]
                second = 1.0 - first
                flip = parity[quad, :, at]
                high = value.astype(BF16).astype(F32)
                rest = value - high
                pieces = []
                for piece in (high, rest):
                    for keep in (first, second):
                        kept = piece * keep
                        pieces.append(kept)
                        pieces.append(kept * flip)
                lhs[quad, :, at] = jnp.concatenate(pieces, axis=0).astype(BF16)
                return inner_carry

            lax.fori_loop(0, width // lane_step, build, 0)
            for half in range(2):
                pair = 2 * quad + half

                @pl.when(p == 0)
                def _():
                    leg_copy(pair).wait()

                out = lax.dot_general(lhs[quad], leg[pair], NT, preferred_element_type=F32)
                out = out[0:32] + out[32:64]
                at = 4 * half
                for slot in range(2):
                    rows = jnp.concatenate([out[16 * slot + at:16 * slot + at + 4],
                                            out[16 * slot + 8 + at:16 * slot + 8 + at + 4]], axis=0)
                    if sheets * 128 > local:
                        rows = jnp.concatenate([rows, jnp.zeros((8, sheets * 128 - local), F32)], axis=1)
                    for sheet in range(sheets):
                        modes[sheet, pl.ds(2 * pair + slot, 8, stride=8), :] = rows[:, 128 * sheet:128 * sheet + 128]

        @pl.when(p > 0)
        def _():
            for quad in range(2):
                wait_bytes(rs_recv0.at[p - 1, pl.ds(0, n_blk - 1)], ag_send.at[p - 1, quad])

        for sheet in range(sheets):
            turned[128 * sheet:128 * sheet + 128, :] = modes[sheet].T

        @pl.when(p == 2)
        def _():
            norm = cross = jnp.zeros((8, 1), F32)
            for quad in range(2):
                for held in (live, dead):
                    norm = norm + lane_sum(held[1, quad] * held[1, quad])
                    cross = cross + lane_sum(held[1, quad] * held[2, quad])
            scalar[...] = put_scalars(by_realization(norm) + by_realization(cross))

        for d in range(n_order):
            send[d] = jnp.where(row8 < cycles, turned[cycles * d:cycles * d + 8, :], scalar[...])
        exchange_start(2 * p)

        @pl.when(p == 0)
        def _():
            build_table()
            load_copy(3).wait()
            load_copy(4).wait()
            build_weight()

        exchange_wait(2 * p)

        @pl.when(p == 2)
        def _():
            total = sum_tiles(lambda s: recv[2 * p, s], n_order)
            norm, cross = pair_at(total, 7, 0), pair_at(total, 7, 2)
            ratio = [norm[0] / cross[0], norm[1] / cross[1]]
            step = rows_from(ratio)
            steps[0] = jnp.broadcast_to(rows_from(norm), (8, 128))
            steps[1] = jnp.broadcast_to(step, (8, 128))
            steps[2] = jnp.broadcast_to(ratio[0], (8, 128))
            steps[3] = jnp.broadcast_to(ratio[1], (8, 128))
            sums = [jnp.zeros((8, 1), F32)] * 4
            for quad in range(2):
                for r1, held, inv in ((r1_live, live, prior_live), (r1_dead, dead, prior_dead)):
                    before = held[1, quad]
                    after = before - step * held[2, quad]
                    r1[quad] = after
                    scaled = inv[quad] * after
                    sums = [total + lane_sum(value) for total, value in zip(
                        sums, (after * after, scaled * after, scaled * before, inv[quad] * before * before))]
            scalar[...] = put_scalars([value for total in sums for value in by_realization(total)])

        def shuffle(g, inner_carry):
            lanes = pl.ds(pl.multiple_of(g * 128, 128), 128)
            flip = sign[:, lanes]
            held = [recv[2 * p, g * 8 + i] for i in range(8)]
            straight = []
            for hr in range(4):
                acc = held[0] if hr == 0 else pltpu.roll(held[0], (128 - 16 * hr) % 128, 1)
                for i in range(1, 8):
                    by = (16 * i - 16 * hr) % 128
                    moved = held[i] if by == 0 else pltpu.roll(held[i], by, 1)
                    acc = jnp.where(group8 == i, moved, acc)
                straight.append(acc)
            flipped = [acc * flip for acc in straight]
            rows = jnp.concatenate(straight + flipped, axis=0)
            high, rest = split_bf16(rows)
            flhs[0:64, lanes] = high
            flhs[64:128, lanes] = rest
            return inner_carry

        lax.fori_loop(0, groups, shuffle, 0)

        anal[...] = jnp.zeros_like(anal)
        chunk = min(512, half_turn)

        def fourier(t, inner_carry):
            lanes = pl.ds(pl.multiple_of(t * chunk, 128), chunk)
            block = table[:, lanes]
            sky = jnp.dot(flhs[...], block, preferred_element_type=F32)
            sky = sky[0:64] + sky[64:128]
            scaled = sky * weight[:, :, lanes].reshape(64, chunk)
            high, rest = split_bf16(scaled)
            out = lax.dot_general(jnp.concatenate([high, rest], axis=0), block, NT, preferred_element_type=F32)
            anal[...] += out[0:64] + out[64:128]

            @pl.when(p == 1)
            def _():
                sky_kept[:, lanes] = sky

            @pl.when(p == 2)
            def _():
                for hr in range(8):
                    rows = slice(8 * hr, 8 * hr + 8)
                    before = sky_kept[rows, lanes]
                    after = before - steps[2 + hr % 2][:, 0:1] * sky[rows]
                    weighed = weight[hr, :, lanes]
                    heavy = weighed * after
                    for at, value in enumerate((heavy * after, heavy * before, weighed * before * before)):
                        total = pixel_sums[2 * at + hr % 2]
                        for k in range(chunk // 128):
                            total = total + value[:, 128 * k:128 * k + 128]
                        pixel_sums[2 * at + hr % 2] = total

            return inner_carry

        lax.fori_loop(0, half_turn // chunk, fourier, 0)

        @pl.when(p == 2)
        def _():
            tile = scalar[...]
            for at in range(6):
                value = jnp.sum(lane_sum(pixel_sums[at]), axis=0, keepdims=True)
                tile = jnp.where(item8 == 8 + at, value, tile)
            scalar[...] = tile

        def shuffle_back(g, inner_carry):
            lanes = pl.ds(pl.multiple_of(g * 128, 128), 128)
            flip = sign[:, lanes]
            rows = [anal[8 * hr:8 * hr + 8, lanes] + flip * anal[32 + 8 * hr:40 + 8 * hr, lanes] for hr in range(4)]
            base = scalar[...]
            for i in range(8):
                acc = jnp.zeros((8, 128), F32)
                for hr in range(4):
                    by = (16 * hr - 16 * i) % 128
                    moved = rows[hr] if by == 0 else pltpu.roll(rows[hr], by, 1)
                    acc = jnp.where(group8 == hr, moved, acc)
                send[g * 8 + i] = jnp.where(row8 < cycles, acc, base)
            return inner_carry

        lax.fori_loop(0, groups, shuffle_back, 0)
        exchange_start(2 * p + 1)

        @pl.when(p == 0)
        def _():
            for at in (0, 1, 2, 5, 6):
                load_copy(at).wait()

        for quad in range(2):
            image = prior_dead[quad] * dead[p, quad]
            dead[p + 1, quad] = jnp.where(p == 0, rhs_dead[quad] - image, image)
        exchange_wait(2 * p + 1)

        for d in range(n_order):
            turned[cycles * d:cycles * d + cycles, :] = recv[2 * p + 1, d, 0:cycles, :]
        for sheet in range(sheets):
            back[sheet] = turned[128 * sheet:128 * sheet + 128, :].T

        for quad in range(2):
            for half in range(2):
                pair = 2 * quad + half
                rows = jnp.concatenate([
                    jnp.concatenate([back[sheet, pl.ds(2 * pair + slot, 8, stride=8), :] for sheet in range(sheets)],
                                    axis=1)
                    for slot in range(2)], axis=0)
                high, rest = split_bf16(rows[:, 0:local])
                both = jnp.concatenate([high, rest], axis=0)
                mine_rows = slice(4 * half, 4 * half + 4)
                one_row = slice(4 * half, 4 * half + 1)

                def analyse(t, inner_carry):
                    at = pl.ds(pl.multiple_of(t * 2 * part, 128), 2 * part)
                    out = jnp.dot(both, leg[pair, :, at], preferred_element_type=F32)
                    out = out[0:16] + out[16:32]
                    kept = jnp.where(mask[quad, one_row, at] > 0.5, out[0:8], out[8:16])
                    value = kept[0:4] + parity[quad, one_row, at] * kept[4:8]
                    partial[quad, 2 * t, mine_rows, 0:part] = value[:, 0:part]
                    partial[quad, 2 * t + 1, mine_rows, 0:part] = value[:, part:2 * part]
                    return inner_carry

                lax.fori_loop(0, n_blk // 2, analyse, 0)
                out = jnp.dot(both, leg[pair, :, degrees:degrees + 128], preferred_element_type=F32)
                out = out[0:16] + out[16:32]
                extras[quad, mine_rows, :] = out[8:12] + out[12:16]
            if quad == 1:
                total = sum_tiles(lambda s: recv[2 * p + 1, s], n_order)
                tile = jnp.where(lane8 == 0, extras[0], 0.0)
                tile = jnp.where(lane8 == 1, pltpu.roll(extras[1], 1, 1), tile)
                scalar[...] = total
                tile = jnp.where((lane8 >= 64) & (row8 == 7), total, tile)
                for b in range(n_blk):
                    partial[1, b, :, part:part + 128] = tile
            for to in partners:
                source = partial.at[0, to, :, pl.ds(0, part)] if quad == 0 else partial.at[1, to]
                target = rs_recv0 if quad == 0 else rs_recv1
                pltpu.make_async_remote_copy(
                    src_ref=source, dst_ref=target.at[p, mine],
                    send_sem=rs_send.at[p, quad], recv_sem=rs_arrive.at[p, quad],
                    device_id=(me, to), device_id_type=MESH).start()

        my_lanes = pl.ds(pl.multiple_of(mine * part, 128), part)
        for quad in range(2):
            arrived = rs_recv0 if quad == 0 else rs_recv1
            arrived[p, mine] = partial[quad, mine, :, 0:arrived.shape[3]]
            wait_bytes(arrived.at[p, pl.ds(0, n_blk - 1)], rs_arrive.at[p, quad])
            total = sum_tiles(lambda b: arrived[p, b], n_blk)
            shard[quad] = total[:, 0:part]
            for to in partners:
                pltpu.make_async_remote_copy(
                    src_ref=shard.at[quad], dst_ref=summed.at[p, quad, :, my_lanes],
                    send_sem=ag_send.at[p, quad], recv_sem=ag_arrive.at[p, quad],
                    device_id=(me, to), device_id_type=MESH).start()
            summed[p, quad, :, my_lanes] = total[:, 0:part]
            wait_bytes(arrived.at[p, pl.ds(0, n_blk - 1)], rs_send.at[p, quad])
        tile = total[:, part:part + 128]
        extra_sum[0] = jnp.where(lane8 == 0, tile, 0.0)
        extra_sum[1] = jnp.where(lane8 == 0, pltpu.roll(tile, 127, 1), 0.0)
        extra_sum[2] = tile
        return carry

    lax.fori_loop(0, 3, application, 0)

    within_order, over_all = scalar[...], extra_sum[2]
    norm = [steps[0, 0:1, 0:1], steps[0, 2:3, 0:1]]
    ratios, seconds = [], []
    for r in range(2):
        after = scalar_at(within_order, 7, r)
        ratio = after / norm[r]
        curve = (scalar_at(within_order, 7, 2 + r) + scalar_at(over_all, 7, 8 + r)
                 + 2.0 * ratio * (scalar_at(within_order, 7, 4 + r) + scalar_at(over_all, 7, 10 + r))
                 + ratio * ratio * (scalar_at(within_order, 7, 6 + r) + scalar_at(over_all, 7, 12 + r)))
        ratios.append(ratio)
        seconds.append(after / curve)
    ratio, second = rows_from(ratios), rows_from(seconds)
    step = steps[1, :, 0:1]

    def finish(quad, lanes, held, r1, last, x_out, r_out):
        before, middle = held[1, quad, :, lanes], held[2, quad, :, lanes]
        after = r1[quad, :, lanes]
        direction = after + ratio * before
        image = (1.0 + ratio) * middle - step * last
        x_out[quad, :, lanes] = held[0, quad, :, lanes] + step * before + second * direction
        r_out[quad, :, lanes] = after - second * image

    main, tail = pl.ds(0, degrees), pl.ds(degrees, 128)
    for quad in range(2):
        finish(quad, main, dead, r1_dead, dead[3, quad], x_out_dead, r_out_dead)
        last = prior_live[quad, :, tail] * live[2, quad, :, tail] + extra_sum[quad]
        finish(quad, tail, live, r1_live, last, x_out_live, r_out_live)
    for quad in range(2):
        wait_bytes(rs_recv0.at[2, pl.ds(0, n_blk - 1)], ag_arrive.at[2, quad])
        last = prior_live[quad, :, main] * live[2, quad, :, main] + summed[2, quad]
        finish(quad, main, live, r1_live, last, x_out_live, r_out_live)
    for quad in range(2):
        wait_bytes(rs_recv0.at[2, pl.ds(0, n_blk - 1)], ag_send.at[2, quad])


def per_device(n_order, n_blk, right_side, start_guess, legendre, orders, prior_inv, noise_inv, pixel_flags):
    slots, local, degrees = legendre.shape
    cycles, pixels = noise_inv.shape[1], noise_inv.shape[2]
    width = degrees + 128
    part = degrees // n_blk
    smem = pl.BlockSpec(memory_space=pltpu.SMEM)
    vmem = pl.BlockSpec(memory_space=pltpu.VMEM)
    hbm = pl.BlockSpec(memory_space=pl.ANY)
    live_shape = jax.ShapeDtypeStruct((2, 8, width), F32)
    dead_shape = jax.ShapeDtypeStruct((2, 8, degrees), F32)
    columns = 16 * n_order
    sheets = -(-(local + 8) // 128)
    half_turn = pixels // 2
    rows_step = local // 2 if (local // 2) % 16 == 0 else local
    packed = pl.pallas_call(
        functools.partial(pack_kernel, degrees, rows_step),
        grid=(4, local // rows_step),
        in_specs=[smem, pl.BlockSpec((1, 2, rows_step, degrees), lambda k, b: (k, 0, b, 0)), vmem, vmem, vmem],
        out_specs=[pl.BlockSpec((1, rows_step, width), lambda k, b: (k, b, 0))] + [vmem] * 9,
        out_shape=[jax.ShapeDtypeStruct((4, local, width), BF16), jax.ShapeDtypeStruct((8, 128), jnp.int32)]
        + [live_shape, dead_shape] * 3 + [live_shape] * 2,
        scratch_shapes=[pltpu.VMEM((2, 8, degrees), F32)] * 2,
        compiler_params=pltpu.CompilerParams(vmem_limit_bytes=VMEM_LIMIT),
        name="pack",
    )(orders, legendre.reshape(4, 2, local, degrees), right_side, start_guess, prior_inv.reshape(1, degrees))
    leg, numbers, rhs_live, rhs_dead, x_live, x_dead, prior_live, prior_dead, mask, parity = packed

    scratch = [
        pltpu.VMEM((4, local, width), BF16),
        pltpu.VMEM((3, 2, 8, width), F32),
        pltpu.VMEM((4, 2, 8, degrees), F32),
        pltpu.VMEM((2, 8, width), F32),
        pltpu.VMEM((2, 8, degrees), F32),
        pltpu.VMEM((2, 8, width), F32),
        pltpu.VMEM((2, 8, degrees), F32),
        pltpu.VMEM((cycles, 2, pixels), F32),
        pltpu.VMEM((cycles, 2, pixels), jnp.int32),
        pltpu.VMEM((2, 64, width), BF16),
        pltpu.VMEM((sheets, 128, 128), F32),
        pltpu.VMEM((sheets * 128, 128), F32),
        pltpu.VMEM((sheets, 128, 128), F32),
        pltpu.VMEM((n_order, 8, 128), F32),
        pltpu.VMEM((6, n_order, 8, 128), F32),
        pltpu.VMEM((n_order, 8, 128), jnp.int32),
        pltpu.VMEM((8, 128), F32),
        pltpu.VMEM((128, columns), BF16),
        pltpu.VMEM((8, 8, half_turn), F32),
        pltpu.VMEM((64, columns), F32),
        pltpu.VMEM((8, columns), F32),
        pltpu.VMEM((n_order, 2, 8, 128), F32),
        pltpu.VMEM((n_order, 2, 8, 128), F32),
        pltpu.VMEM((columns, half_turn), BF16),
        pltpu.VMEM((64, half_turn), F32),
        pltpu.VMEM((6, 8, 128), F32),
        pltpu.VMEM((2, n_blk, 8, part + 128), F32),
        pltpu.VMEM((2, 8, 128), F32),
        pltpu.VMEM((2, 8, part), F32),
        pltpu.VMEM((3, n_blk, 8, part), F32),
        pltpu.VMEM((3, n_blk, 8, part + 128), F32),
        pltpu.VMEM((3, 2, 8, degrees), F32),
        pltpu.VMEM((3, 8, 128), F32),
        pltpu.VMEM((2, 8, width), F32),
        pltpu.VMEM((2, 8, degrees), F32),
        pltpu.VMEM((4, 8, 128), F32),
        pltpu.SemaphoreType.DMA((4,)),
        pltpu.SemaphoreType.DMA((7,)),
        pltpu.SemaphoreType.DMA((2,)),
        pltpu.SemaphoreType.DMA((6,)),
        pltpu.SemaphoreType.DMA((6,)),
        pltpu.SemaphoreType.DMA((3, 2)),
        pltpu.SemaphoreType.DMA((3, 2)),
        pltpu.SemaphoreType.DMA((3, 2)),
        pltpu.SemaphoreType.DMA((3, 2)),
    ]
    results = pl.pallas_call(
        functools.partial(main_kernel, n_order, n_blk, degrees, cycles, pixels),
        in_specs=[vmem, hbm, hbm, hbm, vmem, hbm, hbm, hbm, vmem, vmem, hbm, hbm],
        out_specs=[vmem] * 4,
        out_shape=[live_shape, dead_shape, live_shape, dead_shape],
        scratch_shapes=scratch,
        compiler_params=pltpu.CompilerParams(
            collective_id=0, has_side_effects=True, vmem_limit_bytes=VMEM_LIMIT),
        name="steps",
    )(numbers, leg, rhs_live, rhs_dead, x_live, x_dead, prior_live, prior_dead, mask, parity,
      noise_inv.transpose(1, 0, 2), pixel_flags.transpose(1, 0, 2))

    full = jax.ShapeDtypeStruct(right_side.shape, F32)
    return tuple(pl.pallas_call(
        functools.partial(unpack_kernel, degrees),
        in_specs=[smem] + [vmem] * 4,
        out_specs=[vmem] * 2,
        out_shape=[full, full],
        scratch_shapes=[pltpu.VMEM((2, 8, degrees), F32)] * 2,
        compiler_params=pltpu.CompilerParams(vmem_limit_bytes=VMEM_LIMIT),
        name="unpack",
    )(orders, *results))


def solution(mesh):
    in_specs = (
        P(None, None, "order", None),
        P(None, None, "order", None),
        P("order", "blk", None),
        P("order"),
        P(),
        P(None, ("blk", "order"), None),
        P(None, ("blk", "order"), None),
    )
    out_specs = (P(None, None, "order", None), P(None, None, "order", None))
    body = functools.partial(per_device, mesh.shape["order"], mesh.shape["blk"])
    return jax.shard_map(body, mesh=mesh, in_specs=in_specs, out_specs=out_specs, check_vma=False)
```

```python
import functools

import jax
import jax.numpy as jnp
from jax import lax
from jax.experimental import pallas as pl
from jax.experimental.pallas import tpu as pltpu
from jax.sharding import PartitionSpec as P

MESH = pl.DeviceIdType.MESH
F32 = jnp.float32
BF16 = jnp.bfloat16
VMEM_LIMIT = 56 * 1024 * 1024
PACK_VMEM = 56 * 1024 * 1024
NT = (((1,), (1,)), ((), ()))


def iota(shape, dim):
    return lax.broadcasted_iota(jnp.int32, shape, dim)


def tile_lanes(t, shift, less, tiles):
    at = lax.rem(t - shift // 128 - less + 2 * tiles, tiles) * 128
    return pl.ds(pl.multiple_of(at, 128), 128)


def rolled_tiles(load, shift, tiles, lane):
    within = lax.rem(shift, 128)
    before = pltpu.roll(load(tile_lanes(0, shift, 1, tiles)), within, 1)
    for t in range(tiles):
        now = pltpu.roll(load(tile_lanes(t, shift, 0, tiles)), within, 1)
        yield jnp.where(lane >= within, now, before)
        before = now


def pack_kernel(degrees, span, orders, leg_hbm, rhs, guess, prior,
                leg_out, numbers, rhs_live, rhs_dead, x_live, x_dead, prior_live, prior_dead,
                mask, parity, stage, packed, rows_a, rows_b, in_sems, out_sems):
    tiles = degrees // 128
    blocks = tiles // span
    local = packed.shape[1]
    lane16 = iota((16, 128), 1)
    lane8 = iota((8, 128), 1)
    row8 = iota((8, 128), 0)
    upper = row8 < 4

    for pair in range(4):
        own_blocks = orders[2 * pair] // (128 * span)
        for j in range(blocks + 1):
            second = j <= own_blocks
            slot = 2 * pair + jnp.where(second, 1, 0)
            column = jnp.where(second, blocks - 1 - own_blocks + j, j - 1) * (128 * span)
            lanes = pl.ds(pl.multiple_of(column, 128), 128 * span)
            pltpu.make_async_copy(leg_hbm.at[slot, :, lanes],
                                  stage.at[pair, :, pl.ds(j * 128 * span, 128 * span)], in_sems.at[pair]).start()

    tile = jnp.zeros((8, 128), jnp.int32)
    for m in range(8):
        tile = jnp.where(row8 == m, orders[m], tile)
    numbers[...] = tile
    tail = slice(degrees, degrees + 128)
    sources = [(rhs, rhs_live, rhs_dead), (guess, x_live, x_dead)]
    for quad in range(2):
        low, high = orders[4 * quad], orders[4 * quad + 2]
        shifts = jnp.where(upper, low, high)
        number_b = jnp.where(upper, orders[4 * quad + 1], orders[4 * quad + 3])
        for at, (source, live, dead) in enumerate(sources):
            for half in range(2):
                slot = 4 * quad + 2 * half
                for r in range(2):
                    for c in range(2):
                        row = half * 4 + r * 2 + c
                        rows_a[quad, at, row:row + 1, :] = source[r, c, slot:slot + 1, :]
                        rows_b[quad, at, row:row + 1, :] = source[r, c, slot + 1:slot + 2, :]

        def both(load):
            for one, two in zip(rolled_tiles(load, low, tiles, lane8), rolled_tiles(load, high, tiles, lane8)):
                yield jnp.where(upper, one, two)

        for at, (source, live, dead) in enumerate(sources):
            for t, rolled in enumerate(both(lambda lanes: rows_b[quad, at, :, lanes])):
                lanes = slice(t * 128, t * 128 + 128)
                own = lane8 + t * 128 >= shifts
                first = rows_a[quad, at, :, lanes]
                idle = jnp.where(own, rolled, first)
                if t == tiles - 1:
                    idle = jnp.where(lane8 == 127, 0.0, idle)
                live[quad, :, lanes] = jnp.where(own, first, rolled)
                dead[quad, :, lanes] = idle
            live[quad, :, tail] = jnp.where(lane8 == 0, pltpu.roll(rolled, 1, 1), 0.0)
        for t, rolled in enumerate(both(lambda lanes: jnp.broadcast_to(prior[:, lanes], (8, 128)))):
            lanes = slice(t * 128, t * 128 + 128)
            place = lane8 + t * 128
            own = place >= shifts
            first = jnp.broadcast_to(prior[:, lanes], (8, 128))
            prior_live[quad, :, lanes] = jnp.where(own, first, rolled)
            prior_dead[quad, :, lanes] = jnp.where(own, rolled, first)
            total = jnp.where(own, place + shifts, place - shifts + degrees + number_b)
            parity[quad, :, lanes] = (1 - 2 * (total & 1)).astype(F32)
            mask[quad, :, lanes] = own.astype(F32)
        prior_live[quad, :, tail] = jnp.where(lane8 == 0, pltpu.roll(rolled, 1, 1), 0.0)
        parity[quad, :, tail] = jnp.ones((8, 128), F32)
        mask[quad, :, tail] = jnp.zeros((8, 128), F32)

    for pair in range(4):
        shift = orders[2 * pair]
        within = lax.rem(shift, 128)
        back = span - 1 - lax.rem(shift // 128, span)
        pltpu.make_async_copy(stage.at[pair], stage.at[pair], in_sems.at[pair]).wait()

        def rows_of(step, carry):
            rows = pl.ds(pl.multiple_of(step * 16, 16), 16)

            def moved(t):
                lanes = pl.ds(pl.multiple_of((t + back) * 128, 128), 128)
                return pltpu.roll(stage[pair, rows, lanes], within, 1)

            before = moved(0)
            extra = jnp.where(lane16 == 0, pltpu.roll(before, 1, 1), jnp.zeros_like(before))
            packed[pair, rows, degrees:degrees + 128] = extra
            for t in range(tiles):
                now = moved(t + 1)
                rolled = jnp.where(lane16 >= within, now, before)
                first = stage[pair, rows, (t + span) * 128:(t + span) * 128 + 128]
                packed[pair, rows, t * 128:t * 128 + 128] = jnp.where(lane16 + t * 128 >= shift, first, rolled)
                before = now
            return carry

        lax.fori_loop(0, local // 16, rows_of, 0, unroll=4 if local % 64 == 0 else 1)
        pltpu.make_async_copy(packed.at[pair], leg_out.at[pair], out_sems.at[pair]).start()
    for pair in range(4):
        pltpu.make_async_copy(packed.at[pair], leg_out.at[pair], out_sems.at[pair]).wait()


def unpack_kernel(degrees, orders, x_live, x_dead, r_live, r_dead, x_out, r_out, rows_a, rows_b):
    tiles = degrees // 128
    lane8 = iota((8, 128), 1)
    upper = iota((8, 128), 0) < 4
    for quad in range(2):
        low, high = orders[4 * quad], orders[4 * quad + 2]
        shifts = jnp.where(upper, low, high)
        back_low, back_high = lax.rem(degrees - low, degrees), lax.rem(degrees - high, degrees)
        for at, (live, dead, out) in enumerate(((x_live, x_dead, x_out), (r_live, r_dead, r_out))):
            for t in range(tiles):
                lanes = slice(t * 128, t * 128 + 128)
                own = lane8 + t * 128 >= shifts
                alive, idle = live[quad, :, lanes], dead[quad, :, lanes]
                rows_a[at, :, lanes] = jnp.where(own, alive, idle)
                second = jnp.where(own, idle, alive)
                if t == tiles - 1:
                    extra = live[quad, :, degrees:degrees + 128]
                    second = jnp.where(lane8 == 127, pltpu.roll(extra, 127, 1), second)
                rows_b[at, :, lanes] = second
            load = lambda lanes: rows_b[at, :, lanes]
            back = zip(rolled_tiles(load, back_low, tiles, lane8), rolled_tiles(load, back_high, tiles, lane8))
            kept = [jnp.where(upper, one, two) for one, two in back]
            for t, value in enumerate(kept):
                rows_b[at, :, t * 128:t * 128 + 128] = value
            for half in range(2):
                slot = 4 * quad + 2 * half
                for r in range(2):
                    for c in range(2):
                        row = half * 4 + r * 2 + c
                        out[r, c, slot:slot + 1, :] = rows_a[at, row:row + 1, :]
                        out[r, c, slot + 1:slot + 2, :] = rows_b[at, row:row + 1, :]


def split_bf16(values):
    high = values.astype(BF16)
    return high, (values - high.astype(F32)).astype(BF16)


def main_kernel(n_order, n_blk, degrees, cycles, pixels,
                own_orders, leg_hbm, rhs_live_hbm, rhs_dead_hbm, x_live, x_dead_hbm, prior_live_hbm, prior_dead_hbm,
                mask, parity, noise_hbm, flags_hbm,
                x_out_live, x_out_dead, r_out_live, r_out_dead,
                leg, live, dead, rhs_live, rhs_dead, prior_live, prior_dead, noise, flags,
                lhs, modes, turned, back, send, recv, order_recv, scalar,
                flhs, weight, anal, sign, current, turn, table, sky_kept, pixel_sums,
                partial, extras, shard, rs_recv0, rs_recv1, summed, extra_sum,
                r1_live, r1_dead, steps,
                leg_sems, load_sems, order_sems, a2a_send, a2a_recv, rs_send, rs_arrive, ag_send, ag_arrive):
    me = lax.axis_index("order")
    mine = lax.axis_index("blk")
    tiles = degrees // 128
    half_turn = pixels // 2
    columns = 16 * n_order
    groups = columns // 128
    local = cycles * n_order
    part = degrees // n_blk
    sheets = modes.shape[0]

    def leg_copy(pair):
        return pltpu.make_async_copy(leg_hbm.at[pair], leg.at[pair], leg_sems.at[pair])

    def load_copy(at):
        source, target = ((x_dead_hbm, dead.at[0]), (prior_live_hbm, prior_live), (prior_dead_hbm, prior_dead),
                          (noise_hbm, noise), (flags_hbm, flags), (rhs_live_hbm, rhs_live),
                          (rhs_dead_hbm, rhs_dead))[at]
        return pltpu.make_async_copy(source, target, load_sems.at[at])

    for pair in range(4):
        leg_copy(pair).start()
    for at in range(7):
        load_copy(at).start()

    side_x = 2
    side_y = n_order // 4
    if n_order == 32:
        side_x, side_y = 4, 4
    offsets = [(a, b, c) for a in range(side_y) for b in range(side_x) for c in range(2) if a or b or c]
    offsets.sort(key=lambda o: -(2 * min(o[0], side_y - o[0]) + 2 * min(o[1], side_x - o[1]) + o[2]))
    my_y, my_x, my_c = me // (2 * side_x), (me // 2) % side_x, me % 2
    peers = [lax.rem(my_y + a, side_y) * (2 * side_x) + lax.rem(my_x + b, side_x) * 2 + lax.rem(my_c + c, 2)
             for a, b, c in offsets]
    steps_z = sorted(range(1, n_blk), key=lambda i: -min(i, n_blk - i))
    partners = [lax.rem(mine + i, n_blk) for i in steps_z]

    barrier = pltpu.get_barrier_semaphore()
    for to in peers:
        pl.semaphore_signal(barrier, inc=1, device_id=(to, mine), device_id_type=MESH)
    for to in partners:
        pl.semaphore_signal(barrier, inc=1, device_id=(me, to), device_id_type=MESH)

    def wait_bytes(ref, sem):
        pltpu.make_async_copy(ref, ref, sem).wait()

    row8 = iota((8, 128), 0)
    lane8 = iota((8, 128), 1)
    modes[...] = jnp.zeros_like(modes)
    turned[...] = jnp.zeros_like(turned)
    scalar[...] = jnp.zeros_like(scalar)
    pixel_sums[...] = jnp.zeros_like(pixel_sums)
    live[0] = x_live[...]

    pl.semaphore_wait(barrier, n_order - 1 + n_blk - 1)

    for to in peers:
        pltpu.make_async_remote_copy(
            src_ref=own_orders, dst_ref=order_recv.at[me],
            send_sem=order_sems.at[0], recv_sem=order_sems.at[1],
            device_id=(to, mine), device_id_type=MESH).start()
    order_recv[me] = own_orders[...]

    def exchange_start(step):
        for to in peers:
            pltpu.make_async_remote_copy(
                src_ref=send.at[to], dst_ref=recv.at[step, me],
                send_sem=a2a_send.at[step], recv_sem=a2a_recv.at[step],
                device_id=(to, mine), device_id_type=MESH).start()
        recv[step, me] = send[me]

    def exchange_wait(step):
        wait_bytes(recv.at[step, pl.ds(0, n_order - 1)], a2a_recv.at[step])
        wait_bytes(send.at[pl.ds(0, n_order - 1)], a2a_send.at[step])

    def build_weight():
        weight[...] = jnp.zeros_like(weight)
        for j in range(cycles):
            value = noise[j] * flags[j].astype(F32)
            for h in range(2):
                for image in range(2):
                    row = value[h:h + 1, image * half_turn:(image + 1) * half_turn]
                    for r in range(2):
                        weight[image * 4 + h * 2 + r, j:j + 1, :] = row

    def build_table():
        wait_bytes(order_recv.at[pl.ds(0, n_order - 1)], order_sems.at[1])
        wait_bytes(order_recv.at[pl.ds(0, n_order - 1)], order_sems.at[0])
        number = order_recv[...]
        lane = iota((n_order, 8, 128), 2)
        scale = jnp.where(number == 0, 1.0, 2.0) * (pixels ** -0.5)

        def angle(product):
            value = product.astype(F32)
            value = value - pixels * jnp.floor(value * (1.0 / pixels))
            return value * (2.0 * jnp.pi / pixels)

        base = angle(number * lane)
        current[:, 0] = scale * jnp.cos(base)
        current[:, 1] = -scale * jnp.sin(base)
        step = angle(number * 128)
        turn[:, 0] = jnp.cos(step)
        turn[:, 1] = jnp.sin(step)
        odd = (1 - 2 * (number & 1)).astype(F32)
        sign_rows = jnp.concatenate([odd, odd], axis=1).reshape(columns, 128)
        sign[...] = sign_rows.T[0:8]

        def block(q, carry):
            lanes = pl.ds(pl.multiple_of(q * 128, 128), 128)

            def some(piece, inner):
                for k in range(8):
                    s = piece * 8 + k
                    cosine, sine = current[s, 0], current[s, 1]
                    rows = pl.ds(pl.multiple_of(s * 16, 16), 16)
                    table[rows, lanes] = jnp.concatenate([cosine, sine], axis=0).astype(BF16)
                    turn_c, turn_s = turn[s, 0], turn[s, 1]
                    current[s, 0] = cosine * turn_c + sine * turn_s
                    current[s, 1] = sine * turn_c - cosine * turn_s
                return inner

            return lax.fori_loop(0, n_order // 8, some, carry)

        lax.fori_loop(0, half_turn // 128, block, 0)

    group8 = lane8 // 16
    item8 = lane8 // 8
    first_row8 = (iota((8, 1), 0) % 4) < 2

    def by_realization(total):
        zero = jnp.sum(jnp.where(first_row8, total, 0.0), axis=0, keepdims=True)
        one = jnp.sum(jnp.where(first_row8, 0.0, total), axis=0, keepdims=True)
        return [zero, one]

    def lane_sum(value):
        return jnp.sum(value, axis=1, keepdims=True)

    def put_scalars(values):
        tile = jnp.zeros((8, 128), F32)
        for at, value in enumerate(values):
            tile = jnp.where(item8 == at, value, tile)
        return tile

    def sum_tiles(load, count):
        values = [load(s) for s in range(count)]
        while len(values) > 1:
            values = [a + b for a, b in zip(values[::2], values[1::2])]
        return values[0]

    def scalar_at(total, row, at):
        return total[row:row + 1, 8 * at:8 * at + 1]

    def rows_from(pair):
        return jnp.where(first_row8, pair[0], pair[1])

    def pair_at(total, row, at):
        return [scalar_at(total, row, at), scalar_at(total, row, at + 1)]

    lane_step = 128 * max(n for n in (5, 3, 1) if (tiles + 1) % n == 0)
    width = degrees + 128

    def application(p, carry):
        for quad in range(2):
            @pl.when(p > 0)
            def _():
                wait_bytes(rs_recv0.at[p - 1, pl.ds(0, n_blk - 1)], ag_arrive.at[p - 1, quad])
                main = pl.ds(0, degrees)
                image = prior_live[quad, :, main] * live[p - 1, quad, :, main] + summed[p - 1, quad]
                live[p, quad, :, main] = jnp.where(p == 1, rhs_live[quad, :, main] - image, image)
                tail = pl.ds(degrees, 128)
                image = prior_live[quad, :, tail] * live[p - 1, quad, :, tail] + extra_sum[quad]
                live[p, quad, :, tail] = jnp.where(p == 1, rhs_live[quad, :, tail] - image, image)

            def build(t, inner_carry):
                at = pl.ds(t * lane_step, lane_step)
                value = live[p, quad, :, at]
                first = mask[quad, :, at]
                second = 1.0 - first
                flip = parity[quad, :, at]
                high = value.astype(BF16).astype(F32)
                rest = value - high
                pieces = []
                for piece in (high, rest):
                    for keep in (first, second):
                        kept = piece * keep
                        pieces.append(kept)
                        pieces.append(kept * flip)
                lhs[quad, :, at] = jnp.concatenate(pieces, axis=0).astype(BF16)
                return inner_carry

            for t in range(width // lane_step):
                build(t, 0)
            for half in range(2):
                pair = 2 * quad + half

                @pl.when(p == 0)
                def _():
                    leg_copy(pair).wait()

                out = lax.dot_general(lhs[quad], leg[pair], NT, preferred_element_type=F32)
                out = out[0:32] + out[32:64]
                at = 4 * half
                for slot in range(2):
                    rows = jnp.concatenate([out[16 * slot + at:16 * slot + at + 4],
                                            out[16 * slot + 8 + at:16 * slot + 8 + at + 4]], axis=0)
                    if sheets * 128 > local:
                        rows = jnp.concatenate([rows, jnp.zeros((8, sheets * 128 - local), F32)], axis=1)
                    for sheet in range(sheets):
                        modes[sheet, pl.ds(2 * pair + slot, 8, stride=8), :] = rows[:, 128 * sheet:128 * sheet + 128]

        @pl.when(p > 0)
        def _():
            for quad in range(2):
                wait_bytes(rs_recv0.at[p - 1, pl.ds(0, n_blk - 1)], ag_send.at[p - 1, quad])

        for sheet in range(sheets):
            turned[128 * sheet:128 * sheet + 128, :] = modes[sheet].T

        @pl.when(p == 2)
        def _():
            norm = cross = jnp.zeros((8, 1), F32)
            for quad in range(2):
                for held in (live, dead):
                    norm = norm + lane_sum(held[1, quad] * held[1, quad])
                    cross = cross + lane_sum(held[1, quad] * held[2, quad])
            scalar[...] = put_scalars(by_realization(norm) + by_realization(cross))

        for d in range(n_order):
            send[d] = jnp.where(row8 < cycles, turned[cycles * d:cycles * d + 8, :], scalar[...])
        exchange_start(2 * p)

        @pl.when(p == 0)
        def _():
            build_table()
            load_copy(3).wait()
            load_copy(4).wait()
            build_weight()

        exchange_wait(2 * p)

        @pl.when(p == 2)
        def _():
            total = sum_tiles(lambda s: recv[2 * p, s], n_order)
            norm, cross = pair_at(total, 7, 0), pair_at(total, 7, 2)
            ratio = [norm[0] / cross[0], norm[1] / cross[1]]
            step = rows_from(ratio)
            steps[0] = jnp.broadcast_to(rows_from(norm), (8, 128))
            steps[1] = jnp.broadcast_to(step, (8, 128))
            steps[2] = jnp.broadcast_to(ratio[0], (8, 128))
            steps[3] = jnp.broadcast_to(ratio[1], (8, 128))
            sums = [jnp.zeros((8, 1), F32)] * 4
            for quad in range(2):
                for r1, held, inv in ((r1_live, live, prior_live), (r1_dead, dead, prior_dead)):
                    before = held[1, quad]
                    after = before - step * held[2, quad]
                    r1[quad] = after
                    scaled = inv[quad] * after
                    sums = [total + lane_sum(value) for total, value in zip(
                        sums, (after * after, scaled * after, scaled * before, inv[quad] * before * before))]
            scalar[...] = put_scalars([value for total in sums for value in by_realization(total)])

        def shuffle(g, inner_carry):
            lanes = pl.ds(g * 128, 128)
            flip = sign[:, lanes]
            held = [recv[2 * p, g * 8 + i] for i in range(8)]
            straight = []
            for hr in range(4):
                acc = held[0] if hr == 0 else pltpu.roll(held[0], (128 - 16 * hr) % 128, 1)
                for i in range(1, 8):
                    by = (16 * i - 16 * hr) % 128
                    moved = held[i] if by == 0 else pltpu.roll(held[i], by, 1)
                    acc = jnp.where(group8 == i, moved, acc)
                straight.append(acc)
            flipped = [acc * flip for acc in straight]
            rows = jnp.concatenate(straight + flipped, axis=0)
            high, rest = split_bf16(rows)
            flhs[0:64, lanes] = high
            flhs[64:128, lanes] = rest
            return inner_carry

        for g in range(groups):
            shuffle(g, 0)

        anal[...] = jnp.zeros_like(anal)
        chunk = min(1536, half_turn)

        def fourier(t, inner_carry):
            lanes = pl.ds(pl.multiple_of(t * chunk, 128), chunk)
            block = table[:, lanes]
            sky = jnp.dot(flhs[...], block, preferred_element_type=F32)
            sky = sky[0:64] + sky[64:128]
            scaled = sky * weight[:, :, lanes].reshape(64, chunk)
            high, rest = split_bf16(scaled)
            out = lax.dot_general(jnp.concatenate([high, rest], axis=0), block, NT, preferred_element_type=F32)
            anal[...] += out[0:64] + out[64:128]

            @pl.when(p == 1)
            def _():
                sky_kept[:, lanes] = sky

            @pl.when(p == 2)
            def _():
                for hr in range(8):
                    rows = slice(8 * hr, 8 * hr + 8)
                    before = sky_kept[rows, lanes]
                    after = before - steps[2 + hr % 2][:, 0:1] * sky[rows]
                    weighed = weight[hr, :, lanes]
                    heavy = weighed * after
                    for at, value in enumerate((heavy * after, heavy * before, weighed * before * before)):
                        total = pixel_sums[2 * at + hr % 2]
                        for k in range(chunk // 128):
                            total = total + value[:, 128 * k:128 * k + 128]
                        pixel_sums[2 * at + hr % 2] = total

            return inner_carry

        lax.fori_loop(0, half_turn // chunk, fourier, 0)

        @pl.when(p == 2)
        def _():
            tile = scalar[...]
            for at in range(6):
                value = jnp.sum(lane_sum(pixel_sums[at]), axis=0, keepdims=True)
                tile = jnp.where(item8 == 8 + at, value, tile)
            scalar[...] = tile

        def shuffle_back(g, inner_carry):
            lanes = pl.ds(g * 128, 128)
            flip = sign[:, lanes]
            rows = [anal[8 * hr:8 * hr + 8, lanes] + flip * anal[32 + 8 * hr:40 + 8 * hr, lanes] for hr in range(4)]
            base = scalar[...]
            for i in range(8):
                acc = jnp.zeros((8, 128), F32)
                for hr in range(4):
                    by = (16 * hr - 16 * i) % 128
                    moved = rows[hr] if by == 0 else pltpu.roll(rows[hr], by, 1)
                    acc = jnp.where(group8 == hr, moved, acc)
                send[g * 8 + i] = jnp.where(row8 < cycles, acc, base)
            return inner_carry

        for g in range(groups):
            shuffle_back(g, 0)
        exchange_start(2 * p + 1)

        @pl.when(p == 0)
        def _():
            for at in (0, 1, 2, 5, 6):
                load_copy(at).wait()

        for quad in range(2):
            image = prior_dead[quad] * dead[p, quad]
            dead[p + 1, quad] = jnp.where(p == 0, rhs_dead[quad] - image, image)
        exchange_wait(2 * p + 1)

        for d in range(n_order):
            turned[cycles * d:cycles * d + cycles, :] = recv[2 * p + 1, d, 0:cycles, :]
        for sheet in range(sheets):
            back[sheet] = turned[128 * sheet:128 * sheet + 128, :].T

        for quad in range(2):
            for half in range(2):
                pair = 2 * quad + half
                rows = jnp.concatenate([
                    jnp.concatenate([back[sheet, pl.ds(2 * pair + slot, 8, stride=8), :] for sheet in range(sheets)],
                                    axis=1)
                    for slot in range(2)], axis=0)
                high, rest = split_bf16(rows[:, 0:local])
                both = jnp.concatenate([high, rest], axis=0)
                mine_rows = slice(4 * half, 4 * half + 4)
                one_row = slice(4 * half, 4 * half + 1)

                def analyse(t, inner_carry):
                    at = pl.ds(t * 2 * part, 2 * part)
                    out = jnp.dot(both, leg[pair, :, at], preferred_element_type=F32)
                    out = out[0:16] + out[16:32]
                    kept = jnp.where(mask[quad, one_row, at] > 0.5, out[0:8], out[8:16])
                    value = kept[0:4] + parity[quad, one_row, at] * kept[4:8]
                    partial[quad, 2 * t, mine_rows, 0:part] = value[:, 0:part]
                    partial[quad, 2 * t + 1, mine_rows, 0:part] = value[:, part:2 * part]
                    return inner_carry

                for t in range(n_blk // 2):
                    analyse(t, 0)
                out = jnp.dot(both, leg[pair, :, degrees:degrees + 128], preferred_element_type=F32)
                out = out[0:16] + out[16:32]
                extras[quad, mine_rows, :] = out[8:12] + out[12:16]
            if quad == 1:
                total = sum_tiles(lambda s: recv[2 * p + 1, s], n_order)
                tile = jnp.where(lane8 == 0, extras[0], 0.0)
                tile = jnp.where(lane8 == 1, pltpu.roll(extras[1], 1, 1), tile)
                scalar[...] = total
                tile = jnp.where((lane8 >= 64) & (row8 == 7), total, tile)
                for b in range(n_blk):
                    partial[1, b, :, part:part + 128] = tile
            for to in partners:
                source = partial.at[0, to, :, pl.ds(0, part)] if quad == 0 else partial.at[1, to]
                target = rs_recv0 if quad == 0 else rs_recv1
                pltpu.make_async_remote_copy(
                    src_ref=source, dst_ref=target.at[p, mine],
                    send_sem=rs_send.at[p, quad], recv_sem=rs_arrive.at[p, quad],
                    device_id=(me, to), device_id_type=MESH).start()

        my_lanes = pl.ds(pl.multiple_of(mine * part, 128), part)
        for quad in range(2):
            arrived = rs_recv0 if quad == 0 else rs_recv1
            arrived[p, mine] = partial[quad, mine, :, 0:arrived.shape[3]]
            wait_bytes(arrived.at[p, pl.ds(0, n_blk - 1)], rs_arrive.at[p, quad])
            total = sum_tiles(lambda b: arrived[p, b], n_blk)
            shard[quad] = total[:, 0:part]
            for to in partners:
                pltpu.make_async_remote_copy(
                    src_ref=shard.at[quad], dst_ref=summed.at[p, quad, :, my_lanes],
                    send_sem=ag_send.at[p, quad], recv_sem=ag_arrive.at[p, quad],
                    device_id=(me, to), device_id_type=MESH).start()
            summed[p, quad, :, my_lanes] = total[:, 0:part]
            wait_bytes(arrived.at[p, pl.ds(0, n_blk - 1)], rs_send.at[p, quad])
        tile = total[:, part:part + 128]
        extra_sum[0] = jnp.where(lane8 == 0, tile, 0.0)
        extra_sum[1] = jnp.where(lane8 == 0, pltpu.roll(tile, 127, 1), 0.0)
        extra_sum[2] = tile
        return carry

    lax.fori_loop(0, 3, application, 0)

    within_order, over_all = scalar[...], extra_sum[2]
    norm = [steps[0, 0:1, 0:1], steps[0, 2:3, 0:1]]
    ratios, seconds = [], []
    for r in range(2):
        after = scalar_at(within_order, 7, r)
        ratio = after / norm[r]
        curve = (scalar_at(within_order, 7, 2 + r) + scalar_at(over_all, 7, 8 + r)
                 + 2.0 * ratio * (scalar_at(within_order, 7, 4 + r) + scalar_at(over_all, 7, 10 + r))
                 + ratio * ratio * (scalar_at(within_order, 7, 6 + r) + scalar_at(over_all, 7, 12 + r)))
        ratios.append(ratio)
        seconds.append(after / curve)
    ratio, second = rows_from(ratios), rows_from(seconds)
    step = steps[1, :, 0:1]

    def finish(quad, lanes, held, r1, last, x_out, r_out):
        before, middle = held[1, quad, :, lanes], held[2, quad, :, lanes]
        after = r1[quad, :, lanes]
        direction = after + ratio * before
        image = (1.0 + ratio) * middle - step * last
        x_out[quad, :, lanes] = held[0, quad, :, lanes] + step * before + second * direction
        r_out[quad, :, lanes] = after - second * image

    main, tail = pl.ds(0, degrees), pl.ds(degrees, 128)
    for quad in range(2):
        finish(quad, main, dead, r1_dead, dead[3, quad], x_out_dead, r_out_dead)
        last = prior_live[quad, :, tail] * live[2, quad, :, tail] + extra_sum[quad]
        finish(quad, tail, live, r1_live, last, x_out_live, r_out_live)
    for quad in range(2):
        wait_bytes(rs_recv0.at[2, pl.ds(0, n_blk - 1)], ag_arrive.at[2, quad])
        last = prior_live[quad, :, main] * live[2, quad, :, main] + summed[2, quad]
        finish(quad, main, live, r1_live, last, x_out_live, r_out_live)
    for quad in range(2):
        wait_bytes(rs_recv0.at[2, pl.ds(0, n_blk - 1)], ag_send.at[2, quad])


def per_device(n_order, n_blk, right_side, start_guess, legendre, orders, prior_inv, noise_inv, pixel_flags):
    slots, local, degrees = legendre.shape
    cycles, pixels = noise_inv.shape[1], noise_inv.shape[2]
    width = degrees + 128
    part = degrees // n_blk
    smem = pl.BlockSpec(memory_space=pltpu.SMEM)
    vmem = pl.BlockSpec(memory_space=pltpu.VMEM)
    hbm = pl.BlockSpec(memory_space=pl.ANY)
    live_shape = jax.ShapeDtypeStruct((2, 8, width), F32)
    dead_shape = jax.ShapeDtypeStruct((2, 8, degrees), F32)
    columns = 16 * n_order
    sheets = -(-(local + 8) // 128)
    half_turn = pixels // 2
    span = 3 if (degrees // 128) % 3 == 0 else 1
    packed = pl.pallas_call(
        functools.partial(pack_kernel, degrees, span),
        in_specs=[smem, hbm, vmem, vmem, vmem],
        out_specs=[hbm] + [vmem] * 9,
        out_shape=[jax.ShapeDtypeStruct((4, local, width), BF16), jax.ShapeDtypeStruct((8, 128), jnp.int32)]
        + [live_shape, dead_shape] * 3 + [live_shape] * 2,
        scratch_shapes=[
            pltpu.VMEM((4, local, degrees + 128 * span), BF16),
            pltpu.VMEM((4, local, width), BF16),
            pltpu.VMEM((2, 2, 8, degrees), F32),
            pltpu.VMEM((2, 2, 8, degrees), F32),
            pltpu.SemaphoreType.DMA((4,)),
            pltpu.SemaphoreType.DMA((4,)),
        ],
        compiler_params=pltpu.CompilerParams(vmem_limit_bytes=PACK_VMEM),
        name="pack",
    )(orders, legendre, right_side, start_guess, prior_inv.reshape(1, degrees))
    leg, numbers, rhs_live, rhs_dead, x_live, x_dead, prior_live, prior_dead, mask, parity = packed

    scratch = [
        pltpu.VMEM((4, local, width), BF16),
        pltpu.VMEM((3, 2, 8, width), F32),
        pltpu.VMEM((4, 2, 8, degrees), F32),
        pltpu.VMEM((2, 8, width), F32),
        pltpu.VMEM((2, 8, degrees), F32),
        pltpu.VMEM((2, 8, width), F32),
        pltpu.VMEM((2, 8, degrees), F32),
        pltpu.VMEM((cycles, 2, pixels), F32),
        pltpu.VMEM((cycles, 2, pixels), jnp.int32),
        pltpu.VMEM((2, 64, width), BF16),
        pltpu.VMEM((sheets, 128, 128), F32),
        pltpu.VMEM((sheets * 128, 128), F32),
        pltpu.VMEM((sheets, 128, 128), F32),
        pltpu.VMEM((n_order, 8, 128), F32),
        pltpu.VMEM((6, n_order, 8, 128), F32),
        pltpu.VMEM((n_order, 8, 128), jnp.int32),
        pltpu.VMEM((8, 128), F32),
        pltpu.VMEM((128, columns), BF16),
        pltpu.VMEM((8, 8, half_turn), F32),
        pltpu.VMEM((64, columns), F32),
        pltpu.VMEM((8, columns), F32),
        pltpu.VMEM((n_order, 2, 8, 128), F32),
        pltpu.VMEM((n_order, 2, 8, 128), F32),
        pltpu.VMEM((columns, half_turn), BF16),
        pltpu.VMEM((64, half_turn), F32),
        pltpu.VMEM((6, 8, 128), F32),
        pltpu.VMEM((2, n_blk, 8, part + 128), F32),
        pltpu.VMEM((2, 8, 128), F32),
        pltpu.VMEM((2, 8, part), F32),
        pltpu.VMEM((3, n_blk, 8, part), F32),
        pltpu.VMEM((3, n_blk, 8, part + 128), F32),
        pltpu.VMEM((3, 2, 8, degrees), F32),
        pltpu.VMEM((3, 8, 128), F32),
        pltpu.VMEM((2, 8, width), F32),
        pltpu.VMEM((2, 8, degrees), F32),
        pltpu.VMEM((4, 8, 128), F32),
        pltpu.SemaphoreType.DMA((4,)),
        pltpu.SemaphoreType.DMA((7,)),
        pltpu.SemaphoreType.DMA((2,)),
        pltpu.SemaphoreType.DMA((6,)),
        pltpu.SemaphoreType.DMA((6,)),
        pltpu.SemaphoreType.DMA((3, 2)),
        pltpu.SemaphoreType.DMA((3, 2)),
        pltpu.SemaphoreType.DMA((3, 2)),
        pltpu.SemaphoreType.DMA((3, 2)),
    ]
    results = pl.pallas_call(
        functools.partial(main_kernel, n_order, n_blk, degrees, cycles, pixels),
        in_specs=[vmem, hbm, hbm, hbm, vmem, hbm, hbm, hbm, vmem, vmem, hbm, hbm],
        out_specs=[vmem] * 4,
        out_shape=[live_shape, dead_shape, live_shape, dead_shape],
        scratch_shapes=scratch,
        compiler_params=pltpu.CompilerParams(
            collective_id=0, has_side_effects=True, vmem_limit_bytes=VMEM_LIMIT),
        name="steps",
    )(numbers, leg, rhs_live, rhs_dead, x_live, x_dead, prior_live, prior_dead, mask, parity,
      noise_inv.transpose(1, 0, 2), pixel_flags.transpose(1, 0, 2))

    full = jax.ShapeDtypeStruct(right_side.shape, F32)
    return tuple(pl.pallas_call(
        functools.partial(unpack_kernel, degrees),
        in_specs=[smem] + [vmem] * 4,
        out_specs=[vmem] * 2,
        out_shape=[full, full],
        scratch_shapes=[pltpu.VMEM((2, 8, degrees), F32)] * 2,
        compiler_params=pltpu.CompilerParams(vmem_limit_bytes=VMEM_LIMIT),
        name="unpack",
    )(orders, *results))


def solution(mesh):
    in_specs = (
        P(None, None, "order", None),
        P(None, None, "order", None),
        P("order", "blk", None),
        P("order"),
        P(),
        P(None, ("blk", "order"), None),
        P(None, ("blk", "order"), None),
    )
    out_specs = (P(None, None, "order", None), P(None, None, "order", None))
    body = functools.partial(per_device, mesh.shape["order"], mesh.shape["blk"])
    return jax.shard_map(body, mesh=mesh, in_specs=in_specs, out_specs=out_specs, check_vma=False)
```

```python
import functools

import jax
import jax.numpy as jnp
from jax import lax
from jax.experimental import pallas as pl
from jax.experimental.pallas import tpu as pltpu
from jax.sharding import PartitionSpec as P

MESH = pl.DeviceIdType.MESH
F32 = jnp.float32
BF16 = jnp.bfloat16
VMEM_LIMIT = 56 * 1024 * 1024
PACK_VMEM = 56 * 1024 * 1024
NT = (((1,), (1,)), ((), ()))


def iota(shape, dim):
    return lax.broadcasted_iota(jnp.int32, shape, dim)


def tile_lanes(t, shift, less, tiles):
    at = lax.rem(t - shift // 128 - less + 2 * tiles, tiles) * 128
    return pl.ds(pl.multiple_of(at, 128), 128)


def rolled_tiles(load, shift, tiles, lane):
    within = lax.rem(shift, 128)
    before = pltpu.roll(load(tile_lanes(0, shift, 1, tiles)), within, 1)
    for t in range(tiles):
        now = pltpu.roll(load(tile_lanes(t, shift, 0, tiles)), within, 1)
        yield jnp.where(lane >= within, now, before)
        before = now


def pack_kernel(degrees, span, orders, leg_hbm, rhs, guess, prior,
                leg_out, numbers, rhs_live, rhs_dead, x_live, x_dead, prior_live, prior_dead,
                mask, parity, stage, packed, rows_a, rows_b, in_sems, out_sems):
    tiles = degrees // 128
    blocks = tiles // span
    local = packed.shape[1]
    lane16 = iota((16, 128), 1)
    lane8 = iota((8, 128), 1)
    row8 = iota((8, 128), 0)
    upper = row8 < 4

    for pair in range(4):
        own_blocks = orders[2 * pair] // (128 * span)
        for j in range(blocks + 1):
            second = j <= own_blocks
            slot = 2 * pair + jnp.where(second, 1, 0)
            column = jnp.where(second, blocks - 1 - own_blocks + j, j - 1) * (128 * span)
            lanes = pl.ds(pl.multiple_of(column, 128), 128 * span)
            pltpu.make_async_copy(leg_hbm.at[slot, :, lanes],
                                  stage.at[pair, :, pl.ds(j * 128 * span, 128 * span)], in_sems.at[pair]).start()

    tile = jnp.zeros((8, 128), jnp.int32)
    for m in range(8):
        tile = jnp.where(row8 == m, orders[m], tile)
    numbers[...] = tile
    tail = slice(degrees, degrees + 128)
    sources = [(rhs, rhs_live, rhs_dead), (guess, x_live, x_dead)]
    for quad in range(2):
        low, high = orders[4 * quad], orders[4 * quad + 2]
        shifts = jnp.where(upper, low, high)
        number_b = jnp.where(upper, orders[4 * quad + 1], orders[4 * quad + 3])
        for at, (source, live, dead) in enumerate(sources):
            for half in range(2):
                slot = 4 * quad + 2 * half
                for r in range(2):
                    for c in range(2):
                        row = half * 4 + r * 2 + c
                        rows_a[quad, at, row:row + 1, :] = source[r, c, slot:slot + 1, :]
                        rows_b[quad, at, row:row + 1, :] = source[r, c, slot + 1:slot + 2, :]

        def both(load):
            for one, two in zip(rolled_tiles(load, low, tiles, lane8), rolled_tiles(load, high, tiles, lane8)):
                yield jnp.where(upper, one, two)

        for at, (source, live, dead) in enumerate(sources):
            for t, rolled in enumerate(both(lambda lanes: rows_b[quad, at, :, lanes])):
                lanes = slice(t * 128, t * 128 + 128)
                own = lane8 + t * 128 >= shifts
                first = rows_a[quad, at, :, lanes]
                idle = jnp.where(own, rolled, first)
                if t == tiles - 1:
                    idle = jnp.where(lane8 == 127, 0.0, idle)
                live[quad, :, lanes] = jnp.where(own, first, rolled)
                dead[quad, :, lanes] = idle
            live[quad, :, tail] = jnp.where(lane8 == 0, pltpu.roll(rolled, 1, 1), 0.0)
        for t, rolled in enumerate(both(lambda lanes: jnp.broadcast_to(prior[:, lanes], (8, 128)))):
            lanes = slice(t * 128, t * 128 + 128)
            place = lane8 + t * 128
            own = place >= shifts
            first = jnp.broadcast_to(prior[:, lanes], (8, 128))
            prior_live[quad, :, lanes] = jnp.where(own, first, rolled)
            prior_dead[quad, :, lanes] = jnp.where(own, rolled, first)
            total = jnp.where(own, place + shifts, place - shifts + degrees + number_b)
            parity[quad, :, lanes] = (1 - 2 * (total & 1)).astype(F32)
            mask[quad, :, lanes] = own.astype(F32)
        prior_live[quad, :, tail] = jnp.where(lane8 == 0, pltpu.roll(rolled, 1, 1), 0.0)
        parity[quad, :, tail] = jnp.ones((8, 128), F32)
        mask[quad, :, tail] = jnp.zeros((8, 128), F32)

    for pair in range(4):
        shift = orders[2 * pair]
        within = lax.rem(shift, 128)
        back = span - 1 - lax.rem(shift // 128, span)
        pltpu.make_async_copy(stage.at[pair], stage.at[pair], in_sems.at[pair]).wait()

        def rows_of(step, carry):
            rows = pl.ds(pl.multiple_of(step * 16, 16), 16)

            def moved(t):
                lanes = pl.ds(pl.multiple_of((t + back) * 128, 128), 128)
                return pltpu.roll(stage[pair, rows, lanes], within, 1)

            before = moved(0)
            extra = jnp.where(lane16 == 0, pltpu.roll(before, 1, 1), jnp.zeros_like(before))
            packed[pair, rows, degrees:degrees + 128] = extra
            for t in range(tiles):
                now = moved(t + 1)
                rolled = jnp.where(lane16 >= within, now, before)
                first = stage[pair, rows, (t + span) * 128:(t + span) * 128 + 128]
                packed[pair, rows, t * 128:t * 128 + 128] = jnp.where(lane16 + t * 128 >= shift, first, rolled)
                before = now
            return carry

        lax.fori_loop(0, local // 16, rows_of, 0, unroll=4 if local % 64 == 0 else 1)
        pltpu.make_async_copy(packed.at[pair], leg_out.at[pair], out_sems.at[pair]).start()
    for pair in range(4):
        pltpu.make_async_copy(packed.at[pair], leg_out.at[pair], out_sems.at[pair]).wait()


def unpack_kernel(degrees, orders, x_live, x_dead, r_live, r_dead, x_out, r_out, rows_a, rows_b):
    tiles = degrees // 128
    lane8 = iota((8, 128), 1)
    upper = iota((8, 128), 0) < 4
    for quad in range(2):
        low, high = orders[4 * quad], orders[4 * quad + 2]
        shifts = jnp.where(upper, low, high)
        back_low, back_high = lax.rem(degrees - low, degrees), lax.rem(degrees - high, degrees)
        for at, (live, dead, out) in enumerate(((x_live, x_dead, x_out), (r_live, r_dead, r_out))):
            for t in range(tiles):
                lanes = slice(t * 128, t * 128 + 128)
                own = lane8 + t * 128 >= shifts
                alive, idle = live[quad, :, lanes], dead[quad, :, lanes]
                rows_a[at, :, lanes] = jnp.where(own, alive, idle)
                second = jnp.where(own, idle, alive)
                if t == tiles - 1:
                    extra = live[quad, :, degrees:degrees + 128]
                    second = jnp.where(lane8 == 127, pltpu.roll(extra, 127, 1), second)
                rows_b[at, :, lanes] = second
            load = lambda lanes: rows_b[at, :, lanes]
            back = zip(rolled_tiles(load, back_low, tiles, lane8), rolled_tiles(load, back_high, tiles, lane8))
            kept = [jnp.where(upper, one, two) for one, two in back]
            for t, value in enumerate(kept):
                rows_b[at, :, t * 128:t * 128 + 128] = value
            for half in range(2):
                slot = 4 * quad + 2 * half
                for r in range(2):
                    for c in range(2):
                        row = half * 4 + r * 2 + c
                        out[r, c, slot:slot + 1, :] = rows_a[at, row:row + 1, :]
                        out[r, c, slot + 1:slot + 2, :] = rows_b[at, row:row + 1, :]


def split_bf16(values):
    high = values.astype(BF16)
    return high, (values - high.astype(F32)).astype(BF16)


def main_kernel(n_order, n_blk, degrees, cycles, pixels,
                own_orders, leg_hbm, rhs_live_hbm, rhs_dead_hbm, x_live_hbm, x_dead_hbm, prior_live_hbm,
                prior_dead_hbm, mask_hbm, parity_hbm, noise_hbm, flags_hbm,
                x_out_live, x_out_dead, r_out_live, r_out_dead,
                leg, leg_turned, live, dead, rhs_live, rhs_dead, prior_live, prior_dead, mask, parity, noise, flags,
                lhs, modes, turned, back, send, recv, order_recv, scalar,
                flhs, weight, anal, sign, current, turn, table, table_turned, sky_kept, pixel_sums,
                partial, extras, shard, rs_recv0, rs_recv1, summed, extra_sum,
                r1_live, r1_dead, steps,
                leg_sems, load_sems, order_sems, a2a_send, a2a_recv, rs_send, rs_arrive, ag_send, ag_arrive):
    me = lax.axis_index("order")
    mine = lax.axis_index("blk")
    tiles = degrees // 128
    half_turn = pixels // 2
    columns = 16 * n_order
    groups = columns // 128
    local = cycles * n_order
    part = degrees // n_blk
    sheets = modes.shape[0]

    def leg_copy(pair):
        return pltpu.make_async_copy(leg_hbm.at[pair], leg.at[pair], leg_sems.at[pair])

    def load_copy(at):
        source, target = ((x_dead_hbm, dead.at[0]), (prior_live_hbm, prior_live), (prior_dead_hbm, prior_dead),
                          (noise_hbm, noise), (flags_hbm, flags), (rhs_live_hbm, rhs_live),
                          (rhs_dead_hbm, rhs_dead), (x_live_hbm, live.at[0]), (mask_hbm, mask),
                          (parity_hbm, parity))[at]
        return pltpu.make_async_copy(source, target, load_sems.at[at])

    side_x = 2
    side_y = n_order // 4
    if n_order == 32:
        side_x, side_y = 4, 4
    offsets = [(a, b, c) for a in range(side_y) for b in range(side_x) for c in range(2) if a or b or c]
    offsets.sort(key=lambda o: -(2 * min(o[0], side_y - o[0]) + 2 * min(o[1], side_x - o[1]) + o[2]))
    my_y, my_x, my_c = me // (2 * side_x), (me // 2) % side_x, me % 2
    peers = [lax.rem(my_y + a, side_y) * (2 * side_x) + lax.rem(my_x + b, side_x) * 2 + lax.rem(my_c + c, 2)
             for a, b, c in offsets]
    steps_z = sorted(range(1, n_blk), key=lambda i: -min(i, n_blk - i))
    partners = [lax.rem(mine + i, n_blk) for i in steps_z]

    barrier = pltpu.get_barrier_semaphore()
    for to in peers:
        pl.semaphore_signal(barrier, inc=1, device_id=(to, mine), device_id_type=MESH)
    for to in partners:
        pl.semaphore_signal(barrier, inc=1, device_id=(me, to), device_id_type=MESH)
    for at in (7, 8, 9):
        load_copy(at).start()
    for pair in range(4):
        leg_copy(pair).start()
    for at in range(7):
        load_copy(at).start()

    def wait_bytes(ref, sem):
        pltpu.make_async_copy(ref, ref, sem).wait()

    row8 = iota((8, 128), 0)
    lane8 = iota((8, 128), 1)
    modes[...] = jnp.zeros_like(modes)
    turned[...] = jnp.zeros_like(turned)
    scalar[...] = jnp.zeros_like(scalar)
    pixel_sums[...] = jnp.zeros_like(pixel_sums)
    for at in (7, 8, 9):
        load_copy(at).wait()

    pl.semaphore_wait(barrier, n_order - 1 + n_blk - 1)

    for to in peers:
        pltpu.make_async_remote_copy(
            src_ref=own_orders, dst_ref=order_recv.at[me],
            send_sem=order_sems.at[0], recv_sem=order_sems.at[1],
            device_id=(to, mine), device_id_type=MESH).start()
    order_recv[me] = own_orders[...]

    def exchange_start(step):
        for to in peers:
            pltpu.make_async_remote_copy(
                src_ref=send.at[to], dst_ref=recv.at[step, me],
                send_sem=a2a_send.at[step], recv_sem=a2a_recv.at[step],
                device_id=(to, mine), device_id_type=MESH).start()
        recv[step, me] = send[me]

    def exchange_wait(step):
        wait_bytes(recv.at[step, pl.ds(0, n_order - 1)], a2a_recv.at[step])
        wait_bytes(send.at[pl.ds(0, n_order - 1)], a2a_send.at[step])

    def build_weight():
        weight[...] = jnp.zeros_like(weight)
        for j in range(cycles):
            value = noise[j] * flags[j].astype(F32)
            for h in range(2):
                for image in range(2):
                    row = value[h:h + 1, image * half_turn:(image + 1) * half_turn]
                    for r in range(2):
                        weight[image * 4 + h * 2 + r, j:j + 1, :] = row

    def build_table():
        wait_bytes(order_recv.at[pl.ds(0, n_order - 1)], order_sems.at[1])
        wait_bytes(order_recv.at[pl.ds(0, n_order - 1)], order_sems.at[0])
        number = order_recv[...]
        lane = iota((n_order, 8, 128), 2)
        scale = jnp.where(number == 0, 1.0, 2.0) * (pixels ** -0.5)

        def angle(product):
            value = product.astype(F32)
            value = value - pixels * jnp.floor(value * (1.0 / pixels))
            return value * (2.0 * jnp.pi / pixels)

        base = angle(number * lane)
        current[:, 0] = scale * jnp.cos(base)
        current[:, 1] = -scale * jnp.sin(base)
        step = angle(number * 128)
        turn[:, 0] = jnp.cos(step)
        turn[:, 1] = jnp.sin(step)
        odd = (1 - 2 * (number & 1)).astype(F32)
        sign_rows = jnp.concatenate([odd, odd], axis=1).reshape(columns, 128)
        sign[...] = sign_rows.T[0:8]

        def block(q, carry):
            lanes = pl.ds(pl.multiple_of(q * 128, 128), 128)

            def some(piece, inner):
                for k in range(8):
                    s = piece * 8 + k
                    cosine, sine = current[s, 0], current[s, 1]
                    rows = pl.ds(pl.multiple_of(s * 16, 16), 16)
                    table[rows, lanes] = jnp.concatenate([cosine, sine], axis=0).astype(BF16)
                    turn_c, turn_s = turn[s, 0], turn[s, 1]
                    current[s, 0] = cosine * turn_c + sine * turn_s
                    current[s, 1] = sine * turn_c - cosine * turn_s
                return inner

            return lax.fori_loop(0, n_order // 8, some, carry)

        lax.fori_loop(0, half_turn // 128, block, 0)

    group8 = lane8 // 16
    item8 = lane8 // 8
    first_row8 = (iota((8, 1), 0) % 4) < 2

    def by_realization(total):
        zero = jnp.sum(jnp.where(first_row8, total, 0.0), axis=0, keepdims=True)
        one = jnp.sum(jnp.where(first_row8, 0.0, total), axis=0, keepdims=True)
        return [zero, one]

    def lane_sum(value):
        return jnp.sum(value, axis=1, keepdims=True)

    def put_scalars(values):
        tile = jnp.zeros((8, 128), F32)
        for at, value in enumerate(values):
            tile = jnp.where(item8 == at, value, tile)
        return tile

    def sum_tiles(load, count):
        values = [load(s) for s in range(count)]
        while len(values) > 1:
            values = [a + b for a, b in zip(values[::2], values[1::2])]
        return values[0]

    def scalar_at(total, row, at):
        return total[row:row + 1, 8 * at:8 * at + 1]

    def rows_from(pair):
        return jnp.where(first_row8, pair[0], pair[1])

    def pair_at(total, row, at):
        return [scalar_at(total, row, at), scalar_at(total, row, at + 1)]

    lane_step = 128 * max(n for n in (5, 3, 1) if (tiles + 1) % n == 0)
    width = degrees + 128

    def application(p, carry):
        for quad in range(2):
            @pl.when(p > 0)
            def _():
                wait_bytes(rs_recv0.at[p - 1, pl.ds(0, n_blk - 1)], ag_arrive.at[p - 1, quad])
                main = pl.ds(0, degrees)
                image = prior_live[quad, :, main] * live[p - 1, quad, :, main] + summed[p - 1, quad]
                live[p, quad, :, main] = jnp.where(p == 1, rhs_live[quad, :, main] - image, image)
                tail = pl.ds(degrees, 128)
                image = prior_live[quad, :, tail] * live[p - 1, quad, :, tail] + extra_sum[quad]
                live[p, quad, :, tail] = jnp.where(p == 1, rhs_live[quad, :, tail] - image, image)

            def build(t, inner_carry):
                at = pl.ds(t * lane_step, lane_step)
                value = live[p, quad, :, at]
                first = mask[quad, :, at]
                second = 1.0 - first
                flip = parity[quad, :, at]
                high = value.astype(BF16).astype(F32)
                rest = value - high
                pieces = []
                for piece in (high, rest):
                    for keep in (first, second):
                        kept = piece * keep
                        pieces.append(kept)
                        pieces.append(kept * flip)
                lhs[quad, :, at] = jnp.concatenate(pieces, axis=0).astype(BF16)
                return inner_carry

            for t in range(width // lane_step):
                build(t, 0)
            for half in range(2):
                pair = 2 * quad + half


                def keep(out, pair=pair, at=4 * half):
                    out = out[0:32] + out[32:64]
                    for slot in range(2):
                        rows = jnp.concatenate([out[16 * slot + at:16 * slot + at + 4],
                                                out[16 * slot + 8 + at:16 * slot + 8 + at + 4]], axis=0)
                        if sheets * 128 > local:
                            rows = jnp.concatenate([rows, jnp.zeros((8, sheets * 128 - local), F32)], axis=1)
                        for sheet in range(sheets):
                            modes[sheet, pl.ds(2 * pair + slot, 8, stride=8), :] = (
                                rows[:, 128 * sheet:128 * sheet + 128])

                @pl.when(p == 0)
                def _():
                    leg_copy(pair).wait()
                    keep(lax.dot_general(lhs[quad], leg[pair], NT, preferred_element_type=F32))

                @pl.when(p > 0)
                def _():
                    keep(jnp.dot(lhs[quad], leg_turned[pair], preferred_element_type=F32))

        @pl.when(p > 0)
        def _():
            for quad in range(2):
                wait_bytes(rs_recv0.at[p - 1, pl.ds(0, n_blk - 1)], ag_send.at[p - 1, quad])

        for sheet in range(sheets):
            turned[128 * sheet:128 * sheet + 128, :] = modes[sheet].T

        @pl.when(p == 2)
        def _():
            norm = cross = jnp.zeros((8, 1), F32)
            for quad in range(2):
                for held in (live, dead):
                    norm = norm + lane_sum(held[1, quad] * held[1, quad])
                    cross = cross + lane_sum(held[1, quad] * held[2, quad])
            scalar[...] = put_scalars(by_realization(norm) + by_realization(cross))

        for d in range(n_order):
            send[d] = jnp.where(row8 < cycles, turned[cycles * d:cycles * d + 8, :], scalar[...])
        exchange_start(2 * p)

        @pl.when(p == 0)
        def _():
            build_table()
            load_copy(3).wait()
            load_copy(4).wait()
            build_weight()

        exchange_wait(2 * p)

        @pl.when(p == 2)
        def _():
            total = sum_tiles(lambda s: recv[2 * p, s], n_order)
            norm, cross = pair_at(total, 7, 0), pair_at(total, 7, 2)
            ratio = [norm[0] / cross[0], norm[1] / cross[1]]
            step = rows_from(ratio)
            steps[0] = jnp.broadcast_to(rows_from(norm), (8, 128))
            steps[1] = jnp.broadcast_to(step, (8, 128))
            steps[2] = jnp.broadcast_to(ratio[0], (8, 128))
            steps[3] = jnp.broadcast_to(ratio[1], (8, 128))
            sums = [jnp.zeros((8, 1), F32)] * 4
            for quad in range(2):
                for r1, held, inv in ((r1_live, live, prior_live), (r1_dead, dead, prior_dead)):
                    before = held[1, quad]
                    after = before - step * held[2, quad]
                    r1[quad] = after
                    scaled = inv[quad] * after
                    sums = [total + lane_sum(value) for total, value in zip(
                        sums, (after * after, scaled * after, scaled * before, inv[quad] * before * before))]
            scalar[...] = put_scalars([value for total in sums for value in by_realization(total)])

        def shuffle(g, inner_carry):
            lanes = pl.ds(g * 128, 128)
            flip = sign[:, lanes]
            held = [recv[2 * p, g * 8 + i] for i in range(8)]
            straight = []
            for hr in range(4):
                acc = held[0] if hr == 0 else pltpu.roll(held[0], (128 - 16 * hr) % 128, 1)
                for i in range(1, 8):
                    by = (16 * i - 16 * hr) % 128
                    moved = held[i] if by == 0 else pltpu.roll(held[i], by, 1)
                    acc = jnp.where(group8 == i, moved, acc)
                straight.append(acc)
            flipped = [acc * flip for acc in straight]
            rows = jnp.concatenate(straight + flipped, axis=0)
            high, rest = split_bf16(rows)
            flhs[0:64, lanes] = high
            flhs[64:128, lanes] = rest
            return inner_carry

        for g in range(groups):
            shuffle(g, 0)

        anal[...] = jnp.zeros_like(anal)
        chunk = min(1536, half_turn)

        def fourier(t, inner_carry):
            lanes = pl.ds(pl.multiple_of(t * chunk, 128), chunk)
            block = table[:, lanes]
            sky = jnp.dot(flhs[...], block, preferred_element_type=F32)
            sky = sky[0:64] + sky[64:128]
            scaled = sky * weight[:, :, lanes].reshape(64, chunk)
            high, rest = split_bf16(scaled)
            both = jnp.concatenate([high, rest], axis=0)

            @pl.when(p == 0)
            def _():
                out = lax.dot_general(both, block, NT, preferred_element_type=F32)
                anal[...] += out[0:64] + out[64:128]

            @pl.when(p > 0)
            def _():
                out = jnp.dot(both, table_turned[lanes, :], preferred_element_type=F32)
                anal[...] += out[0:64] + out[64:128]

            @pl.when(p == 1)
            def _():
                sky_kept[:, lanes] = sky

            @pl.when(p == 2)
            def _():
                for hr in range(8):
                    rows = slice(8 * hr, 8 * hr + 8)
                    before = sky_kept[rows, lanes]
                    after = before - steps[2 + hr % 2][:, 0:1] * sky[rows]
                    weighed = weight[hr, :, lanes]
                    heavy = weighed * after
                    for at, value in enumerate((heavy * after, heavy * before, weighed * before * before)):
                        total = pixel_sums[2 * at + hr % 2]
                        for k in range(chunk // 128):
                            total = total + value[:, 128 * k:128 * k + 128]
                        pixel_sums[2 * at + hr % 2] = total

            return inner_carry

        lax.fori_loop(0, half_turn // chunk, fourier, 0)

        @pl.when(p == 2)
        def _():
            tile = scalar[...]
            for at in range(6):
                value = jnp.sum(lane_sum(pixel_sums[at]), axis=0, keepdims=True)
                tile = jnp.where(item8 == 8 + at, value, tile)
            scalar[...] = tile

        def shuffle_back(g, inner_carry):
            lanes = pl.ds(g * 128, 128)
            flip = sign[:, lanes]
            rows = [anal[8 * hr:8 * hr + 8, lanes] + flip * anal[32 + 8 * hr:40 + 8 * hr, lanes] for hr in range(4)]
            base = scalar[...]
            for i in range(8):
                acc = jnp.zeros((8, 128), F32)
                for hr in range(4):
                    by = (16 * hr - 16 * i) % 128
                    moved = rows[hr] if by == 0 else pltpu.roll(rows[hr], by, 1)
                    acc = jnp.where(group8 == hr, moved, acc)
                send[g * 8 + i] = jnp.where(row8 < cycles, acc, base)
            return inner_carry

        for g in range(groups):
            shuffle_back(g, 0)
        exchange_start(2 * p + 1)

        @pl.when(p == 0)
        def _():
            for at in (0, 1, 2, 5, 6):
                load_copy(at).wait()

            def turn_leg(pair, inner_carry):
                for t in range(width // lane_step):
                    at = slice(t * lane_step, t * lane_step + lane_step)
                    leg_turned[pair, at, :] = leg[pair, :, at].T
                return inner_carry

            lax.fori_loop(0, 4, turn_leg, 0)

            def turn_table(t, inner_carry):
                at = pl.ds(pl.multiple_of(t * 256, 256), 256)
                table_turned[at, :] = table[:, at].T
                return inner_carry

            lax.fori_loop(0, half_turn // 256, turn_table, 0)

        for quad in range(2):
            image = prior_dead[quad] * dead[p, quad]
            dead[p + 1, quad] = jnp.where(p == 0, rhs_dead[quad] - image, image)
        exchange_wait(2 * p + 1)

        for d in range(n_order):
            turned[cycles * d:cycles * d + cycles, :] = recv[2 * p + 1, d, 0:cycles, :]
        for sheet in range(sheets):
            back[sheet] = turned[128 * sheet:128 * sheet + 128, :].T

        for quad in range(2):
            for half in range(2):
                pair = 2 * quad + half
                rows = jnp.concatenate([
                    jnp.concatenate([back[sheet, pl.ds(2 * pair + slot, 8, stride=8), :] for sheet in range(sheets)],
                                    axis=1)
                    for slot in range(2)], axis=0)
                high, rest = split_bf16(rows[:, 0:local])
                both = jnp.concatenate([high, rest], axis=0)
                mine_rows = slice(4 * half, 4 * half + 4)
                one_row = slice(4 * half, 4 * half + 1)

                def analyse(t, inner_carry):
                    at = pl.ds(t * 2 * part, 2 * part)
                    out = jnp.dot(both, leg[pair, :, at], preferred_element_type=F32)
                    out = out[0:16] + out[16:32]
                    kept = jnp.where(mask[quad, one_row, at] > 0.5, out[0:8], out[8:16])
                    value = kept[0:4] + parity[quad, one_row, at] * kept[4:8]
                    partial[quad, 2 * t, mine_rows, 0:part] = value[:, 0:part]
                    partial[quad, 2 * t + 1, mine_rows, 0:part] = value[:, part:2 * part]
                    return inner_carry

                for t in range(n_blk // 2):
                    analyse(t, 0)
                out = jnp.dot(both, leg[pair, :, degrees:degrees + 128], preferred_element_type=F32)
                out = out[0:16] + out[16:32]
                extras[quad, mine_rows, :] = out[8:12] + out[12:16]
            if quad == 1:
                total = sum_tiles(lambda s: recv[2 * p + 1, s], n_order)
                tile = jnp.where(lane8 == 0, extras[0], 0.0)
                tile = jnp.where(lane8 == 1, pltpu.roll(extras[1], 1, 1), tile)
                scalar[...] = total
                tile = jnp.where((lane8 >= 64) & (row8 == 7), total, tile)
                for b in range(n_blk):
                    partial[1, b, :, part:part + 128] = tile
            for to in partners:
                source = partial.at[0, to, :, pl.ds(0, part)] if quad == 0 else partial.at[1, to]
                target = rs_recv0 if quad == 0 else rs_recv1
                pltpu.make_async_remote_copy(
                    src_ref=source, dst_ref=target.at[p, mine],
                    send_sem=rs_send.at[p, quad], recv_sem=rs_arrive.at[p, quad],
                    device_id=(me, to), device_id_type=MESH).start()

        my_lanes = pl.ds(pl.multiple_of(mine * part, 128), part)
        for quad in range(2):
            arrived = rs_recv0 if quad == 0 else rs_recv1
            arrived[p, mine] = partial[quad, mine, :, 0:arrived.shape[3]]
            wait_bytes(arrived.at[p, pl.ds(0, n_blk - 1)], rs_arrive.at[p, quad])
            total = sum_tiles(lambda b: arrived[p, b], n_blk)
            shard[quad] = total[:, 0:part]
            for to in partners:
                pltpu.make_async_remote_copy(
                    src_ref=shard.at[quad], dst_ref=summed.at[p, quad, :, my_lanes],
                    send_sem=ag_send.at[p, quad], recv_sem=ag_arrive.at[p, quad],
                    device_id=(me, to), device_id_type=MESH).start()
            summed[p, quad, :, my_lanes] = total[:, 0:part]
            wait_bytes(arrived.at[p, pl.ds(0, n_blk - 1)], rs_send.at[p, quad])
        tile = total[:, part:part + 128]
        extra_sum[0] = jnp.where(lane8 == 0, tile, 0.0)
        extra_sum[1] = jnp.where(lane8 == 0, pltpu.roll(tile, 127, 1), 0.0)
        extra_sum[2] = tile
        return carry

    lax.fori_loop(0, 3, application, 0)

    within_order, over_all = scalar[...], extra_sum[2]
    norm = [steps[0, 0:1, 0:1], steps[0, 2:3, 0:1]]
    ratios, seconds = [], []
    for r in range(2):
        after = scalar_at(within_order, 7, r)
        ratio = after / norm[r]
        curve = (scalar_at(within_order, 7, 2 + r) + scalar_at(over_all, 7, 8 + r)
                 + 2.0 * ratio * (scalar_at(within_order, 7, 4 + r) + scalar_at(over_all, 7, 10 + r))
                 + ratio * ratio * (scalar_at(within_order, 7, 6 + r) + scalar_at(over_all, 7, 12 + r)))
        ratios.append(ratio)
        seconds.append(after / curve)
    ratio, second = rows_from(ratios), rows_from(seconds)
    step = steps[1, :, 0:1]

    def finish(quad, lanes, held, r1, last, x_out, r_out):
        before, middle = held[1, quad, :, lanes], held[2, quad, :, lanes]
        after = r1[quad, :, lanes]
        direction = after + ratio * before
        image = (1.0 + ratio) * middle - step * last
        x_out[quad, :, lanes] = held[0, quad, :, lanes] + step * before + second * direction
        r_out[quad, :, lanes] = after - second * image

    main, tail = pl.ds(0, degrees), pl.ds(degrees, 128)
    for quad in range(2):
        finish(quad, main, dead, r1_dead, dead[3, quad], x_out_dead, r_out_dead)
        last = prior_live[quad, :, tail] * live[2, quad, :, tail] + extra_sum[quad]
        finish(quad, tail, live, r1_live, last, x_out_live, r_out_live)
    for quad in range(2):
        wait_bytes(rs_recv0.at[2, pl.ds(0, n_blk - 1)], ag_arrive.at[2, quad])
        last = prior_live[quad, :, main] * live[2, quad, :, main] + summed[2, quad]
        finish(quad, main, live, r1_live, last, x_out_live, r_out_live)
    for quad in range(2):
        wait_bytes(rs_recv0.at[2, pl.ds(0, n_blk - 1)], ag_send.at[2, quad])


def per_device(n_order, n_blk, right_side, start_guess, legendre, orders, prior_inv, noise_inv, pixel_flags):
    slots, local, degrees = legendre.shape
    cycles, pixels = noise_inv.shape[1], noise_inv.shape[2]
    width = degrees + 128
    part = degrees // n_blk
    smem = pl.BlockSpec(memory_space=pltpu.SMEM)
    vmem = pl.BlockSpec(memory_space=pltpu.VMEM)
    hbm = pl.BlockSpec(memory_space=pl.ANY)
    live_shape = jax.ShapeDtypeStruct((2, 8, width), F32)
    dead_shape = jax.ShapeDtypeStruct((2, 8, degrees), F32)
    columns = 16 * n_order
    sheets = -(-(local + 8) // 128)
    half_turn = pixels // 2
    span = 3 if (degrees // 128) % 3 == 0 else 1
    packed = pl.pallas_call(
        functools.partial(pack_kernel, degrees, span),
        in_specs=[smem, hbm, vmem, vmem, vmem],
        out_specs=[hbm] + [vmem] * 9,
        out_shape=[jax.ShapeDtypeStruct((4, local, width), BF16), jax.ShapeDtypeStruct((8, 128), jnp.int32)]
        + [live_shape, dead_shape] * 3 + [live_shape] * 2,
        scratch_shapes=[
            pltpu.VMEM((4, local, degrees + 128 * span), BF16),
            pltpu.VMEM((4, local, width), BF16),
            pltpu.VMEM((2, 2, 8, degrees), F32),
            pltpu.VMEM((2, 2, 8, degrees), F32),
            pltpu.SemaphoreType.DMA((4,)),
            pltpu.SemaphoreType.DMA((4,)),
        ],
        compiler_params=pltpu.CompilerParams(vmem_limit_bytes=PACK_VMEM),
        name="pack",
    )(orders, legendre, right_side, start_guess, prior_inv.reshape(1, degrees))
    leg, numbers, rhs_live, rhs_dead, x_live, x_dead, prior_live, prior_dead, mask, parity = packed

    scratch = [
        pltpu.VMEM((4, local, width), BF16),
        pltpu.VMEM((4, width, local), BF16),
        pltpu.VMEM((3, 2, 8, width), F32),
        pltpu.VMEM((4, 2, 8, degrees), F32),
        pltpu.VMEM((2, 8, width), F32),
        pltpu.VMEM((2, 8, degrees), F32),
        pltpu.VMEM((2, 8, width), F32),
        pltpu.VMEM((2, 8, degrees), F32),
        pltpu.VMEM((2, 8, width), F32),
        pltpu.VMEM((2, 8, width), F32),
        pltpu.VMEM((cycles, 2, pixels), F32),
        pltpu.VMEM((cycles, 2, pixels), jnp.int32),
        pltpu.VMEM((2, 64, width), BF16),
        pltpu.VMEM((sheets, 128, 128), F32),
        pltpu.VMEM((sheets * 128, 128), F32),
        pltpu.VMEM((sheets, 128, 128), F32),
        pltpu.VMEM((n_order, 8, 128), F32),
        pltpu.VMEM((6, n_order, 8, 128), F32),
        pltpu.VMEM((n_order, 8, 128), jnp.int32),
        pltpu.VMEM((8, 128), F32),
        pltpu.VMEM((128, columns), BF16),
        pltpu.VMEM((8, 8, half_turn), F32),
        pltpu.VMEM((64, columns), F32),
        pltpu.VMEM((8, columns), F32),
        pltpu.VMEM((n_order, 2, 8, 128), F32),
        pltpu.VMEM((n_order, 2, 8, 128), F32),
        pltpu.VMEM((columns, half_turn), BF16),
        pltpu.VMEM((half_turn, columns), BF16),
        pltpu.VMEM((64, half_turn), F32),
        pltpu.VMEM((6, 8, 128), F32),
        pltpu.VMEM((2, n_blk, 8, part + 128), F32),
        pltpu.VMEM((2, 8, 128), F32),
        pltpu.VMEM((2, 8, part), F32),
        pltpu.VMEM((3, n_blk, 8, part), F32),
        pltpu.VMEM((3, n_blk, 8, part + 128), F32),
        pltpu.VMEM((3, 2, 8, degrees), F32),
        pltpu.VMEM((3, 8, 128), F32),
        pltpu.VMEM((2, 8, width), F32),
        pltpu.VMEM((2, 8, degrees), F32),
        pltpu.VMEM((4, 8, 128), F32),
        pltpu.SemaphoreType.DMA((4,)),
        pltpu.SemaphoreType.DMA((10,)),
        pltpu.SemaphoreType.DMA((2,)),
        pltpu.SemaphoreType.DMA((6,)),
        pltpu.SemaphoreType.DMA((6,)),
        pltpu.SemaphoreType.DMA((3, 2)),
        pltpu.SemaphoreType.DMA((3, 2)),
        pltpu.SemaphoreType.DMA((3, 2)),
        pltpu.SemaphoreType.DMA((3, 2)),
    ]
    results = pl.pallas_call(
        functools.partial(main_kernel, n_order, n_blk, degrees, cycles, pixels),
        in_specs=[vmem] + [hbm] * 11,
        out_specs=[vmem] * 4,
        out_shape=[live_shape, dead_shape, live_shape, dead_shape],
        scratch_shapes=scratch,
        compiler_params=pltpu.CompilerParams(
            collective_id=0, has_side_effects=True, vmem_limit_bytes=VMEM_LIMIT),
        name="steps",
    )(numbers, leg, rhs_live, rhs_dead, x_live, x_dead, prior_live, prior_dead, mask, parity,
      noise_inv.transpose(1, 0, 2), pixel_flags.transpose(1, 0, 2))

    full = jax.ShapeDtypeStruct(right_side.shape, F32)
    return tuple(pl.pallas_call(
        functools.partial(unpack_kernel, degrees),
        in_specs=[smem] + [vmem] * 4,
        out_specs=[vmem] * 2,
        out_shape=[full, full],
        scratch_shapes=[pltpu.VMEM((2, 8, degrees), F32)] * 2,
        compiler_params=pltpu.CompilerParams(vmem_limit_bytes=VMEM_LIMIT),
        name="unpack",
    )(orders, *results))


def solution(mesh):
    in_specs = (
        P(None, None, "order", None),
        P(None, None, "order", None),
        P("order", "blk", None),
        P("order"),
        P(),
        P(None, ("blk", "order"), None),
        P(None, ("blk", "order"), None),
    )
    out_specs = (P(None, None, "order", None), P(None, None, "order", None))
    body = functools.partial(per_device, mesh.shape["order"], mesh.shape["blk"])
    return jax.shard_map(body, mesh=mesh, in_specs=in_specs, out_specs=out_specs, check_vma=False)
```

```python
import functools

import jax
import jax.numpy as jnp
from jax import lax
from jax.experimental import pallas as pl
from jax.experimental.pallas import tpu as pltpu
from jax.sharding import PartitionSpec as P

MESH = pl.DeviceIdType.MESH
F32 = jnp.float32
BF16 = jnp.bfloat16
VMEM_LIMIT = 56 * 1024 * 1024
NT = (((1,), (1,)), ((), ()))


def iota(shape, dim):
    return lax.broadcasted_iota(jnp.int32, shape, dim)


def tile_lanes(t, shift, less, tiles):
    at = lax.rem(t - shift // 128 - less + 2 * tiles, tiles) * 128
    return pl.ds(pl.multiple_of(at, 128), 128)


def rolled_tiles(load, shift, tiles, lane):
    within = lax.rem(shift, 128)
    before = pltpu.roll(load(tile_lanes(0, shift, 1, tiles)), within, 1)
    for t in range(tiles):
        now = pltpu.roll(load(tile_lanes(t, shift, 0, tiles)), within, 1)
        yield jnp.where(lane >= within, now, before)
        before = now


def rotate_tiles(tiles, whole):
    count = len(tiles)
    for bit in range((count - 1).bit_length()):
        moved = (whole & (1 << bit)) != 0
        tiles = [jnp.where(moved, tiles[(t - (1 << bit)) % count], tiles[t]) for t in range(count)]
    return tiles


def lane_shift(value, within):
    return pltpu.roll(value, within, 1)


def unpack_kernel(degrees, orders, x_live, x_dead, r_live, r_dead, x_out, r_out, rows_a, rows_b):
    tiles = degrees // 128
    lane8 = iota((8, 128), 1)
    upper = iota((8, 128), 0) < 4
    for quad in range(2):
        low, high = orders[4 * quad], orders[4 * quad + 2]
        shifts = jnp.where(upper, low, high)
        back_low, back_high = lax.rem(degrees - low, degrees), lax.rem(degrees - high, degrees)
        for at, (live, dead, out) in enumerate(((x_live, x_dead, x_out), (r_live, r_dead, r_out))):
            for t in range(tiles):
                lanes = slice(t * 128, t * 128 + 128)
                own = lane8 + t * 128 >= shifts
                alive, idle = live[quad, :, lanes], dead[quad, :, lanes]
                rows_a[at, :, lanes] = jnp.where(own, alive, idle)
                second = jnp.where(own, idle, alive)
                if t == tiles - 1:
                    extra = live[quad, :, degrees:degrees + 128]
                    second = jnp.where(lane8 == 127, pltpu.roll(extra, 127, 1), second)
                rows_b[at, :, lanes] = second
            load = lambda lanes: rows_b[at, :, lanes]
            back = zip(rolled_tiles(load, back_low, tiles, lane8), rolled_tiles(load, back_high, tiles, lane8))
            kept = [jnp.where(upper, one, two) for one, two in back]
            for t, value in enumerate(kept):
                rows_b[at, :, t * 128:t * 128 + 128] = value
            for half in range(2):
                slot = 4 * quad + 2 * half
                for r in range(2):
                    for c in range(2):
                        row = half * 4 + r * 2 + c
                        out[r, c, slot:slot + 1, :] = rows_a[at, row:row + 1, :]
                        out[r, c, slot + 1:slot + 2, :] = rows_b[at, row:row + 1, :]


def split_bf16(values):
    high = values.astype(BF16)
    return high, (values - high.astype(F32)).astype(BF16)


def main_kernel(n_order, n_blk, degrees, cycles, pixels,
                orders, leg_hbm, guess_hbm, rhs_hbm, prior, noise_hbm, flags_hbm,
                x_out_live, x_out_dead, r_out_live, r_out_dead,
                raw0, raw1, raw2, raw3, own_orders, guess, rhs, rows_a, rows_b,
                leg, leg_turned, live, dead, rhs_live, rhs_dead, prior_live, prior_dead, mask, parity, noise, flags,
                lhs, modes, turned, back, send, recv, order_recv, scalar,
                flhs, weight, anal, sign, current, turn, table, table_turned, sky_kept, pixel_sums,
                partial, extras, shard, rs_recv0, rs_recv1, summed, extra_sum,
                r1_live, r1_dead, steps,
                leg_sems, load_sems, order_sems, a2a_send, a2a_recv, rs_send, rs_arrive, ag_send, ag_arrive):
    me = lax.axis_index("order")
    mine = lax.axis_index("blk")
    tiles = degrees // 128
    half_turn = pixels // 2
    columns = 16 * n_order
    groups = columns // 128
    local = cycles * n_order
    part = degrees // n_blk
    sheets = modes.shape[0]

    raws = (raw0, raw1, raw2, raw3)

    def leg_copy(pair):
        return pltpu.make_async_copy(leg_hbm.at[pl.ds(2 * pair, 2)], raws[pair], leg_sems.at[pair])

    def load_copy(at):
        source, target = ((guess_hbm, guess), (rhs_hbm, rhs), (noise_hbm, noise), (flags_hbm, flags))[at]
        return pltpu.make_async_copy(source, target, load_sems.at[at])

    load_copy(0).start()
    for pair in range(4):
        leg_copy(pair).start()

    side_x = 2
    side_y = n_order // 4
    if n_order == 32:
        side_x, side_y = 4, 4
    offsets = [(a, b, c) for a in range(side_y) for b in range(side_x) for c in range(2) if a or b or c]
    offsets.sort(key=lambda o: -(2 * min(o[0], side_y - o[0]) + 2 * min(o[1], side_x - o[1]) + o[2]))
    my_y, my_x, my_c = me // (2 * side_x), (me // 2) % side_x, me % 2
    peers = [lax.rem(my_y + a, side_y) * (2 * side_x) + lax.rem(my_x + b, side_x) * 2 + lax.rem(my_c + c, 2)
             for a, b, c in offsets]
    steps_z = sorted(range(1, n_blk), key=lambda i: -min(i, n_blk - i))
    partners = [lax.rem(mine + i, n_blk) for i in steps_z]

    barrier = pltpu.get_barrier_semaphore()
    for to in peers:
        pl.semaphore_signal(barrier, inc=1, device_id=(to, mine), device_id_type=MESH)
    for to in partners:
        pl.semaphore_signal(barrier, inc=1, device_id=(me, to), device_id_type=MESH)
    for at in (1, 2, 3):
        load_copy(at).start()

    def wait_bytes(ref, sem):
        pltpu.make_async_copy(ref, ref, sem).wait()

    row8 = iota((8, 128), 0)
    lane8 = iota((8, 128), 1)
    modes[...] = jnp.zeros_like(modes)
    turned[...] = jnp.zeros_like(turned)
    scalar[...] = jnp.zeros_like(scalar)
    pixel_sums[...] = jnp.zeros_like(pixel_sums)
    upper8 = row8 < 4
    lane16 = iota((16, 128), 1)
    zero16 = iota((16, 128), 0) * 0

    def shift_rows(quad):
        return jnp.where(upper8, orders[4 * quad], orders[4 * quad + 2])

    def rolled_rows(values, quad):
        shifts = shift_rows(quad)
        whole, within = shifts // 128, shifts % 128
        low, high = orders[4 * quad] % 128, orders[4 * quad + 2] % 128
        moved = [jnp.where(upper8, lane_shift(value, low), lane_shift(value, high))
                 for value in rotate_tiles(values, whole)]
        return [jnp.where(lane8 >= within, moved[t], moved[t - 1]) for t in range(tiles)]

    def split_vector(source, live_out, dead_out):
        for quad in range(2):
            for half in range(2):
                slot = 4 * quad + 2 * half
                for r in range(2):
                    for c in range(2):
                        row = half * 4 + r * 2 + c
                        rows_a[quad, row:row + 1, :] = source[r, c, slot:slot + 1, :]
                        rows_b[quad, row:row + 1, :] = source[r, c, slot + 1:slot + 2, :]
            shifts = shift_rows(quad)
            rolled = rolled_rows([rows_b[quad, :, t * 128:t * 128 + 128] for t in range(tiles)], quad)
            for t in range(tiles):
                lanes = slice(t * 128, t * 128 + 128)
                own = lane8 + t * 128 >= shifts
                first = rows_a[quad, :, lanes]
                idle = jnp.where(own, rolled[t], first)
                if t == tiles - 1:
                    idle = jnp.where(lane8 == 127, 0.0, idle)
                live_out[quad, :, lanes] = jnp.where(own, first, rolled[t])
                dead_out[quad, :, lanes] = idle
            live_out[quad, :, degrees:degrees + 128] = jnp.where(lane8 == 0, pltpu.roll(rolled[-1], 1, 1), 0.0)

    def split_prior():
        for quad in range(2):
            shifts = shift_rows(quad)
            firsts = [jnp.broadcast_to(prior[:, t * 128:t * 128 + 128], (8, 128)) for t in range(tiles)]
            rolled = rolled_rows(firsts, quad)
            for t in range(tiles):
                lanes = slice(t * 128, t * 128 + 128)
                own = lane8 + t * 128 >= shifts
                prior_live[quad, :, lanes] = jnp.where(own, firsts[t], rolled[t])
                prior_dead[quad, :, lanes] = jnp.where(own, rolled[t], firsts[t])
            prior_live[quad, :, degrees:degrees + 128] = jnp.where(lane8 == 0, pltpu.roll(rolled[-1], 1, 1), 0.0)

    def fill_masks():
        for quad in range(2):
            shifts = shift_rows(quad)
            number_b = jnp.where(upper8, orders[4 * quad + 1], orders[4 * quad + 3])
            for t in range(tiles):
                lanes = slice(t * 128, t * 128 + 128)
                place = lane8 + t * 128
                own = place >= shifts
                total = jnp.where(own, place + shifts, place - shifts + degrees + number_b)
                parity[quad, :, lanes] = (1 - 2 * (total & 1)).astype(F32)
                mask[quad, :, lanes] = own.astype(F32)
            parity[quad, :, degrees:degrees + 128] = jnp.ones((8, 128), F32)
            mask[quad, :, degrees:degrees + 128] = jnp.zeros((8, 128), F32)

    tile = jnp.zeros((8, 128), jnp.int32)
    for m in range(8):
        tile = jnp.where(row8 == m, orders[m], tile)
    own_orders[...] = tile
    fill_masks()
    load_copy(0).wait()
    split_vector(guess, live.at[0], dead.at[0])

    pl.semaphore_wait(barrier, n_order - 1 + n_blk - 1)

    for to in peers:
        pltpu.make_async_remote_copy(
            src_ref=own_orders, dst_ref=order_recv.at[me],
            send_sem=order_sems.at[0], recv_sem=order_sems.at[1],
            device_id=(to, mine), device_id_type=MESH).start()
    order_recv[me] = own_orders[...]

    for pair in range(4):
        leg_copy(pair).wait()
        raw = raws[pair]
        shift = orders[2 * pair]
        within = shift % 128
        whole = zero16 + shift // 128

        def pack_rows(step, carry):
            rows = pl.ds(pl.multiple_of(step * 16, 16), 16)
            moved = rotate_tiles([raw[1, rows, t * 128:t * 128 + 128] for t in range(tiles)], whole)
            moved = [lane_shift(value, within) for value in moved]
            for t in range(tiles):
                rolled = jnp.where(lane16 >= within, moved[t], moved[t - 1])
                first = raw[0, rows, t * 128:t * 128 + 128]
                leg[pair, rows, t * 128:t * 128 + 128] = jnp.where(lane16 + t * 128 >= shift, first, rolled)
            extra = jnp.where(lane16 == 0, pltpu.roll(rolled, 1, 1), jnp.zeros_like(rolled))
            leg[pair, rows, degrees:degrees + 128] = extra
            return carry

        lax.fori_loop(0, local // 16, pack_rows, 0, unroll=4 if local % 64 == 0 else 1)

    def exchange_start(step):
        for to in peers:
            pltpu.make_async_remote_copy(
                src_ref=send.at[to], dst_ref=recv.at[step, me],
                send_sem=a2a_send.at[step], recv_sem=a2a_recv.at[step],
                device_id=(to, mine), device_id_type=MESH).start()
        recv[step, me] = send[me]

    def exchange_wait(step):
        wait_bytes(recv.at[step, pl.ds(0, n_order - 1)], a2a_recv.at[step])
        wait_bytes(send.at[pl.ds(0, n_order - 1)], a2a_send.at[step])

    def build_weight():
        weight[...] = jnp.zeros_like(weight)
        for j in range(cycles):
            value = noise[j] * flags[j].astype(F32)
            for h in range(2):
                for image in range(2):
                    row = value[h:h + 1, image * half_turn:(image + 1) * half_turn]
                    for r in range(2):
                        weight[image * 4 + h * 2 + r, j:j + 1, :] = row

    def build_table():
        wait_bytes(order_recv.at[pl.ds(0, n_order - 1)], order_sems.at[1])
        wait_bytes(order_recv.at[pl.ds(0, n_order - 1)], order_sems.at[0])
        number = order_recv[...]
        lane = iota((n_order, 8, 128), 2)
        scale = jnp.where(number == 0, 1.0, 2.0) * (pixels ** -0.5)

        def angle(product):
            value = product.astype(F32)
            value = value - pixels * jnp.floor(value * (1.0 / pixels))
            return value * (2.0 * jnp.pi / pixels)

        base = angle(number * lane)
        current[:, 0] = scale * jnp.cos(base)
        current[:, 1] = -scale * jnp.sin(base)
        step = angle(number * 128)
        turn[:, 0] = jnp.cos(step)
        turn[:, 1] = jnp.sin(step)
        odd = (1 - 2 * (number & 1)).astype(F32)
        sign_rows = jnp.concatenate([odd, odd], axis=1).reshape(columns, 128)
        sign[...] = sign_rows.T[0:8]

        def block(q, carry):
            lanes = pl.ds(pl.multiple_of(q * 128, 128), 128)

            def some(piece, inner):
                for k in range(8):
                    s = piece * 8 + k
                    cosine, sine = current[s, 0], current[s, 1]
                    rows = pl.ds(pl.multiple_of(s * 16, 16), 16)
                    table[rows, lanes] = jnp.concatenate([cosine, sine], axis=0).astype(BF16)
                    turn_c, turn_s = turn[s, 0], turn[s, 1]
                    current[s, 0] = cosine * turn_c + sine * turn_s
                    current[s, 1] = sine * turn_c - cosine * turn_s
                return inner

            return lax.fori_loop(0, n_order // 8, some, carry)

        lax.fori_loop(0, half_turn // 128, block, 0)

    group8 = lane8 // 16
    item8 = lane8 // 8
    first_row8 = (iota((8, 1), 0) % 4) < 2

    def by_realization(total):
        zero = jnp.sum(jnp.where(first_row8, total, 0.0), axis=0, keepdims=True)
        one = jnp.sum(jnp.where(first_row8, 0.0, total), axis=0, keepdims=True)
        return [zero, one]

    def lane_sum(value):
        return jnp.sum(value, axis=1, keepdims=True)

    def put_scalars(values):
        tile = jnp.zeros((8, 128), F32)
        for at, value in enumerate(values):
            tile = jnp.where(item8 == at, value, tile)
        return tile

    def sum_tiles(load, count):
        values = [load(s) for s in range(count)]
        while len(values) > 1:
            values = [a + b for a, b in zip(values[::2], values[1::2])]
        return values[0]

    def scalar_at(total, row, at):
        return total[row:row + 1, 8 * at:8 * at + 1]

    def rows_from(pair):
        return jnp.where(first_row8, pair[0], pair[1])

    def pair_at(total, row, at):
        return [scalar_at(total, row, at), scalar_at(total, row, at + 1)]

    lane_step = 128 * max(n for n in (5, 3, 1) if (tiles + 1) % n == 0)
    width = degrees + 128

    def application(p, carry):
        for quad in range(2):
            @pl.when(p > 0)
            def _():
                wait_bytes(rs_recv0.at[p - 1, pl.ds(0, n_blk - 1)], ag_arrive.at[p - 1, quad])
                main = pl.ds(0, degrees)
                image = prior_live[quad, :, main] * live[p - 1, quad, :, main] + summed[p - 1, quad]
                live[p, quad, :, main] = jnp.where(p == 1, rhs_live[quad, :, main] - image, image)
                tail = pl.ds(degrees, 128)
                image = prior_live[quad, :, tail] * live[p - 1, quad, :, tail] + extra_sum[quad]
                live[p, quad, :, tail] = jnp.where(p == 1, rhs_live[quad, :, tail] - image, image)

            def build(t, inner_carry):
                at = pl.ds(t * lane_step, lane_step)
                value = live[p, quad, :, at]
                first = mask[quad, :, at]
                second = 1.0 - first
                flip = parity[quad, :, at]
                high = value.astype(BF16).astype(F32)
                rest = value - high
                pieces = []
                for piece in (high, rest):
                    for keep in (first, second):
                        kept = piece * keep
                        pieces.append(kept)
                        pieces.append(kept * flip)
                lhs[quad, :, at] = jnp.concatenate(pieces, axis=0).astype(BF16)
                return inner_carry

            for t in range(width // lane_step):
                build(t, 0)
            for half in range(2):
                pair = 2 * quad + half


                def keep(out, pair=pair, at=4 * half):
                    out = out[0:32] + out[32:64]
                    for slot in range(2):
                        rows = jnp.concatenate([out[16 * slot + at:16 * slot + at + 4],
                                                out[16 * slot + 8 + at:16 * slot + 8 + at + 4]], axis=0)
                        if sheets * 128 > local:
                            rows = jnp.concatenate([rows, jnp.zeros((8, sheets * 128 - local), F32)], axis=1)
                        for sheet in range(sheets):
                            modes[sheet, pl.ds(2 * pair + slot, 8, stride=8), :] = (
                                rows[:, 128 * sheet:128 * sheet + 128])

                @pl.when(p == 0)
                def _():
                    keep(lax.dot_general(lhs[quad], leg[pair], NT, preferred_element_type=F32))

                @pl.when(p > 0)
                def _():
                    keep(jnp.dot(lhs[quad], leg_turned[pair], preferred_element_type=F32))

        @pl.when(p > 0)
        def _():
            for quad in range(2):
                wait_bytes(rs_recv0.at[p - 1, pl.ds(0, n_blk - 1)], ag_send.at[p - 1, quad])

        for sheet in range(sheets):
            turned[128 * sheet:128 * sheet + 128, :] = modes[sheet].T

        @pl.when(p == 2)
        def _():
            norm = cross = jnp.zeros((8, 1), F32)
            for quad in range(2):
                for held in (live, dead):
                    norm = norm + lane_sum(held[1, quad] * held[1, quad])
                    cross = cross + lane_sum(held[1, quad] * held[2, quad])
            scalar[...] = put_scalars(by_realization(norm) + by_realization(cross))

        for d in range(n_order):
            send[d] = jnp.where(row8 < cycles, turned[cycles * d:cycles * d + 8, :], scalar[...])
        exchange_start(2 * p)

        @pl.when(p == 0)
        def _():
            build_table()
            load_copy(2).wait()
            load_copy(3).wait()
            build_weight()
            split_prior()

        exchange_wait(2 * p)

        @pl.when(p == 2)
        def _():
            total = sum_tiles(lambda s: recv[2 * p, s], n_order)
            norm, cross = pair_at(total, 7, 0), pair_at(total, 7, 2)
            ratio = [norm[0] / cross[0], norm[1] / cross[1]]
            step = rows_from(ratio)
            steps[0] = jnp.broadcast_to(rows_from(norm), (8, 128))
            steps[1] = jnp.broadcast_to(step, (8, 128))
            steps[2] = jnp.broadcast_to(ratio[0], (8, 128))
            steps[3] = jnp.broadcast_to(ratio[1], (8, 128))
            sums = [jnp.zeros((8, 1), F32)] * 4
            for quad in range(2):
                for r1, held, inv in ((r1_live, live, prior_live), (r1_dead, dead, prior_dead)):
                    before = held[1, quad]
                    after = before - step * held[2, quad]
                    r1[quad] = after
                    scaled = inv[quad] * after
                    sums = [total + lane_sum(value) for total, value in zip(
                        sums, (after * after, scaled * after, scaled * before, inv[quad] * before * before))]
            scalar[...] = put_scalars([value for total in sums for value in by_realization(total)])

        def shuffle(g, inner_carry):
            lanes = pl.ds(g * 128, 128)
            flip = sign[:, lanes]
            held = [recv[2 * p, g * 8 + i] for i in range(8)]
            straight = []
            for hr in range(4):
                acc = held[0] if hr == 0 else pltpu.roll(held[0], (128 - 16 * hr) % 128, 1)
                for i in range(1, 8):
                    by = (16 * i - 16 * hr) % 128
                    moved = held[i] if by == 0 else pltpu.roll(held[i], by, 1)
                    acc = jnp.where(group8 == i, moved, acc)
                straight.append(acc)
            flipped = [acc * flip for acc in straight]
            rows = jnp.concatenate(straight + flipped, axis=0)
            high, rest = split_bf16(rows)
            flhs[0:64, lanes] = high
            flhs[64:128, lanes] = rest
            return inner_carry

        for g in range(groups):
            shuffle(g, 0)

        anal[...] = jnp.zeros_like(anal)
        chunk = min(1536, half_turn)

        def fourier(t, inner_carry):
            lanes = pl.ds(pl.multiple_of(t * chunk, 128), chunk)
            block = table[:, lanes]
            sky = jnp.dot(flhs[...], block, preferred_element_type=F32)
            sky = sky[0:64] + sky[64:128]
            scaled = sky * weight[:, :, lanes].reshape(64, chunk)
            high, rest = split_bf16(scaled)
            both = jnp.concatenate([high, rest], axis=0)

            @pl.when(p == 0)
            def _():
                out = lax.dot_general(both, block, NT, preferred_element_type=F32)
                anal[...] += out[0:64] + out[64:128]

            @pl.when(p > 0)
            def _():
                out = jnp.dot(both, table_turned[lanes, :], preferred_element_type=F32)
                anal[...] += out[0:64] + out[64:128]

            @pl.when(p == 1)
            def _():
                sky_kept[:, lanes] = sky

            @pl.when(p == 2)
            def _():
                for hr in range(8):
                    rows = slice(8 * hr, 8 * hr + 8)
                    before = sky_kept[rows, lanes]
                    after = before - steps[2 + hr % 2][:, 0:1] * sky[rows]
                    weighed = weight[hr, :, lanes]
                    heavy = weighed * after
                    for at, value in enumerate((heavy * after, heavy * before, weighed * before * before)):
                        total = pixel_sums[2 * at + hr % 2]
                        for k in range(chunk // 128):
                            total = total + value[:, 128 * k:128 * k + 128]
                        pixel_sums[2 * at + hr % 2] = total

            return inner_carry

        lax.fori_loop(0, half_turn // chunk, fourier, 0)

        @pl.when(p == 2)
        def _():
            tile = scalar[...]
            for at in range(6):
                value = jnp.sum(lane_sum(pixel_sums[at]), axis=0, keepdims=True)
                tile = jnp.where(item8 == 8 + at, value, tile)
            scalar[...] = tile

        def shuffle_back(g, inner_carry):
            lanes = pl.ds(g * 128, 128)
            flip = sign[:, lanes]
            rows = [anal[8 * hr:8 * hr + 8, lanes] + flip * anal[32 + 8 * hr:40 + 8 * hr, lanes] for hr in range(4)]
            base = scalar[...]
            for i in range(8):
                acc = jnp.zeros((8, 128), F32)
                for hr in range(4):
                    by = (16 * hr - 16 * i) % 128
                    moved = rows[hr] if by == 0 else pltpu.roll(rows[hr], by, 1)
                    acc = jnp.where(group8 == hr, moved, acc)
                send[g * 8 + i] = jnp.where(row8 < cycles, acc, base)
            return inner_carry

        for g in range(groups):
            shuffle_back(g, 0)
        exchange_start(2 * p + 1)

        @pl.when(p == 0)
        def _():
            load_copy(1).wait()
            split_vector(rhs, rhs_live, rhs_dead)

            def turn_leg(pair, inner_carry):
                for t in range(width // lane_step):
                    at = slice(t * lane_step, t * lane_step + lane_step)
                    leg_turned[pair, at, :] = leg[pair, :, at].T
                return inner_carry

            lax.fori_loop(0, 4, turn_leg, 0)

            def turn_table(t, inner_carry):
                at = pl.ds(pl.multiple_of(t * 256, 256), 256)
                table_turned[at, :] = table[:, at].T
                return inner_carry

            lax.fori_loop(0, half_turn // 256, turn_table, 0)

        for quad in range(2):
            image = prior_dead[quad] * dead[p, quad]
            dead[p + 1, quad] = jnp.where(p == 0, rhs_dead[quad] - image, image)
        exchange_wait(2 * p + 1)

        for d in range(n_order):
            turned[cycles * d:cycles * d + cycles, :] = recv[2 * p + 1, d, 0:cycles, :]
        for sheet in range(sheets):
            back[sheet] = turned[128 * sheet:128 * sheet + 128, :].T

        for quad in range(2):
            for half in range(2):
                pair = 2 * quad + half
                rows = jnp.concatenate([
                    jnp.concatenate([back[sheet, pl.ds(2 * pair + slot, 8, stride=8), :] for sheet in range(sheets)],
                                    axis=1)
                    for slot in range(2)], axis=0)
                high, rest = split_bf16(rows[:, 0:local])
                both = jnp.concatenate([high, rest], axis=0)
                mine_rows = slice(4 * half, 4 * half + 4)
                one_row = slice(4 * half, 4 * half + 1)

                def analyse(t, inner_carry):
                    at = pl.ds(t * 2 * part, 2 * part)
                    out = jnp.dot(both, leg[pair, :, at], preferred_element_type=F32)
                    out = out[0:16] + out[16:32]
                    kept = jnp.where(mask[quad, one_row, at] > 0.5, out[0:8], out[8:16])
                    value = kept[0:4] + parity[quad, one_row, at] * kept[4:8]
                    partial[quad, 2 * t, mine_rows, 0:part] = value[:, 0:part]
                    partial[quad, 2 * t + 1, mine_rows, 0:part] = value[:, part:2 * part]
                    return inner_carry

                for t in range(n_blk // 2):
                    analyse(t, 0)
                out = jnp.dot(both, leg[pair, :, degrees:degrees + 128], preferred_element_type=F32)
                out = out[0:16] + out[16:32]
                extras[quad, mine_rows, :] = out[8:12] + out[12:16]
            if quad == 1:
                total = sum_tiles(lambda s: recv[2 * p + 1, s], n_order)
                tile = jnp.where(lane8 == 0, extras[0], 0.0)
                tile = jnp.where(lane8 == 1, pltpu.roll(extras[1], 1, 1), tile)
                scalar[...] = total
                tile = jnp.where((lane8 >= 64) & (row8 == 7), total, tile)
                for b in range(n_blk):
                    partial[1, b, :, part:part + 128] = tile
            for to in partners:
                source = partial.at[0, to, :, pl.ds(0, part)] if quad == 0 else partial.at[1, to]
                target = rs_recv0 if quad == 0 else rs_recv1
                pltpu.make_async_remote_copy(
                    src_ref=source, dst_ref=target.at[p, mine],
                    send_sem=rs_send.at[p, quad], recv_sem=rs_arrive.at[p, quad],
                    device_id=(me, to), device_id_type=MESH).start()

        my_lanes = pl.ds(pl.multiple_of(mine * part, 128), part)
        for quad in range(2):
            arrived = rs_recv0 if quad == 0 else rs_recv1
            arrived[p, mine] = partial[quad, mine, :, 0:arrived.shape[3]]
            wait_bytes(arrived.at[p, pl.ds(0, n_blk - 1)], rs_arrive.at[p, quad])
            total = sum_tiles(lambda b: arrived[p, b], n_blk)
            shard[quad] = total[:, 0:part]
            for to in partners:
                pltpu.make_async_remote_copy(
                    src_ref=shard.at[quad], dst_ref=summed.at[p, quad, :, my_lanes],
                    send_sem=ag_send.at[p, quad], recv_sem=ag_arrive.at[p, quad],
                    device_id=(me, to), device_id_type=MESH).start()
            summed[p, quad, :, my_lanes] = total[:, 0:part]
            wait_bytes(arrived.at[p, pl.ds(0, n_blk - 1)], rs_send.at[p, quad])
        tile = total[:, part:part + 128]
        extra_sum[0] = jnp.where(lane8 == 0, tile, 0.0)
        extra_sum[1] = jnp.where(lane8 == 0, pltpu.roll(tile, 127, 1), 0.0)
        extra_sum[2] = tile
        return carry

    lax.fori_loop(0, 3, application, 0)

    within_order, over_all = scalar[...], extra_sum[2]
    norm = [steps[0, 0:1, 0:1], steps[0, 2:3, 0:1]]
    ratios, seconds = [], []
    for r in range(2):
        after = scalar_at(within_order, 7, r)
        ratio = after / norm[r]
        curve = (scalar_at(within_order, 7, 2 + r) + scalar_at(over_all, 7, 8 + r)
                 + 2.0 * ratio * (scalar_at(within_order, 7, 4 + r) + scalar_at(over_all, 7, 10 + r))
                 + ratio * ratio * (scalar_at(within_order, 7, 6 + r) + scalar_at(over_all, 7, 12 + r)))
        ratios.append(ratio)
        seconds.append(after / curve)
    ratio, second = rows_from(ratios), rows_from(seconds)
    step = steps[1, :, 0:1]

    def finish(quad, lanes, held, r1, last, x_out, r_out):
        before, middle = held[1, quad, :, lanes], held[2, quad, :, lanes]
        after = r1[quad, :, lanes]
        direction = after + ratio * before
        image = (1.0 + ratio) * middle - step * last
        x_out[quad, :, lanes] = held[0, quad, :, lanes] + step * before + second * direction
        r_out[quad, :, lanes] = after - second * image

    main, tail = pl.ds(0, degrees), pl.ds(degrees, 128)
    for quad in range(2):
        finish(quad, main, dead, r1_dead, dead[3, quad], x_out_dead, r_out_dead)
        last = prior_live[quad, :, tail] * live[2, quad, :, tail] + extra_sum[quad]
        finish(quad, tail, live, r1_live, last, x_out_live, r_out_live)
    for quad in range(2):
        wait_bytes(rs_recv0.at[2, pl.ds(0, n_blk - 1)], ag_arrive.at[2, quad])
        last = prior_live[quad, :, main] * live[2, quad, :, main] + summed[2, quad]
        finish(quad, main, live, r1_live, last, x_out_live, r_out_live)
    for quad in range(2):
        wait_bytes(rs_recv0.at[2, pl.ds(0, n_blk - 1)], ag_send.at[2, quad])


def per_device(n_order, n_blk, right_side, start_guess, legendre, orders, prior_inv, noise_inv, pixel_flags):
    slots, local, degrees = legendre.shape
    cycles, pixels = noise_inv.shape[1], noise_inv.shape[2]
    width = degrees + 128
    part = degrees // n_blk
    smem = pl.BlockSpec(memory_space=pltpu.SMEM)
    vmem = pl.BlockSpec(memory_space=pltpu.VMEM)
    hbm = pl.BlockSpec(memory_space=pl.ANY)
    live_shape = jax.ShapeDtypeStruct((2, 8, width), F32)
    dead_shape = jax.ShapeDtypeStruct((2, 8, degrees), F32)
    columns = 16 * n_order
    sheets = -(-(local + 8) // 128)
    half_turn = pixels // 2
    scratch = [pltpu.VMEM((2, local, degrees), BF16)] * 4 + [
        pltpu.VMEM((8, 128), jnp.int32),
        pltpu.VMEM(right_side.shape, F32),
        pltpu.VMEM(right_side.shape, F32),
        pltpu.VMEM((2, 8, degrees), F32),
        pltpu.VMEM((2, 8, degrees), F32),
        pltpu.VMEM((4, local, width), BF16),
        pltpu.VMEM((4, width, local), BF16),
        pltpu.VMEM((3, 2, 8, width), F32),
        pltpu.VMEM((4, 2, 8, degrees), F32),
        pltpu.VMEM((2, 8, width), F32),
        pltpu.VMEM((2, 8, degrees), F32),
        pltpu.VMEM((2, 8, width), F32),
        pltpu.VMEM((2, 8, degrees), F32),
        pltpu.VMEM((2, 8, width), F32),
        pltpu.VMEM((2, 8, width), F32),
        pltpu.VMEM((cycles, 2, pixels), F32),
        pltpu.VMEM((cycles, 2, pixels), jnp.int32),
        pltpu.VMEM((2, 64, width), BF16),
        pltpu.VMEM((sheets, 128, 128), F32),
        pltpu.VMEM((sheets * 128, 128), F32),
        pltpu.VMEM((sheets, 128, 128), F32),
        pltpu.VMEM((n_order, 8, 128), F32),
        pltpu.VMEM((6, n_order, 8, 128), F32),
        pltpu.VMEM((n_order, 8, 128), jnp.int32),
        pltpu.VMEM((8, 128), F32),
        pltpu.VMEM((128, columns), BF16),
        pltpu.VMEM((8, 8, half_turn), F32),
        pltpu.VMEM((64, columns), F32),
        pltpu.VMEM((8, columns), F32),
        pltpu.VMEM((n_order, 2, 8, 128), F32),
        pltpu.VMEM((n_order, 2, 8, 128), F32),
        pltpu.VMEM((columns, half_turn), BF16),
        pltpu.VMEM((half_turn, columns), BF16),
        pltpu.VMEM((64, half_turn), F32),
        pltpu.VMEM((6, 8, 128), F32),
        pltpu.VMEM((2, n_blk, 8, part + 128), F32),
        pltpu.VMEM((2, 8, 128), F32),
        pltpu.VMEM((2, 8, part), F32),
        pltpu.VMEM((3, n_blk, 8, part), F32),
        pltpu.VMEM((3, n_blk, 8, part + 128), F32),
        pltpu.VMEM((3, 2, 8, degrees), F32),
        pltpu.VMEM((3, 8, 128), F32),
        pltpu.VMEM((2, 8, width), F32),
        pltpu.VMEM((2, 8, degrees), F32),
        pltpu.VMEM((4, 8, 128), F32),
        pltpu.SemaphoreType.DMA((4,)),
        pltpu.SemaphoreType.DMA((4,)),
        pltpu.SemaphoreType.DMA((2,)),
        pltpu.SemaphoreType.DMA((6,)),
        pltpu.SemaphoreType.DMA((6,)),
        pltpu.SemaphoreType.DMA((3, 2)),
        pltpu.SemaphoreType.DMA((3, 2)),
        pltpu.SemaphoreType.DMA((3, 2)),
        pltpu.SemaphoreType.DMA((3, 2)),
    ]
    results = pl.pallas_call(
        functools.partial(main_kernel, n_order, n_blk, degrees, cycles, pixels),
        in_specs=[smem, hbm, hbm, hbm, vmem, hbm, hbm],
        out_specs=[vmem] * 4,
        out_shape=[live_shape, dead_shape, live_shape, dead_shape],
        scratch_shapes=scratch,
        compiler_params=pltpu.CompilerParams(
            collective_id=0, has_side_effects=True, vmem_limit_bytes=VMEM_LIMIT),
        name="steps",
    )(orders, legendre, start_guess, right_side, prior_inv.reshape(1, degrees),
      noise_inv.transpose(1, 0, 2), pixel_flags.transpose(1, 0, 2))

    full = jax.ShapeDtypeStruct(right_side.shape, F32)
    return tuple(pl.pallas_call(
        functools.partial(unpack_kernel, degrees),
        in_specs=[smem] + [vmem] * 4,
        out_specs=[vmem] * 2,
        out_shape=[full, full],
        scratch_shapes=[pltpu.VMEM((2, 8, degrees), F32)] * 2,
        compiler_params=pltpu.CompilerParams(vmem_limit_bytes=VMEM_LIMIT),
        name="unpack",
    )(orders, *results))


def solution(mesh):
    in_specs = (
        P(None, None, "order", None),
        P(None, None, "order", None),
        P("order", "blk", None),
        P("order"),
        P(),
        P(None, ("blk", "order"), None),
        P(None, ("blk", "order"), None),
    )
    out_specs = (P(None, None, "order", None), P(None, None, "order", None))
    body = functools.partial(per_device, mesh.shape["order"], mesh.shape["blk"])
    return jax.shard_map(body, mesh=mesh, in_specs=in_specs, out_specs=out_specs, check_vma=False)
```

```python
import functools

import jax
import jax.numpy as jnp
from jax import lax
from jax.experimental import pallas as pl
from jax.experimental.pallas import tpu as pltpu
from jax.sharding import PartitionSpec as P

MESH = pl.DeviceIdType.MESH
F32 = jnp.float32
BF16 = jnp.bfloat16
VMEM_LIMIT = 56 * 1024 * 1024
NT = (((1,), (1,)), ((), ()))


def iota(shape, dim):
    return lax.broadcasted_iota(jnp.int32, shape, dim)


def tile_lanes(t, shift, less, tiles):
    at = lax.rem(t - shift // 128 - less + 2 * tiles, tiles) * 128
    return pl.ds(pl.multiple_of(at, 128), 128)


def rolled_tiles(load, shift, tiles, lane):
    within = lax.rem(shift, 128)
    before = pltpu.roll(load(tile_lanes(0, shift, 1, tiles)), within, 1)
    for t in range(tiles):
        now = pltpu.roll(load(tile_lanes(t, shift, 0, tiles)), within, 1)
        yield jnp.where(lane >= within, now, before)
        before = now


def rotate_tiles(tiles, whole):
    count = len(tiles)
    for bit in range((count - 1).bit_length()):
        moved = (whole & (1 << bit)) != 0
        tiles = [jnp.where(moved, tiles[(t - (1 << bit)) % count], tiles[t]) for t in range(count)]
    return tiles


def lane_shift(value, within):
    return pltpu.roll(value, within, 1)


def split_rows(value, first, flip):
    high = value.astype(BF16).astype(F32)
    pieces = []
    for piece in (high, value - high):
        for keep in (first, 1.0 - first):
            kept = piece * keep
            pieces.append(kept)
            pieces.append(kept * flip)
    return jnp.concatenate(pieces, axis=0).astype(BF16)


def place_modes(modes, out, pair, local):
    sheets = modes.shape[0]
    at = 4 * (pair % 2)
    out = out[0:32] + out[32:64]
    for slot in range(2):
        rows = jnp.concatenate([out[16 * slot + at:16 * slot + at + 4],
                                out[16 * slot + 8 + at:16 * slot + 8 + at + 4]], axis=0)
        if sheets * 128 > local:
            rows = jnp.concatenate([rows, jnp.zeros((8, sheets * 128 - local), F32)], axis=1)
        for sheet in range(sheets):
            modes[sheet, pl.ds(2 * pair + slot, 8, stride=8), :] = rows[:, 128 * sheet:128 * sheet + 128]


def unpack_kernel(degrees, orders, x_live, x_dead, r_live, r_dead, x_out, r_out, rows_a, rows_b):
    tiles = degrees // 128
    lane8 = iota((8, 128), 1)
    upper = iota((8, 128), 0) < 4
    for quad in range(2):
        low, high = orders[4 * quad], orders[4 * quad + 2]
        shifts = jnp.where(upper, low, high)
        back_low, back_high = lax.rem(degrees - low, degrees), lax.rem(degrees - high, degrees)
        for at, (live, dead, out) in enumerate(((x_live, x_dead, x_out), (r_live, r_dead, r_out))):
            for t in range(tiles):
                lanes = slice(t * 128, t * 128 + 128)
                own = lane8 + t * 128 >= shifts
                alive, idle = live[quad, :, lanes], dead[quad, :, lanes]
                rows_a[at, :, lanes] = jnp.where(own, alive, idle)
                second = jnp.where(own, idle, alive)
                if t == tiles - 1:
                    extra = live[quad, :, degrees:degrees + 128]
                    second = jnp.where(lane8 == 127, pltpu.roll(extra, 127, 1), second)
                rows_b[at, :, lanes] = second
            load = lambda lanes: rows_b[at, :, lanes]
            back = zip(rolled_tiles(load, back_low, tiles, lane8), rolled_tiles(load, back_high, tiles, lane8))
            kept = [jnp.where(upper, one, two) for one, two in back]
            for t, value in enumerate(kept):
                rows_b[at, :, t * 128:t * 128 + 128] = value
            for half in range(2):
                slot = 4 * quad + 2 * half
                for r in range(2):
                    for c in range(2):
                        row = half * 4 + r * 2 + c
                        out[r, c, slot:slot + 1, :] = rows_a[at, row:row + 1, :]
                        out[r, c, slot + 1:slot + 2, :] = rows_b[at, row:row + 1, :]


def split_bf16(values):
    high = values.astype(BF16)
    return high, (values - high.astype(F32)).astype(BF16)


def main_kernel(n_order, n_blk, degrees, cycles, pixels,
                orders, leg_hbm, guess_hbm, rhs_hbm, prior, noise_hbm, flags_hbm,
                x_out_live, x_out_dead, r_out_live, r_out_dead,
                raw0, raw1, raw2, raw3, own_orders, guess, rhs, rows_a, rows_b,
                leg, leg_turned, live, dead, rhs_live, rhs_dead, prior_live, prior_dead, mask, parity, noise, flags,
                lhs, modes, turned, back, send, recv, order_recv, scalar,
                flhs, weight, anal, sign, current, turn, table, table_turned, sky_kept, pixel_sums,
                partial, extras, shard, rs_recv0, rs_recv1, summed, extra_sum,
                r1_live, r1_dead, steps,
                leg_sems, load_sems, order_sems, a2a_send, a2a_recv, rs_send, rs_arrive, ag_send, ag_arrive):
    me = lax.axis_index("order")
    mine = lax.axis_index("blk")
    tiles = degrees // 128
    half_turn = pixels // 2
    columns = 16 * n_order
    groups = columns // 128
    local = cycles * n_order
    part = degrees // n_blk
    sheets = modes.shape[0]

    raws = (raw0, raw1, raw2, raw3)

    def leg_copy(pair):
        return pltpu.make_async_copy(leg_hbm.at[pl.ds(2 * pair, 2)], raws[pair], leg_sems.at[pair])

    def load_copy(at):
        source, target = ((guess_hbm, guess), (rhs_hbm, rhs), (noise_hbm, noise), (flags_hbm, flags))[at]
        return pltpu.make_async_copy(source, target, load_sems.at[at])

    for at in (0, 2, 3):
        load_copy(at).start()
    for pair in range(4):
        leg_copy(pair).start()

    side_x = 2
    side_y = n_order // 4
    if n_order == 32:
        side_x, side_y = 4, 4
    offsets = [(a, b, c) for a in range(side_y) for b in range(side_x) for c in range(2) if a or b or c]
    offsets.sort(key=lambda o: -(2 * min(o[0], side_y - o[0]) + 2 * min(o[1], side_x - o[1]) + o[2]))
    my_y, my_x, my_c = me // (2 * side_x), (me // 2) % side_x, me % 2
    peers = [lax.rem(my_y + a, side_y) * (2 * side_x) + lax.rem(my_x + b, side_x) * 2 + lax.rem(my_c + c, 2)
             for a, b, c in offsets]
    steps_z = sorted(range(1, n_blk), key=lambda i: -min(i, n_blk - i))
    partners = [lax.rem(mine + i, n_blk) for i in steps_z]

    barrier = pltpu.get_barrier_semaphore()
    for to in peers:
        pl.semaphore_signal(barrier, inc=1, device_id=(to, mine), device_id_type=MESH)
    for to in partners:
        pl.semaphore_signal(barrier, inc=1, device_id=(me, to), device_id_type=MESH)
    load_copy(1).start()

    def wait_bytes(ref, sem):
        pltpu.make_async_copy(ref, ref, sem).wait()

    row8 = iota((8, 128), 0)
    lane8 = iota((8, 128), 1)
    modes[...] = jnp.zeros_like(modes)
    turned[...] = jnp.zeros_like(turned)
    scalar[...] = jnp.zeros_like(scalar)
    pixel_sums[...] = jnp.zeros_like(pixel_sums)
    upper8 = row8 < 4
    lane16 = iota((16, 128), 1)
    zero16 = iota((16, 128), 0) * 0

    def shift_rows(quad):
        return jnp.where(upper8, orders[4 * quad], orders[4 * quad + 2])

    def rolled_rows(values, quad):
        shifts = shift_rows(quad)
        whole, within = shifts // 128, shifts % 128
        low, high = orders[4 * quad] % 128, orders[4 * quad + 2] % 128
        moved = [jnp.where(upper8, lane_shift(value, low), lane_shift(value, high))
                 for value in rotate_tiles(values, whole)]
        return [jnp.where(lane8 >= within, moved[t], moved[t - 1]) for t in range(tiles)]

    def split_vector(source, live_out, dead_out):
        for quad in range(2):
            for half in range(2):
                slot = 4 * quad + 2 * half
                for r in range(2):
                    for c in range(2):
                        row = half * 4 + r * 2 + c
                        rows_a[quad, row:row + 1, :] = source[r, c, slot:slot + 1, :]
                        rows_b[quad, row:row + 1, :] = source[r, c, slot + 1:slot + 2, :]
            shifts = shift_rows(quad)
            rolled = rolled_rows([rows_b[quad, :, t * 128:t * 128 + 128] for t in range(tiles)], quad)
            for t in range(tiles):
                lanes = slice(t * 128, t * 128 + 128)
                own = lane8 + t * 128 >= shifts
                first = rows_a[quad, :, lanes]
                idle = jnp.where(own, rolled[t], first)
                if t == tiles - 1:
                    idle = jnp.where(lane8 == 127, 0.0, idle)
                live_out[quad, :, lanes] = jnp.where(own, first, rolled[t])
                dead_out[quad, :, lanes] = idle
            live_out[quad, :, degrees:degrees + 128] = jnp.where(lane8 == 0, pltpu.roll(rolled[-1], 1, 1), 0.0)

    def split_prior():
        for quad in range(2):
            shifts = shift_rows(quad)
            firsts = [jnp.broadcast_to(prior[:, t * 128:t * 128 + 128], (8, 128)) for t in range(tiles)]
            rolled = rolled_rows(firsts, quad)
            for t in range(tiles):
                lanes = slice(t * 128, t * 128 + 128)
                own = lane8 + t * 128 >= shifts
                prior_live[quad, :, lanes] = jnp.where(own, firsts[t], rolled[t])
                prior_dead[quad, :, lanes] = jnp.where(own, rolled[t], firsts[t])
            prior_live[quad, :, degrees:degrees + 128] = jnp.where(lane8 == 0, pltpu.roll(rolled[-1], 1, 1), 0.0)

    def fill_masks():
        for quad in range(2):
            shifts = shift_rows(quad)
            number_b = jnp.where(upper8, orders[4 * quad + 1], orders[4 * quad + 3])
            for t in range(tiles):
                lanes = slice(t * 128, t * 128 + 128)
                place = lane8 + t * 128
                own = place >= shifts
                total = jnp.where(own, place + shifts, place - shifts + degrees + number_b)
                parity[quad, :, lanes] = (1 - 2 * (total & 1)).astype(F32)
                mask[quad, :, lanes] = own.astype(F32)
            parity[quad, :, degrees:degrees + 128] = jnp.ones((8, 128), F32)
            mask[quad, :, degrees:degrees + 128] = jnp.zeros((8, 128), F32)

    tile = jnp.zeros((8, 128), jnp.int32)
    for m in range(8):
        tile = jnp.where(row8 == m, orders[m], tile)
    own_orders[...] = tile
    def build_weight():
        weight[...] = jnp.zeros_like(weight)
        for j in range(cycles):
            value = noise[j] * flags[j].astype(F32)
            for h in range(2):
                for image in range(2):
                    row = value[h:h + 1, image * half_turn:(image + 1) * half_turn]
                    for r in range(2):
                        weight[image * 4 + h * 2 + r, j:j + 1, :] = row

    fill_masks()
    load_copy(0).wait()
    split_vector(guess, live.at[0], dead.at[0])
    split_prior()
    load_copy(2).wait()
    load_copy(3).wait()
    build_weight()

    width = degrees + 128
    lane_step = 128 * max(n for n in (5, 3, 1) if (tiles + 1) % n == 0)

    def build_rows(p, quad):
        for t in range(width // lane_step):
            at = pl.ds(t * lane_step, lane_step)
            lhs[quad, :, at] = split_rows(live[p, quad, :, at], mask[quad, :, at], parity[quad, :, at])

    def turn_modes():
        for sheet in range(sheets):
            turned[128 * sheet:128 * sheet + 128, :] = modes[sheet].T

    for quad in range(2):
        build_rows(0, quad)

    pl.semaphore_wait(barrier, n_order - 1 + n_blk - 1)

    for to in peers:
        pltpu.make_async_remote_copy(
            src_ref=own_orders, dst_ref=order_recv.at[me],
            send_sem=order_sems.at[0], recv_sem=order_sems.at[1],
            device_id=(to, mine), device_id_type=MESH).start()
    order_recv[me] = own_orders[...]

    for pair in range(4):
        leg_copy(pair).wait()
        raw = raws[pair]
        shift = orders[2 * pair]
        within = shift % 128
        whole = zero16 + shift // 128

        def pack_rows(step, carry):
            rows = pl.ds(pl.multiple_of(step * 16, 16), 16)
            moved = rotate_tiles([raw[1, rows, t * 128:t * 128 + 128] for t in range(tiles)], whole)
            moved = [lane_shift(value, within) for value in moved]
            for t in range(tiles):
                rolled = jnp.where(lane16 >= within, moved[t], moved[t - 1])
                first = raw[0, rows, t * 128:t * 128 + 128]
                leg[pair, rows, t * 128:t * 128 + 128] = jnp.where(lane16 + t * 128 >= shift, first, rolled)
            extra = jnp.where(lane16 == 0, pltpu.roll(rolled, 1, 1), jnp.zeros_like(rolled))
            leg[pair, rows, degrees:degrees + 128] = extra
            return carry

        lax.fori_loop(0, local // 16, pack_rows, 0, unroll=4 if local % 64 == 0 else 1)
        place_modes(modes, lax.dot_general(lhs[pair // 2], leg[pair], NT, preferred_element_type=F32), pair, local)

    turn_modes()

    def exchange_start(step):
        for to in peers:
            pltpu.make_async_remote_copy(
                src_ref=send.at[to], dst_ref=recv.at[step, me],
                send_sem=a2a_send.at[step], recv_sem=a2a_recv.at[step],
                device_id=(to, mine), device_id_type=MESH).start()
        recv[step, me] = send[me]

    def exchange_wait(step):
        wait_bytes(recv.at[step, pl.ds(0, n_order - 1)], a2a_recv.at[step])
        wait_bytes(send.at[pl.ds(0, n_order - 1)], a2a_send.at[step])

    def build_table():
        wait_bytes(order_recv.at[pl.ds(0, n_order - 1)], order_sems.at[1])
        wait_bytes(order_recv.at[pl.ds(0, n_order - 1)], order_sems.at[0])
        number = order_recv[...]
        lane = iota((n_order, 8, 128), 2)
        scale = jnp.where(number == 0, 1.0, 2.0) * (pixels ** -0.5)

        def angle(product):
            value = product.astype(F32)
            value = value - pixels * jnp.floor(value * (1.0 / pixels))
            return value * (2.0 * jnp.pi / pixels)

        base = angle(number * lane)
        current[:, 0] = scale * jnp.cos(base)
        current[:, 1] = -scale * jnp.sin(base)
        step = angle(number * 128)
        turn[:, 0] = jnp.cos(step)
        turn[:, 1] = jnp.sin(step)
        odd = (1 - 2 * (number & 1)).astype(F32)
        sign_rows = jnp.concatenate([odd, odd], axis=1).reshape(columns, 128)
        sign[...] = sign_rows.T[0:8]

        def some(piece, inner):
            held = []
            for k in range(8):
                s = piece * 8 + k
                held.append((current[s, 0], current[s, 1], turn[s, 0], turn[s, 1]))
            for q in range(half_turn // 128):
                for k in range(8):
                    cosine, sine, turn_c, turn_s = held[k]
                    rows = pl.ds(pl.multiple_of((piece * 8 + k) * 16, 16), 16)
                    table[rows, q * 128:q * 128 + 128] = jnp.concatenate([cosine, sine], axis=0).astype(BF16)
                    held[k] = (cosine * turn_c + sine * turn_s, sine * turn_c - cosine * turn_s, turn_c, turn_s)
            return inner

        lax.fori_loop(0, n_order // 8, some, 0)

    group8 = lane8 // 16
    item8 = lane8 // 8
    first_row8 = (iota((8, 1), 0) % 4) < 2

    def by_realization(total):
        zero = jnp.sum(jnp.where(first_row8, total, 0.0), axis=0, keepdims=True)
        one = jnp.sum(jnp.where(first_row8, 0.0, total), axis=0, keepdims=True)
        return [zero, one]

    def lane_sum(value):
        return jnp.sum(value, axis=1, keepdims=True)

    def put_scalars(values):
        tile = jnp.zeros((8, 128), F32)
        for at, value in enumerate(values):
            tile = jnp.where(item8 == at, value, tile)
        return tile

    def sum_tiles(load, count):
        values = [load(s) for s in range(count)]
        while len(values) > 1:
            values = [a + b for a, b in zip(values[::2], values[1::2])]
        return values[0]

    def scalar_at(total, row, at):
        return total[row:row + 1, 8 * at:8 * at + 1]

    def rows_from(pair):
        return jnp.where(first_row8, pair[0], pair[1])

    def pair_at(total, row, at):
        return [scalar_at(total, row, at), scalar_at(total, row, at + 1)]


    def application(p, carry):
        @pl.when(p > 0)
        def _():
            for quad in range(2):
                wait_bytes(rs_recv0.at[p - 1, pl.ds(0, n_blk - 1)], ag_arrive.at[p - 1, quad])
                main = pl.ds(0, degrees)
                image = prior_live[quad, :, main] * live[p - 1, quad, :, main] + summed[p - 1, quad]
                live[p, quad, :, main] = jnp.where(p == 1, rhs_live[quad, :, main] - image, image)
                tail = pl.ds(degrees, 128)
                image = prior_live[quad, :, tail] * live[p - 1, quad, :, tail] + extra_sum[quad]
                live[p, quad, :, tail] = jnp.where(p == 1, rhs_live[quad, :, tail] - image, image)
                build_rows(p, quad)
                for half in range(2):
                    pair = 2 * quad + half
                    place_modes(modes, jnp.dot(lhs[quad], leg_turned[pair], preferred_element_type=F32), pair, local)
            for quad in range(2):
                wait_bytes(rs_recv0.at[p - 1, pl.ds(0, n_blk - 1)], ag_send.at[p - 1, quad])
            turn_modes()

        @pl.when(p == 2)
        def _():
            norm = cross = jnp.zeros((8, 1), F32)
            for quad in range(2):
                for held in (live, dead):
                    norm = norm + lane_sum(held[1, quad] * held[1, quad])
                    cross = cross + lane_sum(held[1, quad] * held[2, quad])
            scalar[...] = put_scalars(by_realization(norm) + by_realization(cross))

        for d in range(n_order):
            send[d] = jnp.where(row8 < cycles, turned[cycles * d:cycles * d + 8, :], scalar[...])
        exchange_start(2 * p)

        @pl.when(p == 0)
        def _():
            build_table()

            def turn_table(t, inner_carry):
                at = pl.ds(pl.multiple_of(t * 256, 256), 256)
                table_turned[at, :] = table[:, at].T
                return inner_carry

            lax.fori_loop(0, half_turn // 256, turn_table, 0)

        exchange_wait(2 * p)

        @pl.when(p == 2)
        def _():
            total = sum_tiles(lambda s: recv[2 * p, s], n_order)
            norm, cross = pair_at(total, 7, 0), pair_at(total, 7, 2)
            ratio = [norm[0] / cross[0], norm[1] / cross[1]]
            step = rows_from(ratio)
            steps[0] = jnp.broadcast_to(rows_from(norm), (8, 128))
            steps[1] = jnp.broadcast_to(step, (8, 128))
            steps[2] = jnp.broadcast_to(ratio[0], (8, 128))
            steps[3] = jnp.broadcast_to(ratio[1], (8, 128))
            sums = [jnp.zeros((8, 1), F32)] * 4
            for quad in range(2):
                for r1, held, inv in ((r1_live, live, prior_live), (r1_dead, dead, prior_dead)):
                    before = held[1, quad]
                    after = before - step * held[2, quad]
                    r1[quad] = after
                    scaled = inv[quad] * after
                    sums = [total + lane_sum(value) for total, value in zip(
                        sums, (after * after, scaled * after, scaled * before, inv[quad] * before * before))]
            scalar[...] = put_scalars([value for total in sums for value in by_realization(total)])

        def shuffle(g, inner_carry):
            lanes = pl.ds(g * 128, 128)
            flip = sign[:, lanes]
            held = [recv[2 * p, g * 8 + i] for i in range(8)]
            straight = []
            for hr in range(4):
                acc = held[0] if hr == 0 else pltpu.roll(held[0], (128 - 16 * hr) % 128, 1)
                for i in range(1, 8):
                    by = (16 * i - 16 * hr) % 128
                    moved = held[i] if by == 0 else pltpu.roll(held[i], by, 1)
                    acc = jnp.where(group8 == i, moved, acc)
                straight.append(acc)
            flipped = [acc * flip for acc in straight]
            rows = jnp.concatenate(straight + flipped, axis=0)
            high, rest = split_bf16(rows)
            flhs[0:64, lanes] = high
            flhs[64:128, lanes] = rest
            return inner_carry

        for g in range(groups):
            shuffle(g, 0)

        anal[...] = jnp.zeros_like(anal)
        chunk = min(3072, half_turn)

        def fourier(t, inner_carry):
            lanes = pl.ds(pl.multiple_of(t * chunk, 128), chunk)
            block = table[:, lanes]
            sky = jnp.dot(flhs[...], block, preferred_element_type=F32)
            sky = sky[0:64] + sky[64:128]
            scaled = sky * weight[:, :, lanes].reshape(64, chunk)
            high, rest = split_bf16(scaled)
            both = jnp.concatenate([high, rest], axis=0)

            out = jnp.dot(both, table_turned[lanes, :], preferred_element_type=F32)
            anal[...] += out[0:64] + out[64:128]

            @pl.when(p == 1)
            def _():
                sky_kept[:, lanes] = sky

            @pl.when(p == 2)
            def _():
                for hr in range(8):
                    rows = slice(8 * hr, 8 * hr + 8)
                    before = sky_kept[rows, lanes]
                    after = before - steps[2 + hr % 2][:, 0:1] * sky[rows]
                    weighed = weight[hr, :, lanes]
                    heavy = weighed * after
                    for at, value in enumerate((heavy * after, heavy * before, weighed * before * before)):
                        total = pixel_sums[2 * at + hr % 2]
                        for k in range(chunk // 128):
                            total = total + value[:, 128 * k:128 * k + 128]
                        pixel_sums[2 * at + hr % 2] = total

            return inner_carry

        lax.fori_loop(0, half_turn // chunk, fourier, 0)

        @pl.when(p == 2)
        def _():
            tile = scalar[...]
            for at in range(6):
                value = jnp.sum(lane_sum(pixel_sums[at]), axis=0, keepdims=True)
                tile = jnp.where(item8 == 8 + at, value, tile)
            scalar[...] = tile

        def shuffle_back(g, inner_carry):
            lanes = pl.ds(g * 128, 128)
            flip = sign[:, lanes]
            rows = [anal[8 * hr:8 * hr + 8, lanes] + flip * anal[32 + 8 * hr:40 + 8 * hr, lanes] for hr in range(4)]
            base = scalar[...]
            for i in range(8):
                acc = jnp.zeros((8, 128), F32)
                for hr in range(4):
                    by = (16 * hr - 16 * i) % 128
                    moved = rows[hr] if by == 0 else pltpu.roll(rows[hr], by, 1)
                    acc = jnp.where(group8 == hr, moved, acc)
                send[g * 8 + i] = jnp.where(row8 < cycles, acc, base)
            return inner_carry

        for g in range(groups):
            shuffle_back(g, 0)
        exchange_start(2 * p + 1)

        @pl.when(p == 0)
        def _():
            load_copy(1).wait()
            split_vector(rhs, rhs_live, rhs_dead)

            def turn_leg(pair, inner_carry):
                for t in range(width // lane_step):
                    at = slice(t * lane_step, t * lane_step + lane_step)
                    leg_turned[pair, at, :] = leg[pair, :, at].T
                return inner_carry

            lax.fori_loop(0, 4, turn_leg, 0)

        for quad in range(2):
            image = prior_dead[quad] * dead[p, quad]
            dead[p + 1, quad] = jnp.where(p == 0, rhs_dead[quad] - image, image)
        exchange_wait(2 * p + 1)

        for d in range(n_order):
            turned[cycles * d:cycles * d + cycles, :] = recv[2 * p + 1, d, 0:cycles, :]
        for sheet in range(sheets):
            back[sheet] = turned[128 * sheet:128 * sheet + 128, :].T

        for quad in range(2):
            for half in range(2):
                pair = 2 * quad + half
                rows = jnp.concatenate([
                    jnp.concatenate([back[sheet, pl.ds(2 * pair + slot, 8, stride=8), :] for sheet in range(sheets)],
                                    axis=1)
                    for slot in range(2)], axis=0)
                high, rest = split_bf16(rows[:, 0:local])
                both = jnp.concatenate([high, rest], axis=0)
                mine_rows = slice(4 * half, 4 * half + 4)
                one_row = slice(4 * half, 4 * half + 1)

                def analyse(t, inner_carry):
                    at = pl.ds(t * 2 * part, 2 * part)
                    out = jnp.dot(both, leg[pair, :, at], preferred_element_type=F32)
                    out = out[0:16] + out[16:32]
                    kept = jnp.where(mask[quad, one_row, at] > 0.5, out[0:8], out[8:16])
                    value = kept[0:4] + parity[quad, one_row, at] * kept[4:8]
                    partial[quad, 2 * t, mine_rows, 0:part] = value[:, 0:part]
                    partial[quad, 2 * t + 1, mine_rows, 0:part] = value[:, part:2 * part]
                    return inner_carry

                for t in range(n_blk // 2):
                    analyse(t, 0)
                out = jnp.dot(both, leg[pair, :, degrees:degrees + 128], preferred_element_type=F32)
                out = out[0:16] + out[16:32]
                extras[quad, mine_rows, :] = out[8:12] + out[12:16]
            if quad == 1:
                total = sum_tiles(lambda s: recv[2 * p + 1, s], n_order)
                tile = jnp.where(lane8 == 0, extras[0], 0.0)
                tile = jnp.where(lane8 == 1, pltpu.roll(extras[1], 1, 1), tile)
                scalar[...] = total
                tile = jnp.where((lane8 >= 64) & (row8 == 7), total, tile)
                for b in range(n_blk):
                    partial[1, b, :, part:part + 128] = tile
            for to in partners:
                source = partial.at[0, to, :, pl.ds(0, part)] if quad == 0 else partial.at[1, to]
                target = rs_recv0 if quad == 0 else rs_recv1
                pltpu.make_async_remote_copy(
                    src_ref=source, dst_ref=target.at[p, mine],
                    send_sem=rs_send.at[p, quad], recv_sem=rs_arrive.at[p, quad],
                    device_id=(me, to), device_id_type=MESH).start()

        my_lanes = pl.ds(pl.multiple_of(mine * part, 128), part)
        for quad in range(2):
            arrived = rs_recv0 if quad == 0 else rs_recv1
            arrived[p, mine] = partial[quad, mine, :, 0:arrived.shape[3]]
            wait_bytes(arrived.at[p, pl.ds(0, n_blk - 1)], rs_arrive.at[p, quad])
            total = sum_tiles(lambda b: arrived[p, b], n_blk)
            shard[quad] = total[:, 0:part]
            for to in partners:
                pltpu.make_async_remote_copy(
                    src_ref=shard.at[quad], dst_ref=summed.at[p, quad, :, my_lanes],
                    send_sem=ag_send.at[p, quad], recv_sem=ag_arrive.at[p, quad],
                    device_id=(me, to), device_id_type=MESH).start()
            summed[p, quad, :, my_lanes] = total[:, 0:part]
            wait_bytes(arrived.at[p, pl.ds(0, n_blk - 1)], rs_send.at[p, quad])
        tile = total[:, part:part + 128]
        extra_sum[0] = jnp.where(lane8 == 0, tile, 0.0)
        extra_sum[1] = jnp.where(lane8 == 0, pltpu.roll(tile, 127, 1), 0.0)
        extra_sum[2] = tile
        return carry

    lax.fori_loop(0, 3, application, 0)

    within_order, over_all = scalar[...], extra_sum[2]
    norm = [steps[0, 0:1, 0:1], steps[0, 2:3, 0:1]]
    ratios, seconds = [], []
    for r in range(2):
        after = scalar_at(within_order, 7, r)
        ratio = after / norm[r]
        curve = (scalar_at(within_order, 7, 2 + r) + scalar_at(over_all, 7, 8 + r)
                 + 2.0 * ratio * (scalar_at(within_order, 7, 4 + r) + scalar_at(over_all, 7, 10 + r))
                 + ratio * ratio * (scalar_at(within_order, 7, 6 + r) + scalar_at(over_all, 7, 12 + r)))
        ratios.append(ratio)
        seconds.append(after / curve)
    ratio, second = rows_from(ratios), rows_from(seconds)
    step = steps[1, :, 0:1]

    def finish(quad, lanes, held, r1, last, x_out, r_out):
        before, middle = held[1, quad, :, lanes], held[2, quad, :, lanes]
        after = r1[quad, :, lanes]
        direction = after + ratio * before
        image = (1.0 + ratio) * middle - step * last
        x_out[quad, :, lanes] = held[0, quad, :, lanes] + step * before + second * direction
        r_out[quad, :, lanes] = after - second * image

    main, tail = pl.ds(0, degrees), pl.ds(degrees, 128)
    for quad in range(2):
        finish(quad, main, dead, r1_dead, dead[3, quad], x_out_dead, r_out_dead)
        last = prior_live[quad, :, tail] * live[2, quad, :, tail] + extra_sum[quad]
        finish(quad, tail, live, r1_live, last, x_out_live, r_out_live)
    for quad in range(2):
        wait_bytes(rs_recv0.at[2, pl.ds(0, n_blk - 1)], ag_arrive.at[2, quad])
        last = prior_live[quad, :, main] * live[2, quad, :, main] + summed[2, quad]
        finish(quad, main, live, r1_live, last, x_out_live, r_out_live)
    for quad in range(2):
        wait_bytes(rs_recv0.at[2, pl.ds(0, n_blk - 1)], ag_send.at[2, quad])


def per_device(n_order, n_blk, right_side, start_guess, legendre, orders, prior_inv, noise_inv, pixel_flags):
    slots, local, degrees = legendre.shape
    cycles, pixels = noise_inv.shape[1], noise_inv.shape[2]
    width = degrees + 128
    part = degrees // n_blk
    smem = pl.BlockSpec(memory_space=pltpu.SMEM)
    vmem = pl.BlockSpec(memory_space=pltpu.VMEM)
    hbm = pl.BlockSpec(memory_space=pl.ANY)
    live_shape = jax.ShapeDtypeStruct((2, 8, width), F32)
    dead_shape = jax.ShapeDtypeStruct((2, 8, degrees), F32)
    columns = 16 * n_order
    sheets = -(-(local + 8) // 128)
    half_turn = pixels // 2
    scratch = [pltpu.VMEM((2, local, degrees), BF16)] * 4 + [
        pltpu.VMEM((8, 128), jnp.int32),
        pltpu.VMEM(right_side.shape, F32),
        pltpu.VMEM(right_side.shape, F32),
        pltpu.VMEM((2, 8, degrees), F32),
        pltpu.VMEM((2, 8, degrees), F32),
        pltpu.VMEM((4, local, width), BF16),
        pltpu.VMEM((4, width, local), BF16),
        pltpu.VMEM((3, 2, 8, width), F32),
        pltpu.VMEM((4, 2, 8, degrees), F32),
        pltpu.VMEM((2, 8, width), F32),
        pltpu.VMEM((2, 8, degrees), F32),
        pltpu.VMEM((2, 8, width), F32),
        pltpu.VMEM((2, 8, degrees), F32),
        pltpu.VMEM((2, 8, width), F32),
        pltpu.VMEM((2, 8, width), F32),
        pltpu.VMEM((cycles, 2, pixels), F32),
        pltpu.VMEM((cycles, 2, pixels), jnp.int32),
        pltpu.VMEM((2, 64, width), BF16),
        pltpu.VMEM((sheets, 128, 128), F32),
        pltpu.VMEM((sheets * 128, 128), F32),
        pltpu.VMEM((sheets, 128, 128), F32),
        pltpu.VMEM((n_order, 8, 128), F32),
        pltpu.VMEM((6, n_order, 8, 128), F32),
        pltpu.VMEM((n_order, 8, 128), jnp.int32),
        pltpu.VMEM((8, 128), F32),
        pltpu.VMEM((128, columns), BF16),
        pltpu.VMEM((8, 8, half_turn), F32),
        pltpu.VMEM((64, columns), F32),
        pltpu.VMEM((8, columns), F32),
        pltpu.VMEM((n_order, 2, 8, 128), F32),
        pltpu.VMEM((n_order, 2, 8, 128), F32),
        pltpu.VMEM((columns, half_turn), BF16),
        pltpu.VMEM((half_turn, columns), BF16),
        pltpu.VMEM((64, half_turn), F32),
        pltpu.VMEM((6, 8, 128), F32),
        pltpu.VMEM((2, n_blk, 8, part + 128), F32),
        pltpu.VMEM((2, 8, 128), F32),
        pltpu.VMEM((2, 8, part), F32),
        pltpu.VMEM((3, n_blk, 8, part), F32),
        pltpu.VMEM((3, n_blk, 8, part + 128), F32),
        pltpu.VMEM((3, 2, 8, degrees), F32),
        pltpu.VMEM((3, 8, 128), F32),
        pltpu.VMEM((2, 8, width), F32),
        pltpu.VMEM((2, 8, degrees), F32),
        pltpu.VMEM((4, 8, 128), F32),
        pltpu.SemaphoreType.DMA((4,)),
        pltpu.SemaphoreType.DMA((4,)),
        pltpu.SemaphoreType.DMA((2,)),
        pltpu.SemaphoreType.DMA((6,)),
        pltpu.SemaphoreType.DMA((6,)),
        pltpu.SemaphoreType.DMA((3, 2)),
        pltpu.SemaphoreType.DMA((3, 2)),
        pltpu.SemaphoreType.DMA((3, 2)),
        pltpu.SemaphoreType.DMA((3, 2)),
    ]
    results = pl.pallas_call(
        functools.partial(main_kernel, n_order, n_blk, degrees, cycles, pixels),
        in_specs=[smem, hbm, hbm, hbm, vmem, hbm, hbm],
        out_specs=[vmem] * 4,
        out_shape=[live_shape, dead_shape, live_shape, dead_shape],
        scratch_shapes=scratch,
        compiler_params=pltpu.CompilerParams(
            collective_id=0, has_side_effects=True, vmem_limit_bytes=VMEM_LIMIT),
        name="steps",
    )(orders, legendre, start_guess, right_side, prior_inv.reshape(1, degrees),
      noise_inv.transpose(1, 0, 2), pixel_flags.transpose(1, 0, 2))

    full = jax.ShapeDtypeStruct(right_side.shape, F32)
    return tuple(pl.pallas_call(
        functools.partial(unpack_kernel, degrees),
        in_specs=[smem] + [vmem] * 4,
        out_specs=[vmem] * 2,
        out_shape=[full, full],
        scratch_shapes=[pltpu.VMEM((2, 8, degrees), F32)] * 2,
        compiler_params=pltpu.CompilerParams(vmem_limit_bytes=VMEM_LIMIT),
        name="unpack",
    )(orders, *results))


def solution(mesh):
    in_specs = (
        P(None, None, "order", None),
        P(None, None, "order", None),
        P("order", "blk", None),
        P("order"),
        P(),
        P(None, ("blk", "order"), None),
        P(None, ("blk", "order"), None),
    )
    out_specs = (P(None, None, "order", None), P(None, None, "order", None))
    body = functools.partial(per_device, mesh.shape["order"], mesh.shape["blk"])
    return jax.shard_map(body, mesh=mesh, in_specs=in_specs, out_specs=out_specs, check_vma=False)
```

```python
import functools

import jax
import jax.numpy as jnp
from jax import lax
from jax.experimental import pallas as pl
from jax.experimental.pallas import tpu as pltpu
from jax.sharding import PartitionSpec as P

MESH = pl.DeviceIdType.MESH
F32 = jnp.float32
BF16 = jnp.bfloat16
VMEM_LIMIT = 56 * 1024 * 1024
NT = (((1,), (1,)), ((), ()))


def iota(shape, dim):
    return lax.broadcasted_iota(jnp.int32, shape, dim)


def tile_lanes(t, shift, less, tiles):
    at = lax.rem(t - shift // 128 - less + 2 * tiles, tiles) * 128
    return pl.ds(pl.multiple_of(at, 128), 128)


def rolled_tiles(load, shift, tiles, lane):
    within = lax.rem(shift, 128)
    before = pltpu.roll(load(tile_lanes(0, shift, 1, tiles)), within, 1)
    for t in range(tiles):
        now = pltpu.roll(load(tile_lanes(t, shift, 0, tiles)), within, 1)
        yield jnp.where(lane >= within, now, before)
        before = now


def rotate_tiles(tiles, whole):
    count = len(tiles)
    for bit in range((count - 1).bit_length()):
        moved = (whole & (1 << bit)) != 0
        tiles = [jnp.where(moved, tiles[(t - (1 << bit)) % count], tiles[t]) for t in range(count)]
    return tiles


def lane_shift(value, within):
    return pltpu.roll(value, within, 1)


def split_rows(value, first, flip):
    high = value.astype(BF16).astype(F32)
    pieces = []
    for piece in (high, value - high):
        for keep in (first, 1.0 - first):
            kept = piece * keep
            pieces.append(kept)
            pieces.append(kept * flip)
    return jnp.concatenate(pieces, axis=0).astype(BF16)


def place_modes(modes, out, pair, local):
    sheets = modes.shape[0]
    at = 4 * (pair % 2)
    out = out[0:32] + out[32:64]
    for slot in range(2):
        rows = jnp.concatenate([out[16 * slot + at:16 * slot + at + 4],
                                out[16 * slot + 8 + at:16 * slot + 8 + at + 4]], axis=0)
        if sheets * 128 > local:
            rows = jnp.concatenate([rows, jnp.zeros((8, sheets * 128 - local), F32)], axis=1)
        for sheet in range(sheets):
            modes[sheet, pl.ds(2 * pair + slot, 8, stride=8), :] = rows[:, 128 * sheet:128 * sheet + 128]


def unpack_kernel(degrees, orders, x_live, x_dead, r_live, r_dead, x_out, r_out, rows_a, rows_b):
    tiles = degrees // 128
    lane8 = iota((8, 128), 1)
    upper = iota((8, 128), 0) < 4
    for quad in range(2):
        low, high = orders[4 * quad], orders[4 * quad + 2]
        shifts = jnp.where(upper, low, high)
        back_low, back_high = lax.rem(degrees - low, degrees), lax.rem(degrees - high, degrees)
        for at, (live, dead, out) in enumerate(((x_live, x_dead, x_out), (r_live, r_dead, r_out))):
            for t in range(tiles):
                lanes = slice(t * 128, t * 128 + 128)
                own = lane8 + t * 128 >= shifts
                alive, idle = live[quad, :, lanes], dead[quad, :, lanes]
                rows_a[at, :, lanes] = jnp.where(own, alive, idle)
                second = jnp.where(own, idle, alive)
                if t == tiles - 1:
                    extra = live[quad, :, degrees:degrees + 128]
                    second = jnp.where(lane8 == 127, pltpu.roll(extra, 127, 1), second)
                rows_b[at, :, lanes] = second
            load = lambda lanes: rows_b[at, :, lanes]
            back = zip(rolled_tiles(load, back_low, tiles, lane8), rolled_tiles(load, back_high, tiles, lane8))
            kept = [jnp.where(upper, one, two) for one, two in back]
            for t, value in enumerate(kept):
                rows_b[at, :, t * 128:t * 128 + 128] = value
            for half in range(2):
                slot = 4 * quad + 2 * half
                for r in range(2):
                    for c in range(2):
                        row = half * 4 + r * 2 + c
                        out[r, c, slot:slot + 1, :] = rows_a[at, row:row + 1, :]
                        out[r, c, slot + 1:slot + 2, :] = rows_b[at, row:row + 1, :]


def split_bf16(values):
    high = values.astype(BF16)
    return high, (values - high.astype(F32)).astype(BF16)


def main_kernel(n_order, n_blk, degrees, cycles, pixels,
                orders, leg_hbm, guess_hbm, rhs_hbm, prior, noise_hbm, flags_hbm,
                x_out_live, x_out_dead, r_out_live, r_out_dead,
                raw0, raw1, raw2, raw3, own_orders, guess, rhs, rows_a, rows_b,
                leg, leg_turned, live, dead, rhs_live, rhs_dead, prior_live, prior_dead, mask, parity, noise, flags,
                lhs, modes, turned, back, send, recv, order_recv, scalar,
                flhs, weight, anal, sign, current, turn, table, table_turned, sky_kept, pixel_sums,
                partial, extras, shard, rs_recv0, rs_recv1, summed, extra_sum,
                r1_live, r1_dead, steps,
                leg_sems, load_sems, order_sems, a2a_send, a2a_recv, rs_send, rs_arrive, ag_send, ag_arrive):
    me = lax.axis_index("order")
    mine = lax.axis_index("blk")
    tiles = degrees // 128
    half_turn = pixels // 2
    columns = 16 * n_order
    groups = columns // 128
    local = cycles * n_order
    part = degrees // n_blk
    sheets = modes.shape[0]

    raws = (raw0, raw1, raw2, raw3)

    def leg_copy(pair):
        return pltpu.make_async_copy(leg_hbm.at[pl.ds(2 * pair, 2)], raws[pair], leg_sems.at[pair])

    def load_copy(at):
        source, target = ((guess_hbm, guess), (rhs_hbm, rhs), (noise_hbm, noise), (flags_hbm, flags))[at]
        return pltpu.make_async_copy(source, target, load_sems.at[at])

    for at in (0, 2, 3):
        load_copy(at).start()
    for pair in range(4):
        leg_copy(pair).start()

    side_x = 2
    side_y = n_order // 4
    if n_order == 32:
        side_x, side_y = 4, 4
    offsets = [(a, b, c) for a in range(side_y) for b in range(side_x) for c in range(2) if a or b or c]
    offsets.sort(key=lambda o: -(2 * min(o[0], side_y - o[0]) + 2 * min(o[1], side_x - o[1]) + o[2]))
    my_y, my_x, my_c = me // (2 * side_x), (me // 2) % side_x, me % 2
    peers = [lax.rem(my_y + a, side_y) * (2 * side_x) + lax.rem(my_x + b, side_x) * 2 + lax.rem(my_c + c, 2)
             for a, b, c in offsets]
    steps_z = sorted(range(1, n_blk), key=lambda i: -min(i, n_blk - i))
    partners = [lax.rem(mine + i, n_blk) for i in steps_z]

    barrier = pltpu.get_barrier_semaphore()
    for to in peers:
        pl.semaphore_signal(barrier, inc=1, device_id=(to, mine), device_id_type=MESH)
    for to in partners:
        pl.semaphore_signal(barrier, inc=1, device_id=(me, to), device_id_type=MESH)
    load_copy(1).start()

    def wait_bytes(ref, sem):
        pltpu.make_async_copy(ref, ref, sem).wait()

    row8 = iota((8, 128), 0)
    lane8 = iota((8, 128), 1)
    modes[...] = jnp.zeros_like(modes)
    turned[...] = jnp.zeros_like(turned)
    scalar[...] = jnp.zeros_like(scalar)
    pixel_sums[...] = jnp.zeros_like(pixel_sums)
    upper8 = row8 < 4
    lane16 = iota((16, 128), 1)
    zero16 = iota((16, 128), 0) * 0

    def shift_rows(quad):
        return jnp.where(upper8, orders[4 * quad], orders[4 * quad + 2])

    def rolled_rows(values, quad):
        shifts = shift_rows(quad)
        whole, within = shifts // 128, shifts % 128
        low, high = orders[4 * quad] % 128, orders[4 * quad + 2] % 128
        moved = [jnp.where(upper8, lane_shift(value, low), lane_shift(value, high))
                 for value in rotate_tiles(values, whole)]
        return [jnp.where(lane8 >= within, moved[t], moved[t - 1]) for t in range(tiles)]

    def split_vector(source, live_out, dead_out):
        for quad in range(2):
            for half in range(2):
                slot = 4 * quad + 2 * half
                for r in range(2):
                    for c in range(2):
                        row = half * 4 + r * 2 + c
                        rows_a[quad, row:row + 1, :] = source[r, c, slot:slot + 1, :]
                        rows_b[quad, row:row + 1, :] = source[r, c, slot + 1:slot + 2, :]
            shifts = shift_rows(quad)
            rolled = rolled_rows([rows_b[quad, :, t * 128:t * 128 + 128] for t in range(tiles)], quad)
            for t in range(tiles):
                lanes = slice(t * 128, t * 128 + 128)
                own = lane8 + t * 128 >= shifts
                first = rows_a[quad, :, lanes]
                idle = jnp.where(own, rolled[t], first)
                if t == tiles - 1:
                    idle = jnp.where(lane8 == 127, 0.0, idle)
                live_out[quad, :, lanes] = jnp.where(own, first, rolled[t])
                dead_out[quad, :, lanes] = idle
            live_out[quad, :, degrees:degrees + 128] = jnp.where(lane8 == 0, pltpu.roll(rolled[-1], 1, 1), 0.0)

    def split_prior():
        for quad in range(2):
            shifts = shift_rows(quad)
            firsts = [jnp.broadcast_to(prior[:, t * 128:t * 128 + 128], (8, 128)) for t in range(tiles)]
            rolled = rolled_rows(firsts, quad)
            for t in range(tiles):
                lanes = slice(t * 128, t * 128 + 128)
                own = lane8 + t * 128 >= shifts
                prior_live[quad, :, lanes] = jnp.where(own, firsts[t], rolled[t])
                prior_dead[quad, :, lanes] = jnp.where(own, rolled[t], firsts[t])
            prior_live[quad, :, degrees:degrees + 128] = jnp.where(lane8 == 0, pltpu.roll(rolled[-1], 1, 1), 0.0)

    def fill_masks():
        for quad in range(2):
            shifts = shift_rows(quad)
            number_b = jnp.where(upper8, orders[4 * quad + 1], orders[4 * quad + 3])
            for t in range(tiles):
                lanes = slice(t * 128, t * 128 + 128)
                place = lane8 + t * 128
                own = place >= shifts
                total = jnp.where(own, place + shifts, place - shifts + degrees + number_b)
                parity[quad, :, lanes] = (1 - 2 * (total & 1)).astype(F32)
                mask[quad, :, lanes] = own.astype(F32)
            parity[quad, :, degrees:degrees + 128] = jnp.ones((8, 128), F32)
            mask[quad, :, degrees:degrees + 128] = jnp.zeros((8, 128), F32)

    tile = jnp.zeros((8, 128), jnp.int32)
    for m in range(8):
        tile = jnp.where(row8 == m, orders[m], tile)
    own_orders[...] = tile
    def build_weight():
        weight[...] = jnp.zeros_like(weight)
        for j in range(cycles):
            value = noise[j] * flags[j].astype(F32)
            for h in range(2):
                for image in range(2):
                    row = value[h:h + 1, image * half_turn:(image + 1) * half_turn]
                    for r in range(2):
                        weight[image * 4 + h * 2 + r, j:j + 1, :] = row

    fill_masks()
    load_copy(0).wait()
    split_vector(guess, live.at[0], dead.at[0])
    split_prior()
    load_copy(2).wait()
    load_copy(3).wait()
    build_weight()

    width = degrees + 128
    lane_step = 128 * max(n for n in (5, 3, 1) if (tiles + 1) % n == 0)

    def build_rows(p, quad):
        for t in range(width // lane_step):
            at = pl.ds(t * lane_step, lane_step)
            lhs[quad, :, at] = split_rows(live[p, quad, :, at], mask[quad, :, at], parity[quad, :, at])

    def turn_modes():
        for sheet in range(sheets):
            turned[128 * sheet:128 * sheet + 128, :] = modes[sheet].T

    for quad in range(2):
        build_rows(0, quad)

    pl.semaphore_wait(barrier, n_order - 1 + n_blk - 1)

    for to in peers:
        pltpu.make_async_remote_copy(
            src_ref=own_orders, dst_ref=order_recv.at[me],
            send_sem=order_sems.at[0], recv_sem=order_sems.at[1],
            device_id=(to, mine), device_id_type=MESH).start()
    order_recv[me] = own_orders[...]

    for pair in range(4):
        leg_copy(pair).wait()
        raw = raws[pair]
        shift = orders[2 * pair]
        within = shift % 128
        whole = zero16 + shift // 128

        def pack_rows(step, carry):
            rows = pl.ds(pl.multiple_of(step * 16, 16), 16)
            moved = rotate_tiles([raw[1, rows, t * 128:t * 128 + 128] for t in range(tiles)], whole)
            moved = [lane_shift(value, within) for value in moved]
            for t in range(tiles):
                rolled = jnp.where(lane16 >= within, moved[t], moved[t - 1])
                first = raw[0, rows, t * 128:t * 128 + 128]
                leg[pair, rows, t * 128:t * 128 + 128] = jnp.where(lane16 + t * 128 >= shift, first, rolled)
            extra = jnp.where(lane16 == 0, pltpu.roll(rolled, 1, 1), jnp.zeros_like(rolled))
            leg[pair, rows, degrees:degrees + 128] = extra
            return carry

        lax.fori_loop(0, local // 16, pack_rows, 0, unroll=4 if local % 64 == 0 else 1)
        place_modes(modes, lax.dot_general(lhs[pair // 2], leg[pair], NT, preferred_element_type=F32), pair, local)

    turn_modes()

    def exchange_start(step):
        for to in peers:
            pltpu.make_async_remote_copy(
                src_ref=send.at[to], dst_ref=recv.at[step, me],
                send_sem=a2a_send.at[step], recv_sem=a2a_recv.at[step],
                device_id=(to, mine), device_id_type=MESH).start()
        recv[step, me] = send[me]

    def exchange_wait(step):
        wait_bytes(recv.at[step, pl.ds(0, n_order - 1)], a2a_recv.at[step])
        wait_bytes(send.at[pl.ds(0, n_order - 1)], a2a_send.at[step])

    def build_table():
        wait_bytes(order_recv.at[pl.ds(0, n_order - 1)], order_sems.at[1])
        wait_bytes(order_recv.at[pl.ds(0, n_order - 1)], order_sems.at[0])
        number = order_recv[...]
        lane = iota((n_order, 8, 128), 2)
        scale = jnp.where(number == 0, 1.0, 2.0) * (pixels ** -0.5)

        def angle(product):
            value = product.astype(F32)
            value = value - pixels * jnp.floor(value * (1.0 / pixels))
            return value * (2.0 * jnp.pi / pixels)

        base = angle(number * lane)
        current[:, 0] = scale * jnp.cos(base)
        current[:, 1] = -scale * jnp.sin(base)
        step = angle(number * 128)
        turn[:, 0] = jnp.cos(step)
        turn[:, 1] = jnp.sin(step)
        odd = (1 - 2 * (number & 1)).astype(F32)
        sign_rows = jnp.concatenate([odd, odd], axis=1).reshape(columns, 128)
        sign[...] = sign_rows.T[0:8]

        def some(piece, inner):
            held = []
            for k in range(8):
                s = piece * 8 + k
                held.append((current[s, 0], current[s, 1], turn[s, 0], turn[s, 1]))
            for q in range(half_turn // 128):
                for k in range(8):
                    cosine, sine, turn_c, turn_s = held[k]
                    rows = pl.ds(pl.multiple_of((piece * 8 + k) * 16, 16), 16)
                    table[rows, q * 128:q * 128 + 128] = jnp.concatenate([cosine, sine], axis=0).astype(BF16)
                    held[k] = (cosine * turn_c + sine * turn_s, sine * turn_c - cosine * turn_s, turn_c, turn_s)
            return inner

        lax.fori_loop(0, n_order // 8, some, 0)

    group8 = lane8 // 16
    item8 = lane8 // 8
    first_row8 = (iota((8, 1), 0) % 4) < 2

    def by_realization(total):
        zero = jnp.sum(jnp.where(first_row8, total, 0.0), axis=0, keepdims=True)
        one = jnp.sum(jnp.where(first_row8, 0.0, total), axis=0, keepdims=True)
        return [zero, one]

    def lane_sum(value):
        return jnp.sum(value, axis=1, keepdims=True)

    def put_scalars(values):
        tile = jnp.zeros((8, 128), F32)
        for at, value in enumerate(values):
            tile = jnp.where(item8 == at, value, tile)
        return tile

    def sum_tiles(load, count):
        values = [load(s) for s in range(count)]
        while len(values) > 1:
            values = [a + b for a, b in zip(values[::2], values[1::2])]
        return values[0]

    def scalar_at(total, row, at):
        return total[row:row + 1, 8 * at:8 * at + 1]

    def rows_from(pair):
        return jnp.where(first_row8, pair[0], pair[1])

    def pair_at(total, row, at):
        return [scalar_at(total, row, at), scalar_at(total, row, at + 1)]


    def application(p, carry):
        @pl.when(p > 0)
        def _():
            for quad in range(2):
                wait_bytes(rs_recv0.at[p - 1, pl.ds(0, n_blk - 1)], ag_arrive.at[p - 1, quad])
                main = pl.ds(0, degrees)
                image = prior_live[quad, :, main] * live[p - 1, quad, :, main] + summed[p - 1, quad]
                live[p, quad, :, main] = jnp.where(p == 1, rhs_live[quad, :, main] - image, image)
                tail = pl.ds(degrees, 128)
                image = prior_live[quad, :, tail] * live[p - 1, quad, :, tail] + extra_sum[quad]
                live[p, quad, :, tail] = jnp.where(p == 1, rhs_live[quad, :, tail] - image, image)
                build_rows(p, quad)
                for half in range(2):
                    pair = 2 * quad + half
                    place_modes(modes, jnp.dot(lhs[quad], leg_turned[pair], preferred_element_type=F32), pair, local)
            for quad in range(2):
                wait_bytes(rs_recv0.at[p - 1, pl.ds(0, n_blk - 1)], ag_send.at[p - 1, quad])
            turn_modes()

        @pl.when(p == 2)
        def _():
            norm = cross = jnp.zeros((8, 1), F32)
            for quad in range(2):
                for held in (live, dead):
                    norm = norm + lane_sum(held[1, quad] * held[1, quad])
                    cross = cross + lane_sum(held[1, quad] * held[2, quad])
            scalar[...] = put_scalars(by_realization(norm) + by_realization(cross))

        for d in range(n_order):
            send[d] = jnp.where(row8 < cycles, turned[cycles * d:cycles * d + 8, :], scalar[...])
        exchange_start(2 * p)

        @pl.when(p == 0)
        def _():
            build_table()

            def turn_table(t, inner_carry):
                at = pl.ds(pl.multiple_of(t * 256, 256), 256)
                table_turned[at, :] = table[:, at].T
                return inner_carry

            lax.fori_loop(0, half_turn // 256, turn_table, 0)

        exchange_wait(2 * p)

        @pl.when(p == 2)
        def _():
            total = sum_tiles(lambda s: recv[2 * p, s], n_order)
            norm, cross = pair_at(total, 7, 0), pair_at(total, 7, 2)
            ratio = [norm[0] / cross[0], norm[1] / cross[1]]
            step = rows_from(ratio)
            steps[0] = jnp.broadcast_to(rows_from(norm), (8, 128))
            steps[1] = jnp.broadcast_to(step, (8, 128))
            steps[2] = jnp.broadcast_to(ratio[0], (8, 128))
            steps[3] = jnp.broadcast_to(ratio[1], (8, 128))
            sums = [jnp.zeros((8, 1), F32)] * 4
            for quad in range(2):
                for r1, held, inv in ((r1_live, live, prior_live), (r1_dead, dead, prior_dead)):
                    before = held[1, quad]
                    after = before - step * held[2, quad]
                    r1[quad] = after
                    scaled = inv[quad] * after
                    sums = [total + lane_sum(value) for total, value in zip(
                        sums, (after * after, scaled * after, scaled * before, inv[quad] * before * before))]
            scalar[...] = put_scalars([value for total in sums for value in by_realization(total)])

        def shuffle(g, inner_carry):
            lanes = pl.ds(g * 128, 128)
            flip = sign[:, lanes]
            held = [recv[2 * p, g * 8 + i] for i in range(8)]
            straight = []
            for hr in range(4):
                acc = held[0] if hr == 0 else pltpu.roll(held[0], (128 - 16 * hr) % 128, 1)
                for i in range(1, 8):
                    by = (16 * i - 16 * hr) % 128
                    moved = held[i] if by == 0 else pltpu.roll(held[i], by, 1)
                    acc = jnp.where(group8 == i, moved, acc)
                straight.append(acc)
            flipped = [acc * flip for acc in straight]
            rows = jnp.concatenate(straight + flipped, axis=0)
            high, rest = split_bf16(rows)
            flhs[0:64, lanes] = high
            flhs[64:128, lanes] = rest
            return inner_carry

        for g in range(groups):
            shuffle(g, 0)

        anal[...] = jnp.zeros_like(anal)
        chunk = min(3072, half_turn)

        def fourier(t, inner_carry):
            lanes = pl.ds(pl.multiple_of(t * chunk, 128), chunk)
            block = table[:, lanes]
            sky = jnp.dot(flhs[...], block, preferred_element_type=F32)
            sky = sky[0:64] + sky[64:128]
            scaled = sky * weight[:, :, lanes].reshape(64, chunk)
            high, rest = split_bf16(scaled)
            both = jnp.concatenate([high, rest], axis=0)

            out = jnp.dot(both, table_turned[lanes, :], preferred_element_type=F32)
            anal[...] += out[0:64] + out[64:128]

            @pl.when(p == 1)
            def _():
                sky_kept[:, lanes] = sky

            @pl.when(p == 2)
            def _():
                for hr in range(8):
                    rows = slice(8 * hr, 8 * hr + 8)
                    before = sky_kept[rows, lanes]
                    after = before - steps[2 + hr % 2][:, 0:1] * sky[rows]
                    weighed = weight[hr, :, lanes]
                    heavy = weighed * after
                    for at, value in enumerate((heavy * after, heavy * before, weighed * before * before)):
                        total = pixel_sums[2 * at + hr % 2]
                        for k in range(chunk // 128):
                            total = total + value[:, 128 * k:128 * k + 128]
                        pixel_sums[2 * at + hr % 2] = total

            return inner_carry

        lax.fori_loop(0, half_turn // chunk, fourier, 0)

        @pl.when(p == 2)
        def _():
            tile = scalar[...]
            for at in range(6):
                value = jnp.sum(lane_sum(pixel_sums[at]), axis=0, keepdims=True)
                tile = jnp.where(item8 == 8 + at, value, tile)
            scalar[...] = tile

        def shuffle_back(g, inner_carry):
            lanes = pl.ds(g * 128, 128)
            flip = sign[:, lanes]
            rows = [anal[8 * hr:8 * hr + 8, lanes] + flip * anal[32 + 8 * hr:40 + 8 * hr, lanes] for hr in range(4)]
            base = scalar[...]
            for i in range(8):
                acc = jnp.zeros((8, 128), F32)
                for hr in range(4):
                    by = (16 * hr - 16 * i) % 128
                    moved = rows[hr] if by == 0 else pltpu.roll(rows[hr], by, 1)
                    acc = jnp.where(group8 == hr, moved, acc)
                send[g * 8 + i] = jnp.where(row8 < cycles, acc, base)
            return inner_carry

        for g in range(groups):
            shuffle_back(g, 0)
        exchange_start(2 * p + 1)

        @pl.when(p == 0)
        def _():
            load_copy(1).wait()
            split_vector(rhs, rhs_live, rhs_dead)

            def turn_leg(pair, inner_carry):
                for t in range(width // lane_step):
                    at = slice(t * lane_step, t * lane_step + lane_step)
                    leg_turned[pair, at, :] = leg[pair, :, at].T
                return inner_carry

            lax.fori_loop(0, 4, turn_leg, 0)

        for quad in range(2):
            image = prior_dead[quad] * dead[p, quad]
            dead[p + 1, quad] = jnp.where(p == 0, rhs_dead[quad] - image, image)
        exchange_wait(2 * p + 1)

        for d in range(n_order):
            turned[cycles * d:cycles * d + cycles, :] = recv[2 * p + 1, d, 0:cycles, :]
        for sheet in range(sheets):
            back[sheet] = turned[128 * sheet:128 * sheet + 128, :].T

        for quad in range(2):
            for half in range(2):
                pair = 2 * quad + half
                rows = jnp.concatenate([
                    jnp.concatenate([back[sheet, pl.ds(2 * pair + slot, 8, stride=8), :] for sheet in range(sheets)],
                                    axis=1)
                    for slot in range(2)], axis=0)
                high, rest = split_bf16(rows[:, 0:local])
                both = jnp.concatenate([high, rest], axis=0)
                mine_rows = slice(4 * half, 4 * half + 4)
                one_row = slice(4 * half, 4 * half + 1)

                def analyse(t, inner_carry):
                    at = pl.ds(t * 2 * part, 2 * part)
                    out = jnp.dot(both, leg[pair, :, at], preferred_element_type=F32)
                    out = out[0:16] + out[16:32]
                    kept = jnp.where(mask[quad, one_row, at] > 0.5, out[0:8], out[8:16])
                    value = kept[0:4] + parity[quad, one_row, at] * kept[4:8]
                    partial[quad, 2 * t, mine_rows, 0:part] = value[:, 0:part]
                    partial[quad, 2 * t + 1, mine_rows, 0:part] = value[:, part:2 * part]
                    return inner_carry

                for t in range(n_blk // 2):
                    analyse(t, 0)
                out = jnp.dot(both, leg[pair, :, degrees:degrees + 128], preferred_element_type=F32)
                out = out[0:16] + out[16:32]
                extras[quad, mine_rows, :] = out[8:12] + out[12:16]
            if quad == 1:
                total = sum_tiles(lambda s: recv[2 * p + 1, s], n_order)
                tile = jnp.where(lane8 == 0, extras[0], 0.0)
                tile = jnp.where(lane8 == 1, pltpu.roll(extras[1], 1, 1), tile)
                scalar[...] = total
                tile = jnp.where((lane8 >= 64) & (row8 == 7), total, tile)
                for b in range(n_blk):
                    partial[1, b, :, part:part + 128] = tile
            for to in partners:
                source = partial.at[0, to, :, pl.ds(0, part)] if quad == 0 else partial.at[1, to]
                target = rs_recv0 if quad == 0 else rs_recv1
                pltpu.make_async_remote_copy(
                    src_ref=source, dst_ref=target.at[p, mine],
                    send_sem=rs_send.at[p, quad], recv_sem=rs_arrive.at[p, quad],
                    device_id=(me, to), device_id_type=MESH).start()

        my_lanes = pl.ds(pl.multiple_of(mine * part, 128), part)
        for quad in range(2):
            arrived = rs_recv0 if quad == 0 else rs_recv1
            arrived[p, mine] = partial[quad, mine, :, 0:arrived.shape[3]]
            wait_bytes(arrived.at[p, pl.ds(0, n_blk - 1)], rs_arrive.at[p, quad])
            total = sum_tiles(lambda b: arrived[p, b], n_blk)
            shard[quad] = total[:, 0:part]
            for to in partners:
                pltpu.make_async_remote_copy(
                    src_ref=shard.at[quad], dst_ref=summed.at[p, quad, :, my_lanes],
                    send_sem=ag_send.at[p, quad], recv_sem=ag_arrive.at[p, quad],
                    device_id=(me, to), device_id_type=MESH).start()
            summed[p, quad, :, my_lanes] = total[:, 0:part]
            wait_bytes(arrived.at[p, pl.ds(0, n_blk - 1)], rs_send.at[p, quad])
        tile = total[:, part:part + 128]
        extra_sum[0] = jnp.where(lane8 == 0, tile, 0.0)
        extra_sum[1] = jnp.where(lane8 == 0, pltpu.roll(tile, 127, 1), 0.0)
        extra_sum[2] = tile
        return carry

    lax.fori_loop(0, 3, application, 0)

    within_order, over_all = scalar[...], extra_sum[2]
    norm = [steps[0, 0:1, 0:1], steps[0, 2:3, 0:1]]
    ratios, seconds = [], []
    for r in range(2):
        after = scalar_at(within_order, 7, r)
        ratio = after / norm[r]
        curve = (scalar_at(within_order, 7, 2 + r) + scalar_at(over_all, 7, 8 + r)
                 + 2.0 * ratio * (scalar_at(within_order, 7, 4 + r) + scalar_at(over_all, 7, 10 + r))
                 + ratio * ratio * (scalar_at(within_order, 7, 6 + r) + scalar_at(over_all, 7, 12 + r)))
        ratios.append(ratio)
        seconds.append(after / curve)
    ratio, second = rows_from(ratios), rows_from(seconds)
    step = steps[1, :, 0:1]

    def finish(quad, lanes, held, r1, last, x_out, r_out):
        before, middle = held[1, quad, :, lanes], held[2, quad, :, lanes]
        after = r1[quad, :, lanes]
        direction = after + ratio * before
        image = (1.0 + ratio) * middle - step * last
        x_out[quad, :, lanes] = held[0, quad, :, lanes] + step * before + second * direction
        r_out[quad, :, lanes] = after - second * image

    main, tail = pl.ds(0, degrees), pl.ds(degrees, 128)
    for quad in range(2):
        finish(quad, main, dead, r1_dead, dead[3, quad], x_out_dead, r_out_dead)
        last = prior_live[quad, :, tail] * live[2, quad, :, tail] + extra_sum[quad]
        finish(quad, tail, live, r1_live, last, x_out_live, r_out_live)
    for quad in range(2):
        finish(quad, main, live, r1_live, prior_live[quad, :, main] * live[2, quad, :, main], x_out_live, r_out_live)
    for quad in range(2):
        wait_bytes(rs_recv0.at[2, pl.ds(0, n_blk - 1)], ag_arrive.at[2, quad])
        r_out_live[quad, :, main] = r_out_live[quad, :, main] + (second * step) * summed[2, quad]
    for quad in range(2):
        wait_bytes(rs_recv0.at[2, pl.ds(0, n_blk - 1)], ag_send.at[2, quad])


def per_device(n_order, n_blk, right_side, start_guess, legendre, orders, prior_inv, noise_inv, pixel_flags):
    slots, local, degrees = legendre.shape
    cycles, pixels = noise_inv.shape[1], noise_inv.shape[2]
    width = degrees + 128
    part = degrees // n_blk
    smem = pl.BlockSpec(memory_space=pltpu.SMEM)
    vmem = pl.BlockSpec(memory_space=pltpu.VMEM)
    hbm = pl.BlockSpec(memory_space=pl.ANY)
    live_shape = jax.ShapeDtypeStruct((2, 8, width), F32)
    dead_shape = jax.ShapeDtypeStruct((2, 8, degrees), F32)
    columns = 16 * n_order
    sheets = -(-(local + 8) // 128)
    half_turn = pixels // 2
    scratch = [pltpu.VMEM((2, local, degrees), BF16)] * 4 + [
        pltpu.VMEM((8, 128), jnp.int32),
        pltpu.VMEM(right_side.shape, F32),
        pltpu.VMEM(right_side.shape, F32),
        pltpu.VMEM((2, 8, degrees), F32),
        pltpu.VMEM((2, 8, degrees), F32),
        pltpu.VMEM((4, local, width), BF16),
        pltpu.VMEM((4, width, local), BF16),
        pltpu.VMEM((3, 2, 8, width), F32),
        pltpu.VMEM((4, 2, 8, degrees), F32),
        pltpu.VMEM((2, 8, width), F32),
        pltpu.VMEM((2, 8, degrees), F32),
        pltpu.VMEM((2, 8, width), F32),
        pltpu.VMEM((2, 8, degrees), F32),
        pltpu.VMEM((2, 8, width), F32),
        pltpu.VMEM((2, 8, width), F32),
        pltpu.VMEM((cycles, 2, pixels), F32),
        pltpu.VMEM((cycles, 2, pixels), jnp.int32),
        pltpu.VMEM((2, 64, width), BF16),
        pltpu.VMEM((sheets, 128, 128), F32),
        pltpu.VMEM((sheets * 128, 128), F32),
        pltpu.VMEM((sheets, 128, 128), F32),
        pltpu.VMEM((n_order, 8, 128), F32),
        pltpu.VMEM((6, n_order, 8, 128), F32),
        pltpu.VMEM((n_order, 8, 128), jnp.int32),
        pltpu.VMEM((8, 128), F32),
        pltpu.VMEM((128, columns), BF16),
        pltpu.VMEM((8, 8, half_turn), F32),
        pltpu.VMEM((64, columns), F32),
        pltpu.VMEM((8, columns), F32),
        pltpu.VMEM((n_order, 2, 8, 128), F32),
        pltpu.VMEM((n_order, 2, 8, 128), F32),
        pltpu.VMEM((columns, half_turn), BF16),
        pltpu.VMEM((half_turn, columns), BF16),
        pltpu.VMEM((64, half_turn), F32),
        pltpu.VMEM((6, 8, 128), F32),
        pltpu.VMEM((2, n_blk, 8, part + 128), F32),
        pltpu.VMEM((2, 8, 128), F32),
        pltpu.VMEM((2, 8, part), F32),
        pltpu.VMEM((3, n_blk, 8, part), F32),
        pltpu.VMEM((3, n_blk, 8, part + 128), F32),
        pltpu.VMEM((3, 2, 8, degrees), F32),
        pltpu.VMEM((3, 8, 128), F32),
        pltpu.VMEM((2, 8, width), F32),
        pltpu.VMEM((2, 8, degrees), F32),
        pltpu.VMEM((4, 8, 128), F32),
        pltpu.SemaphoreType.DMA((4,)),
        pltpu.SemaphoreType.DMA((4,)),
        pltpu.SemaphoreType.DMA((2,)),
        pltpu.SemaphoreType.DMA((6,)),
        pltpu.SemaphoreType.DMA((6,)),
        pltpu.SemaphoreType.DMA((3, 2)),
        pltpu.SemaphoreType.DMA((3, 2)),
        pltpu.SemaphoreType.DMA((3, 2)),
        pltpu.SemaphoreType.DMA((3, 2)),
    ]
    results = pl.pallas_call(
        functools.partial(main_kernel, n_order, n_blk, degrees, cycles, pixels),
        in_specs=[smem, hbm, hbm, hbm, vmem, hbm, hbm],
        out_specs=[vmem] * 4,
        out_shape=[live_shape, dead_shape, live_shape, dead_shape],
        scratch_shapes=scratch,
        compiler_params=pltpu.CompilerParams(
            collective_id=0, has_side_effects=True, vmem_limit_bytes=VMEM_LIMIT),
        name="steps",
    )(orders, legendre, start_guess, right_side, prior_inv.reshape(1, degrees),
      noise_inv.transpose(1, 0, 2), pixel_flags.transpose(1, 0, 2))

    full = jax.ShapeDtypeStruct(right_side.shape, F32)
    return tuple(pl.pallas_call(
        functools.partial(unpack_kernel, degrees),
        in_specs=[smem] + [vmem] * 4,
        out_specs=[vmem] * 2,
        out_shape=[full, full],
        scratch_shapes=[pltpu.VMEM((2, 8, degrees), F32)] * 2,
        compiler_params=pltpu.CompilerParams(vmem_limit_bytes=VMEM_LIMIT),
        name="unpack",
    )(orders, *results))


def solution(mesh):
    in_specs = (
        P(None, None, "order", None),
        P(None, None, "order", None),
        P("order", "blk", None),
        P("order"),
        P(),
        P(None, ("blk", "order"), None),
        P(None, ("blk", "order"), None),
    )
    out_specs = (P(None, None, "order", None), P(None, None, "order", None))
    body = functools.partial(per_device, mesh.shape["order"], mesh.shape["blk"])
    return jax.shard_map(body, mesh=mesh, in_specs=in_specs, out_specs=out_specs, check_vma=False)
```
